32 devices in a mesh: dp: 16 (over z, x, core), tensor: 2 (over y).
Axes of the slice: x: 2, y: 2, z: 4, core: 2. Of those that a mesh axis runs over, the one named last changes fastest.
Arguments:
- tokens: bfloat16 [4096, 512], P(('dp', 'tensor')), may hold values from -7 to 7, as said below
- norm_gains: float32 [5, 512], replicated, may hold values from 0.25 to 1.75
- first_in: bfloat16 [512, 2048], P('dp', 'tensor'), may hold values from -0.25 to 0.25
- first_out: bfloat16 [512, 2048], P('dp', 'tensor'), may hold values from -0.125 to 0.125
- attention_in: bfloat16 [4, 512, 512], P(None, 'dp', 'tensor'), may hold values from -0.25 to 0.25
- attention_out: bfloat16 [512, 512], P('dp', 'tensor'), may hold values from -1 to 1
- head_biases: float32 [2, 512], P(None, 'tensor'), may hold values from -3 to 3
- gated_in: bfloat16 [2, 512, 512], P(None, 'dp', 'tensor'), may hold values from -0.25 to 0.25
- pointwise_out: bfloat16 [512, 512], P('dp', 'tensor'), may hold values from -0.25 to 0.25
- depth_kernel: float32 [31, 512], P(None, 'tensor'), may hold values from -1 to 1
- batch_scale: float32 [512], P('tensor'), may hold values from 0.25 to 1.75
- batch_shift: float32 [512], P('tensor'), may hold values from -3 to 3
- second_in: bfloat16 [512, 2048], P('dp', 'tensor'), may hold values from -0.25 to 0.25
- second_out: bfloat16 [512, 2048], P('dp', 'tensor'), may hold values from -0.125 to 0.125
- cotangent: bfloat16 [4096, 512], P(('dp', 'tensor')), may hold values from -6 to 6
Outputs:
- block_out: bfloat16 [4096, 512], P(('dp', 'tensor'))
- grad_tokens: float32 [4096, 512], P(('dp', 'tensor'))
- grad_gains: float32 [5, 512], replicated
- grad_first_in: float32 [512, 2048], P('dp', 'tensor')
- grad_first_out: float32 [512, 2048], P('dp', 'tensor')
- grad_attention_in: float32 [4, 512, 512], P(None, 'dp', 'tensor')
- grad_attention_out: float32 [512, 512], P('dp', 'tensor')
- grad_head_biases: float32 [2, 512], P(None, 'tensor')
- grad_gated_in: float32 [2, 512, 512], P(None, 'dp', 'tensor')
- grad_pointwise_out: float32 [512, 512], P('dp', 'tensor')
- grad_kernel: float32 [31, 512], P(None, 'tensor')
- grad_batch_scale: float32 [512], P('tensor')
- grad_batch_shift: float32 [512], P('tensor')
- grad_second_in: float32 [512, 2048], P('dp', 'tensor')
- grad_second_out: float32 [512, 2048], P('dp', 'tensor')
The draws below stay inside these ranges and needn't reach their ends.
Inputs may be any that keep to these rules, and one draw needn't show every extreme that they name: `tokens`: the block's input.
All inputs are finite; a program needn't handle non-finite values.
Results may differ from the reference program's by a relative error of at most 0.029.
Values may be sent and summed in bfloat16 or wider, within the bound.
No kernel may reach another device: no remote copies, remote signals or barrier semaphores. Data moves between devices by JAX's collectives and lax.ppermute only.
A program may use at most 128 MiB of HBM per device.

```python
import math
import jax
import jax.numpy as jnp
from jax import lax

D = 512
HEAD_TOTAL = 8
HEAD_FEATURES = 64
FF = 2048
KERNEL = 31
SEQUENCE_LENGTH = 256
TOKENS = 4096
N_DP = 16


def draw_tokens(key, part):
    key = jax.random.fold_in(key, 11)
    noise_key, direction_key = jax.random.split(key, 2)
    sequence = jnp.arange(TOKENS) // SEQUENCE_LENGTH
    amplitude = 0.3 + 0.7 * sequence.astype(jnp.float32) / max(TOKENS // SEQUENCE_LENGTH - 1, 1)
    direction = jnp.clip(jax.random.normal(direction_key, (D,), jnp.float32), -2.5, 2.5)
    noise_rows = jnp.clip(jax.random.normal(noise_key, (TOKENS, D), jnp.float32), -4.0, 4.0)
    return (noise_rows + amplitude[:, None] * direction[None, :]).astype(jnp.bfloat16)


def with_spikes(values, own_key, source, target, blocks, factor):
    owner, partner = [(jnp.arange(values.shape[position]) // (values.shape[position] // blocks)).reshape([-1 if axis == position else 1 for axis in range(values.ndim)]) for position in (source, target)]
    chosen = jax.random.permutation(own_key, blocks)[partner]
    strong = (owner == chosen) | (owner == (partner + blocks // 2) % blocks)
    return jnp.where(strong, factor * values, values)


def block_scale(stream_key, dims, cuts, least, largest):
    def one(axis_at, blocks):
        steps = jax.random.uniform(jax.random.fold_in(jax.random.fold_in(stream_key, 6), axis_at), (blocks,), jnp.float32, least / len(cuts), largest / len(cuts))
        return jnp.repeat(jnp.exp(steps), dims[axis_at] // blocks).reshape((-1,) + (1,) * (len(dims) - axis_at - 1))

    level = one(*cuts[0])
    for cut in cuts[1:]:
        level = level * one(*cut)
    return level


def normal_values(rng, dims, scale, bound, cuts=(), kind=jnp.bfloat16):
    array = jax.random.normal(rng, dims, jnp.float32) * scale
    if len(cuts) > 0:
        array = block_scale(rng, dims, cuts, -0.22, 0.18) * array
    return jnp.clip(array, min=-bound, max=bound).astype(kind)


def gaussian_with(rng, dims, deviation, most, cuts, heavy, kind=jnp.bfloat16):
    values = deviation * jax.random.normal(rng, dims, jnp.float32)
    if cuts:
        values = values * block_scale(rng, dims, cuts, -0.22, 0.18)
    return jnp.clip(with_spikes(values, jax.random.fold_in(rng, 3), *heavy), -most, most).astype(kind)


def setup_inputs(seed: int = 0) -> dict:
    streams_of = jax.random.split(jax.random.key(seed), 16)
    tokens = draw_tokens(jax.random.fold_in(streams_of[15], 71), 0)
    norm_gains = jnp.clip(1.0 + 0.15 * jax.random.normal(streams_of[1], (5, D), jnp.float32), 0.25, 1.75)
    first_in = normal_values(streams_of[2], (D, FF), D ** -0.5, 0.25, ((0, 16), (1, 2)))
    first_out = normal_values(streams_of[3], (D, FF), FF ** -0.5, 0.125, ((0, 16), (1, 2)))
    attention_in = normal_values(streams_of[4], (4, D, D), D ** -0.5, 0.25, ((1, 16), (2, 2)))
    attention_out = normal_values(streams_of[5], (D, D), (max(16 * D // SEQUENCE_LENGTH, 1)) ** -0.5, 1.0, ((0, 16), (1, 2)))
    head_biases = normal_values(streams_of[6], (2, D), 0.5, 3.0, ((1, 2),), jnp.float32)
    gated_in = normal_values(streams_of[7], (2, D, D), D ** -0.5, 0.25, ((1, 16), (2, 2)))
    pointwise_out = normal_values(streams_of[8], (D, D), D ** -0.5, 0.25, ((0, 16), (1, 2)))
    depth_kernel = normal_values(streams_of[9], (KERNEL, D), KERNEL ** -0.5, 1.0, ((1, 2),), jnp.float32)
    batch_scale = jnp.clip(1.0 + 0.15 * jax.random.normal(streams_of[10], (D,), jnp.float32), 0.25, 1.75)
    batch_shift = normal_values(streams_of[11], (D,), 0.5, 3.0, ((0, 2),), jnp.float32)
    second_in = normal_values(streams_of[12], (D, FF), D ** -0.5, 0.25, ((0, 16), (1, 2)))
    second_out = normal_values(streams_of[13], (D, FF), FF ** -0.5, 0.125, ((0, 16), (1, 2)))
    cotangent = gaussian_with(streams_of[14], (TOKENS, D), 1.0, 6.0, ((0, 32),), (0, 1, 32, 2.75))
    return {"tokens": tokens, "norm_gains": norm_gains, "first_in": first_in, "first_out": first_out, "attention_in": attention_in, "attention_out": attention_out, "head_biases": head_biases, "gated_in": gated_in, "pointwise_out": pointwise_out, "depth_kernel": depth_kernel, "batch_scale": batch_scale, "batch_shift": batch_shift, "second_in": second_in, "second_out": second_out, "cotangent": cotangent}


@jax.custom_vjp
def low(v):
    return lax.optimization_barrier(v.astype(jnp.bfloat16)).astype(jnp.float32)

@jax.custom_vjp
def low_back(v):
    return v

def low_keep(v):
    return (low(v), None)

def low_pass(kept, grad):
    return (grad,)

def back_keep(v):
    return (v, None)

def back_low(kept, grad):
    return (low(grad),)
low.defvjp(low_keep, low_pass)
low_back.defvjp(back_keep, back_low)
EPSILON = 1e-05
FULL_PRECISION = lax.Precision.HIGHEST

def matmul(left_side, right_side):
    return jnp.dot(left_side, right_side, precision=FULL_PRECISION, preferred_element_type=jnp.float32)

def layer_norm(residual, norm_gain):
    centred = residual - lax.optimization_barrier(jnp.mean(residual, -1, keepdims=True))
    factor = lax.rsqrt(lax.optimization_barrier(jnp.mean(centred * centred, -1, keepdims=True)) + EPSILON)
    return centred * factor * norm_gain

def sinusoid(length, features):
    offsets = jnp.arange(2 * length - 1, dtype=jnp.float32) - (length - 1)
    half_width = features // 2
    frequency = jnp.exp(jnp.arange(half_width, dtype=jnp.float32) * (-math.log(10000.0) / half_width))
    angles = offsets[:, None] * frequency[None, :]
    return jnp.concatenate([jnp.sin(angles), jnp.cos(angles)], 1)

def shift_relative(unscaled_scores):
    head_count = unscaled_scores.shape[0]
    length = unscaled_scores.shape[1]
    wide = unscaled_scores.shape[2]
    flattened = unscaled_scores.reshape(head_count, length * wide)[:, length - 1:length - 1 + length * (wide - 1)]
    return flattened.reshape(head_count, length, wide - 1)[:, :, :length]

def feed_forward(residual, norm_gain, weight_in, weight_out):
    entries = low(layer_norm(residual, norm_gain))
    hidden_pre = low_back(matmul(entries, weight_in))
    hidden = low(hidden_pre * jax.nn.sigmoid(hidden_pre))
    branch = low_back(matmul(hidden, weight_out.T))
    return residual + 0.5 * branch

def attention(residual, norm_gain, projections, weight_out, head_biases):
    entries = low(layer_norm(residual, norm_gain))
    queries = low_back(matmul(entries, projections[0]))
    key_rows = low(low_back(matmul(entries, projections[1])))
    value_rows = low(low_back(matmul(entries, projections[2])))
    query_content = low(queries + head_biases[0])
    query_position = low(queries + head_biases[1])
    position_table = low(sinusoid(SEQUENCE_LENGTH, D))
    score_scale = HEAD_FEATURES ** (-0.5)
    per_head_shape = (SEQUENCE_LENGTH, HEAD_TOTAL, HEAD_FEATURES)

    def one_sequence(pieces):
        content_q, position_query, seq_keys, seq_values = pieces
        position_rows = low(low_back(matmul(position_table, projections[3])))
        content = jnp.einsum('ihd,jhd->hij', content_q.reshape(per_head_shape), seq_keys.reshape(per_head_shape), precision=FULL_PRECISION)
        unscaled_scores = jnp.einsum('tox,box->otb', position_query.reshape(per_head_shape), position_rows.reshape(2 * SEQUENCE_LENGTH - 1, HEAD_TOTAL, HEAD_FEATURES), precision=FULL_PRECISION)
        scores = low_back((content + shift_relative(unscaled_scores)) * score_scale)
        row_top = lax.optimization_barrier(jnp.max(scores, -1, keepdims=True))
        lifted = jnp.exp(scores - row_top)
        probability = lifted / lax.optimization_barrier(jnp.sum(lifted, -1, keepdims=True))
        mixture = jnp.einsum('hij,jhd->ihd', low(probability), seq_values.reshape(per_head_shape), precision=FULL_PRECISION)
        return low(low_back(mixture.reshape(SEQUENCE_LENGTH, D)))
    grouped = (query_content.reshape(N_DP, SEQUENCE_LENGTH, D), query_position.reshape(N_DP, SEQUENCE_LENGTH, D), key_rows.reshape(N_DP, SEQUENCE_LENGTH, D), value_rows.reshape(N_DP, SEQUENCE_LENGTH, D))
    attended = lax.map(jax.checkpoint(one_sequence), grouped).reshape(TOKENS, D)
    return residual + low_back(matmul(attended, weight_out.T))

def convolution(residual, norm_gain, gated_weights, weight_out, depth_kernel, batch_scale, batch_shift):
    entries = low(layer_norm(residual, norm_gain))
    value_pre = low_back(matmul(entries, gated_weights[0]))
    gate_pre = low_back(matmul(entries, gated_weights[1]))
    glued = (value_pre * jax.nn.sigmoid(gate_pre)).reshape(N_DP, SEQUENCE_LENGTH, D)
    half_width = (KERNEL - 1) // 2
    padded = jnp.pad(glued, ((0, 0), (half_width, half_width), (0, 0)))
    convolved = depth_kernel[0] * padded[:, 0:SEQUENCE_LENGTH]
    for tap_index in range(1, KERNEL):
        convolved = convolved + depth_kernel[tap_index] * padded[:, tap_index:tap_index + SEQUENCE_LENGTH]
    convolved = convolved.reshape(TOKENS, D)
    column_mean = lax.optimization_barrier(jnp.mean(convolved, 0))
    variance = lax.optimization_barrier(jnp.mean(convolved * convolved, 0)) - column_mean * column_mean
    shifted = (convolved - column_mean) * lax.rsqrt(variance + EPSILON) * batch_scale + batch_shift
    activated = low(shifted * jax.nn.sigmoid(shifted))
    return residual + low_back(matmul(activated, weight_out.T))

def layer(tokens, norm_gains, first_in, first_out, attention_in, attention_out, head_biases, gated_in, pointwise_out, depth_kernel, batch_scale, batch_shift, second_in, second_out):
    after_first = jax.checkpoint(feed_forward)(tokens, norm_gains[0], first_in, first_out)
    after_attention = jax.checkpoint(attention)(after_first, norm_gains[1], attention_in, attention_out, head_biases)
    after_conv = jax.checkpoint(convolution)(after_attention, norm_gains[2], gated_in, pointwise_out, depth_kernel, batch_scale, batch_shift)
    after_second = jax.checkpoint(feed_forward)(after_conv, norm_gains[3], second_in, second_out)
    return layer_norm(after_second, norm_gains[4])

def reference(tokens, norm_gains, first_in, first_out, attention_in, attention_out, head_biases, gated_in, pointwise_out, depth_kernel, batch_scale, batch_shift, second_in, second_out, cotangent):
    result, pullback = jax.vjp(layer, tokens.astype(jnp.float32), norm_gains, first_in.astype(jnp.float32), first_out.astype(jnp.float32), attention_in.astype(jnp.float32), attention_out.astype(jnp.float32), head_biases, gated_in.astype(jnp.float32), pointwise_out.astype(jnp.float32), depth_kernel, batch_scale, batch_shift, second_in.astype(jnp.float32), second_out.astype(jnp.float32))
    grads = pullback(cotangent.astype(jnp.float32))
    return (result.astype(jnp.bfloat16), grads[0], grads[1], grads[2], grads[3], grads[4], grads[5], grads[6], grads[7], grads[8], grads[9], grads[10], grads[11], grads[12], grads[13])
```

```python
import math

import jax
import jax.numpy as jnp
from jax import lax
from jax.experimental import pallas as pl
from jax.experimental.pallas import tpu as pltpu
from jax.sharding import PartitionSpec as P

HEAD_TOTAL = 8
EPSILON = 1e-05
BF16 = jnp.bfloat16
F32 = jnp.float32


def matmul(left_side, right_side):
    return jnp.dot(left_side, right_side, preferred_element_type=F32)


def right_transposed(left_side, right_side):
    return lax.dot_general(
        left_side, right_side, (((1,), (1,)), ((), ())), preferred_element_type=F32
    )


def left_transposed(left_side, right_side):
    return lax.dot_general(
        left_side, right_side, (((0,), (0,)), ((), ())), preferred_element_type=F32
    )


def swish_slope(pre_value, gate_sigma):
    return gate_sigma * (1.0 + pre_value * (1.0 - gate_sigma))


def norm_parts(residual):
    centred = residual - jnp.mean(residual, -1, keepdims=True)
    factor = lax.rsqrt(jnp.mean(centred * centred, -1, keepdims=True) + EPSILON)
    return centred * factor, factor


def norm_back(gradient, normed, factor, norm_gain):
    scaled = gradient * norm_gain
    inner_sum = (
        scaled
        - jnp.mean(scaled, -1, keepdims=True)
        - normed * jnp.mean(scaled * normed, -1, keepdims=True)
    )
    return factor * inner_sum, jnp.sum(gradient * normed, 0, keepdims=True)


def sinusoid(length, features):
    offsets = jnp.arange(2 * length, dtype=F32) - (length - 1)
    half_width = features // 2
    frequency = jnp.exp(jnp.arange(half_width, dtype=F32) * (-math.log(10000.0) / half_width))
    angles = offsets[:, None] * frequency[None, :]
    table = jnp.concatenate([jnp.sin(angles), jnp.cos(angles)], 1)
    return jnp.where(offsets[:, None] < length, table, 0.0)


def on_chip(function, name, operands, results, scratch=(), flops=300_000_000):
    count = len(operands)
    total = count + len(results)

    def kernel(*refs):
        function(refs[:count], refs[count:total], refs[total:])

    moved = sum(value.size * value.dtype.itemsize for value in operands)
    moved += sum(math.prod(shape) * jnp.dtype(kind).itemsize for shape, kind in results)
    return pl.pallas_call(
        kernel,
        out_shape=[jax.ShapeDtypeStruct(shape, kind) for shape, kind in results],
        in_specs=[pl.BlockSpec(memory_space=pltpu.VMEM)] * count,
        out_specs=[pl.BlockSpec(memory_space=pltpu.VMEM)] * len(results),
        scratch_shapes=list(scratch),
        compiler_params=pltpu.CompilerParams(vmem_limit_bytes=40 * 1024 * 1024),
        cost_estimate=pl.CostEstimate(flops=flops, bytes_accessed=moved, transcendentals=0),
        name=name,
    )(*operands)


def swap(value):
    return lax.ppermute(value, "tensor", [(0, 1), (1, 0)])


def both_halves(own):
    other = swap(own)
    first = lax.axis_index("tensor") == 0
    return jnp.concatenate([jnp.where(first, own, other), jnp.where(first, other, own)], 0)


def sum_over(value, axis):
    size = lax.axis_size(axis)
    if size & (size - 1):
        return lax.psum(value, axis)
    step = 1
    while step < size:
        value = value + lax.ppermute(value, axis, [(k, k ^ step) for k in range(size)])
        step *= 2
    return value


def ff_forward_body(row, residual, gain_ref, weight_ref, outs):
    entries_ref, pre_ref, hidden_ref, part_ref = outs
    half = weight_ref.shape[1] // 2
    normed, _ = norm_parts(residual)
    entries = (normed * gain_ref[row : row + 1, :]).astype(BF16)
    entries_ref[...] = entries
    pre = matmul(entries, weight_ref[:, :half])
    pre_ref[...] = pre
    hidden = (pre * jax.nn.sigmoid(pre)).astype(BF16)
    hidden_ref[...] = hidden
    part_ref[...] = right_transposed(hidden, weight_ref[:, half:]).astype(BF16)


def first_forward(tokens, gains, weights):
    rows, width = tokens.shape
    hidden = weights.shape[1] // 2

    def body(ins, outs, _):
        ff_forward_body(0, ins[0][...].astype(F32), ins[1], ins[2], outs)

    return on_chip(
        body,
        "first_forward",
        (tokens, gains, weights),
        (
            ((rows, width), BF16),
            ((rows, hidden), F32),
            ((rows, hidden), BF16),
            ((rows, width), BF16),
        ),
    )


def second_forward(residual, own, other, gains, weights):
    rows, width = residual.shape
    hidden = weights.shape[1] // 2

    def body(ins, outs, _):
        after = ins[0][...] + (ins[1][...].astype(F32) + ins[2][...].astype(F32))
        outs[0][...] = after
        ff_forward_body(3, after, ins[3], ins[4], outs[1:])

    return on_chip(
        body,
        "second_forward",
        (residual, own, other, gains, weights),
        (
            ((rows, width), F32),
            ((rows, width), BF16),
            ((rows, hidden), F32),
            ((rows, hidden), BF16),
            ((rows, width), BF16),
        ),
    )


def ff_back_body(gradient, pre_ref, weight_ref, branch_ref, slope_ref):
    half = weight_ref.shape[1] // 2
    branch = (0.5 * gradient).astype(BF16)
    branch_ref[...] = branch
    grad_hidden = matmul(branch, weight_ref[:, half:])
    pre = pre_ref[...]
    grad_pre = (grad_hidden * swish_slope(pre, jax.nn.sigmoid(pre))).astype(BF16)
    slope_ref[...] = grad_pre
    return right_transposed(grad_pre, weight_ref[:, :half])


def second_back(residual, own, other, cotangent, pre, gains, weights):
    rows, width = residual.shape
    hidden = weights.shape[1] // 2

    def body(ins, outs, _):
        x_ref, own_ref, other_ref, cot_ref, pre_ref, gain_ref, weight_ref = ins
        out_ref, grad_ref, branch_ref, slope_ref, part_ref, gain_grad_ref = outs
        after = x_ref[...] + 0.5 * (own_ref[...].astype(F32) + other_ref[...].astype(F32))
        normed, factor = norm_parts(after)
        gain = gain_ref[4:5, :]
        out_ref[...] = (normed * gain).astype(BF16)
        gradient, gain_grad_ref[...] = norm_back(
            cot_ref[...].astype(F32), normed, factor, gain
        )
        grad_ref[...] = gradient
        part_ref[...] = ff_back_body(gradient, pre_ref, weight_ref, branch_ref, slope_ref).astype(
            BF16
        )

    return on_chip(
        body,
        "second_back",
        (residual, own, other, cotangent, pre, gains, weights),
        (
            ((rows, width), BF16),
            ((rows, width), F32),
            ((rows, width), BF16),
            ((rows, hidden), BF16),
            ((rows, width), BF16),
            ((1, width), F32),
        ),
    )


def ff_weight_grads(entries, grad_pre, branch, hidden, name):
    width = entries.shape[1]
    half = hidden.shape[1]

    def body(ins, outs, _):
        outs[0][:, :half] = left_transposed(ins[0][...], ins[1][...]).astype(BF16)
        outs[0][:, half:] = left_transposed(ins[2][...], ins[3][...]).astype(BF16)

    return on_chip(
        body, name, (entries, grad_pre, branch, hidden), (((width, 2 * half), BF16),)
    )[0]


def position_forward(table, weights, columns):
    def body(ins, outs, _):
        outs[0][...] = matmul(ins[0][...], ins[1][:, 3 * columns : 4 * columns]).astype(BF16)

    return on_chip(body, "position_forward", (table, weights), (((table.shape[0], columns), BF16),))[0]


def attention_forward(tokens, own, other, gains, weights, positions, biases, heads):
    rows, width = tokens.shape
    columns = biases.shape[1]
    features = columns // heads
    scale = features ** (-0.5)

    def body(ins, outs, _):
        x_ref, own_ref, other_ref, gain_ref, weight_ref, table_ref, bias_ref = ins
        after_ref, e_ref, qc_ref, qp_ref, k_ref, v_ref, prob_ref, mix_ref, part_ref = outs
        after = x_ref[...].astype(F32) + 0.5 * (
            own_ref[...].astype(F32) + other_ref[...].astype(F32)
        )
        after_ref[...] = after
        normed, _ = norm_parts(after)
        entries = (normed * gain_ref[1:2, :]).astype(BF16)
        e_ref[...] = entries
        joined = matmul(entries, weight_ref[:, : 3 * columns])
        queries = joined[:, :columns]
        content_q = (queries + bias_ref[0:1, :]).astype(BF16)
        position_q = (queries + bias_ref[1:2, :]).astype(BF16)
        keys = joined[:, columns : 2 * columns].astype(BF16)
        values = joined[:, 2 * columns :].astype(BF16)
        qc_ref[...] = content_q
        qp_ref[...] = position_q
        k_ref[...] = keys
        v_ref[...] = values
        mixed = []
        for head in range(heads):
            part = slice(head * features, (head + 1) * features)
            content = right_transposed(content_q[:, part], keys[:, part])
            raw = right_transposed(position_q[:, part], table_ref[:, part])
            shifted = pltpu.roll(raw, rows + 1, 1, stride=1, stride_axis=0)[:, :rows]
            scores = (content + shifted) * scale
            lifted = jnp.exp(scores - jnp.max(scores, -1, keepdims=True))
            probability = lifted / jnp.sum(lifted, -1, keepdims=True)
            prob_ref[head] = probability
            mixed.append(matmul(probability.astype(BF16), values[:, part]))
        attended = jnp.concatenate(mixed, 1).astype(BF16)
        mix_ref[...] = attended
        part_ref[...] = right_transposed(attended, weight_ref[:, 4 * columns :]).astype(BF16)

    local = ((rows, columns), BF16)
    return on_chip(
        body,
        "attention_forward",
        (tokens, own, other, gains, weights, positions, biases),
        (
            ((rows, width), F32),
            ((rows, width), BF16),
            local,
            local,
            local,
            local,
            ((heads, rows, rows), F32),
            local,
            ((rows, width), BF16),
        ),
    )


def attention_back(gradient, own, other, residual, gains, weights, positions, kept, heads):
    rows, width = residual.shape
    columns = positions.shape[1]
    features = columns // heads
    scale = features ** (-0.5)

    def body(ins, outs, _):
        (
            grad_ref,
            own_ref,
            other_ref,
            x_ref,
            gain_ref,
            weight_ref,
            table_ref,
            qc_ref,
            qp_ref,
            k_ref,
            v_ref,
            prob_ref,
        ) = ins
        total_ref, branch_ref, joined_ref, table_grad_ref, part_ref, gain_grad_ref, bias_ref = outs
        normed, factor = norm_parts(x_ref[...])
        passed, gain_grad_ref[...] = norm_back(
            own_ref[...].astype(F32) + other_ref[...].astype(F32), normed, factor, gain_ref[2:3, :]
        )
        total = grad_ref[...] + passed
        total_ref[...] = total
        branch = total.astype(BF16)
        branch_ref[...] = branch
        grad_mixed = matmul(branch, weight_ref[:, 4 * columns :]).astype(BF16)
        line = lax.broadcasted_iota(jnp.int32, (rows, rows), 0)
        place = lax.broadcasted_iota(jnp.int32, (rows, rows), 1)
        flip = (line + place == rows - 1).astype(F32).astype(BF16)
        content_q = qc_ref[...]
        keys = k_ref[...]
        values = v_ref[...]
        flipped_q = matmul(flip, qp_ref[...]).astype(BF16)
        zeros = jnp.zeros((rows, rows), F32)
        from_content, from_position, to_keys, to_values, to_table = [], [], [], [], []
        for head in range(heads):
            part = slice(head * features, (head + 1) * features)
            probability = prob_ref[head]
            grad_probability = right_transposed(grad_mixed[:, part], values[:, part])
            to_values.append(left_transposed(probability.astype(BF16), grad_mixed[:, part]))
            inner = jnp.sum(probability * grad_probability, -1, keepdims=True)
            grad_scores = (probability * (grad_probability - inner)).astype(BF16) * scale
            grad_scores = grad_scores.astype(BF16)
            from_content.append(matmul(grad_scores, keys[:, part]))
            to_keys.append(left_transposed(grad_scores, content_q[:, part]))
            flipped = jnp.concatenate([matmul(flip, grad_scores), zeros], 1)
            spread = pltpu.roll(flipped, 0, 1, stride=1, stride_axis=0).astype(BF16)
            from_position.append(matmul(spread, table_ref[:, part]))
            to_table.append(left_transposed(spread, flipped_q[:, part]))
        grad_content = jnp.concatenate(from_content, 1)
        grad_position = jnp.concatenate(from_position, 1)
        high = grad_position.astype(BF16)
        low = (grad_position - high.astype(F32)).astype(BF16)
        grad_position = matmul(flip, high) + matmul(flip, low)
        bias_ref[0:1, :] = jnp.sum(grad_content, 0, keepdims=True)
        bias_ref[1:2, :] = jnp.sum(grad_position, 0, keepdims=True)
        joined = jnp.concatenate(
            [grad_content + grad_position] + to_keys + to_values, 1
        ).astype(BF16)
        joined_ref[...] = joined
        table_grad_ref[...] = jnp.concatenate(to_table, 1).astype(BF16)
        part_ref[...] = right_transposed(joined, weight_ref[:, : 3 * columns]).astype(BF16)

    return on_chip(
        body,
        "attention_back",
        (gradient, own, other, residual, gains, weights, positions) + tuple(kept),
        (
            ((rows, width), F32),
            ((rows, width), BF16),
            ((rows, 3 * columns), BF16),
            ((2 * rows, columns), BF16),
            ((rows, width), BF16),
            ((1, width), F32),
            ((2, columns), F32),
        ),
    )


def attention_weight_grads(entries, joined, table, table_grad, branch, attended):
    width = entries.shape[1]
    columns = attended.shape[1]

    def body(ins, outs, _):
        out_ref = outs[0]
        out_ref[:, : 3 * columns] = left_transposed(ins[0][...], ins[1][...]).astype(BF16)
        out_ref[:, 3 * columns : 4 * columns] = left_transposed(ins[2][...], ins[3][...]).astype(
            BF16
        )
        out_ref[:, 4 * columns :] = left_transposed(ins[4][...], ins[5][...]).astype(BF16)

    return on_chip(
        body,
        "attention_weight_grads",
        (entries, joined, table, table_grad, branch, attended),
        (((width, 5 * columns), BF16),),
    )[0]


PAD = 16


def conv_forward(residual, own, other, gains, weights, depth_kernel):
    rows, width = residual.shape
    taps, columns = depth_kernel.shape
    half_taps = (taps - 1) // 2

    def body(ins, outs, scratch):
        x_ref, own_ref, other_ref, gain_ref, weight_ref, tap_ref = ins
        after_ref, c_ref, value_ref, gate_ref, conv_ref, sums_ref = outs
        padded = scratch[0]
        after = x_ref[...] + (own_ref[...].astype(F32) + other_ref[...].astype(F32))
        after_ref[...] = after
        normed, _ = norm_parts(after)
        entries = (normed * gain_ref[2:3, :]).astype(BF16)
        c_ref[...] = entries
        joined = matmul(entries, weight_ref[:, : 2 * columns])
        value = joined[:, :columns]
        gate = jax.nn.sigmoid(joined[:, columns:])
        value_ref[...] = value
        gate_ref[...] = gate
        padded[:PAD, :] = jnp.zeros((PAD, columns), F32)
        padded[PAD + rows :, :] = jnp.zeros((PAD, columns), F32)
        padded[PAD : PAD + rows, :] = value * gate
        total = jnp.zeros((rows, columns), F32)
        for tap in range(taps):
            start = PAD - half_taps + tap
            total = total + tap_ref[tap : tap + 1, :] * padded[start : start + rows, :]
        conv_ref[...] = total
        sums_ref[0:1, :] = jnp.sum(total, 0, keepdims=True)
        sums_ref[1:2, :] = jnp.sum(total * total, 0, keepdims=True)

    local = ((rows, columns), F32)
    return on_chip(
        body,
        "conv_forward",
        (residual, own, other, gains, weights, depth_kernel),
        (((rows, width), F32), ((rows, width), BF16), local, local, local, ((2, columns), F32)),
        scratch=(pltpu.VMEM((rows + 2 * PAD, columns), F32),),
    )


def batch_norm(conv_ref, sums_ref, batch_ref, token_count):
    column_mean = sums_ref[0:1, :] / token_count
    inverse = lax.rsqrt(sums_ref[1:2, :] / token_count - column_mean * column_mean + EPSILON)
    standard = (conv_ref[...] - column_mean) * inverse
    return standard, inverse, standard * batch_ref[0:1, :] + batch_ref[1:2, :]


def norm_forward(convolved, sums, batch, weights, token_count):
    rows, columns = convolved.shape
    width = weights.shape[0]

    def body(ins, outs, _):
        conv_ref, sums_ref, batch_ref, weight_ref = ins
        _, _, shifted = batch_norm(conv_ref, sums_ref, batch_ref, token_count)
        activated = (shifted * jax.nn.sigmoid(shifted)).astype(BF16)
        outs[0][...] = activated
        outs[1][...] = right_transposed(activated, weight_ref[:, 2 * columns :]).astype(BF16)

    return on_chip(
        body,
        "norm_forward",
        (convolved, sums, batch, weights),
        (((rows, columns), BF16), ((rows, width), BF16)),
    )


def norm_backward(gradient, own, other, residual, gains, weights, convolved, sums, batch, count):
    rows, columns = convolved.shape
    width = weights.shape[0]

    def body(ins, outs, _):
        grad_ref, own_ref, other_ref, x_ref, gain_ref, weight_ref, conv_ref, sums_ref, batch_ref = (
            ins
        )
        total_ref, branch_ref, shifted_ref, grad_sums_ref, gain_grad_ref = outs
        normed, factor = norm_parts(x_ref[...])
        passed, gain_grad_ref[...] = norm_back(
            own_ref[...].astype(F32) + other_ref[...].astype(F32), normed, factor, gain_ref[3:4, :]
        )
        total = grad_ref[...] + passed
        total_ref[...] = total
        branch = total.astype(BF16)
        branch_ref[...] = branch
        standard, _, shifted = batch_norm(conv_ref, sums_ref, batch_ref, count)
        grad_shifted = matmul(branch, weight_ref[:, 2 * columns :]) * swish_slope(
            shifted, jax.nn.sigmoid(shifted)
        )
        shifted_ref[...] = grad_shifted
        grad_sums_ref[0:1, :] = jnp.sum(grad_shifted, 0, keepdims=True)
        grad_sums_ref[1:2, :] = jnp.sum(grad_shifted * standard, 0, keepdims=True)

    return on_chip(
        body,
        "norm_backward",
        (gradient, own, other, residual, gains, weights, convolved, sums, batch),
        (
            ((rows, width), F32),
            ((rows, width), BF16),
            ((rows, columns), F32),
            ((2, columns), F32),
            ((1, width), F32),
        ),
    )


def conv_backward(
    grad_shifted, grad_sums, convolved, sums, batch, value, gate, weights, depth_kernel, count
):
    rows, columns = convolved.shape
    width = weights.shape[0]
    taps = depth_kernel.shape[0]
    half_taps = (taps - 1) // 2

    def body(ins, outs, scratch):
        (
            shifted_ref,
            grad_sums_ref,
            conv_ref,
            sums_ref,
            batch_ref,
            value_ref,
            gate_ref,
            weight_ref,
            tap_ref,
        ) = ins
        grad_conv_ref, joined_ref, part_ref = outs
        padded = scratch[0]
        standard, inverse, _ = batch_norm(conv_ref, sums_ref, batch_ref, count)
        grad_conv = (inverse * batch_ref[0:1, :]) * (
            shifted_ref[...]
            - grad_sums_ref[0:1, :] / count
            - standard * (grad_sums_ref[1:2, :] / count)
        )
        grad_conv_ref[...] = grad_conv
        padded[:PAD, :] = jnp.zeros((PAD, columns), F32)
        padded[PAD + rows :, :] = jnp.zeros((PAD, columns), F32)
        padded[PAD : PAD + rows, :] = grad_conv
        total = jnp.zeros((rows, columns), F32)
        for tap in range(taps):
            start = PAD + half_taps - tap
            total = total + tap_ref[tap : tap + 1, :] * padded[start : start + rows, :]
        gate_sigma = gate_ref[...]
        grad_value = total * gate_sigma
        joined = jnp.concatenate(
            [grad_value, grad_value * value_ref[...] * (1.0 - gate_sigma)], 1
        ).astype(BF16)
        joined_ref[...] = joined
        part_ref[...] = right_transposed(joined, weight_ref[:, : 2 * columns]).astype(BF16)

    return on_chip(
        body,
        "conv_backward",
        (grad_shifted, grad_sums, convolved, sums, batch, value, gate, weights, depth_kernel),
        (((rows, columns), F32), ((rows, 2 * columns), BF16), ((rows, width), BF16)),
        scratch=(pltpu.VMEM((rows + 2 * PAD, columns), F32),),
    )


def conv_weight_grads(entries, joined, branch, activated, value, gate, grad_conv, taps):
    rows, columns = grad_conv.shape
    width = entries.shape[1]
    half_taps = (taps - 1) // 2

    def body(ins, outs, scratch):
        e_ref, joined_ref, branch_ref, y_ref, value_ref, gate_ref, grad_ref = ins
        out_ref, tap_ref = outs
        padded = scratch[0]
        out_ref[:, : 2 * columns] = left_transposed(e_ref[...], joined_ref[...]).astype(BF16)
        out_ref[:, 2 * columns :] = left_transposed(branch_ref[...], y_ref[...]).astype(BF16)
        padded[:PAD, :] = jnp.zeros((PAD, columns), F32)
        padded[PAD + rows :, :] = jnp.zeros((PAD, columns), F32)
        padded[PAD : PAD + rows, :] = value_ref[...] * gate_ref[...]
        grad_conv_value = grad_ref[...]
        for tap in range(taps):
            start = PAD - half_taps + tap
            tap_ref[tap : tap + 1, :] = jnp.sum(
                padded[start : start + rows, :] * grad_conv_value, 0, keepdims=True
            )

    return on_chip(
        body,
        "conv_weight_grads",
        (entries, joined, branch, activated, value, gate, grad_conv),
        (((width, 3 * columns), BF16), ((taps, columns), F32)),
        scratch=(pltpu.VMEM((rows + 2 * PAD, columns), F32),),
    )


def first_back(gradient, own, other, residual, pre, gains, weights):
    rows, width = residual.shape
    hidden = weights.shape[1] // 2

    def body(ins, outs, _):
        grad_ref, own_ref, other_ref, x_ref, pre_ref, gain_ref, weight_ref = ins
        total_ref, branch_ref, slope_ref, part_ref, gain_grad_ref = outs
        normed, factor = norm_parts(x_ref[...])
        passed, gain_grad_ref[...] = norm_back(
            own_ref[...].astype(F32) + other_ref[...].astype(F32), normed, factor, gain_ref[1:2, :]
        )
        total = grad_ref[...] + passed
        total_ref[...] = total
        part_ref[...] = ff_back_body(total, pre_ref, weight_ref, branch_ref, slope_ref).astype(BF16)

    return on_chip(
        body,
        "first_back",
        (gradient, own, other, residual, pre, gains, weights),
        (
            ((rows, width), F32),
            ((rows, width), BF16),
            ((rows, hidden), BF16),
            ((rows, width), BF16),
            ((1, width), F32),
        ),
    )


def input_back(gradient, own, other, tokens, gains):
    rows, width = tokens.shape

    def body(ins, outs, _):
        grad_ref, own_ref, other_ref, x_ref, gain_ref = ins
        normed, factor = norm_parts(x_ref[...].astype(F32))
        passed, outs[1][...] = norm_back(
            own_ref[...].astype(F32) + other_ref[...].astype(F32), normed, factor, gain_ref[0:1, :]
        )
        outs[0][...] = grad_ref[...] + passed

    return on_chip(
        body,
        "input_back",
        (gradient, own, other, tokens, gains),
        (((rows, width), F32), ((1, width), F32)),
        flops=1_000_000,
    )


def own_rows(whole, count):
    return lax.dynamic_slice_in_dim(whole, lax.axis_index("tensor") * count, count, 0)


def columns_of(stacked):
    return [stacked[index] for index in range(stacked.shape[0])]


def scatter_weights(grads):
    return lax.psum_scatter(grads, "dp", scatter_dimension=0, tiled=True).astype(F32)


def stacked_columns(pieces, count):
    width = pieces.shape[1] // count
    return jnp.stack([pieces[:, index * width : (index + 1) * width] for index in range(count)])


def body(
    tokens,
    norm_gains,
    first_in,
    first_out,
    attention_in,
    attention_out,
    head_biases,
    gated_in,
    pointwise_out,
    depth_kernel,
    batch_scale,
    batch_shift,
    second_in,
    second_out,
    cotangent,
):
    own_count = tokens.shape[0]
    local_heads = HEAD_TOTAL // lax.axis_size("tensor")
    length = own_count * lax.axis_size("tensor")
    token_count = float(length * lax.axis_size("dp"))
    columns = attention_out.shape[1]
    hidden = first_in.shape[1]
    table = sinusoid(length, tokens.shape[1]).astype(BF16)
    batch = jnp.stack([batch_scale, batch_shift])

    def gather(pieces):
        return lax.all_gather(jnp.concatenate(pieces, 1), "dp", axis=0, tiled=True)

    first_weights = gather([first_in, first_out])
    rest = gather(
        columns_of(attention_in)
        + [attention_out]
        + columns_of(gated_in)
        + [pointwise_out, second_in, second_out]
    )
    attention_weights = rest[:, : 5 * columns]
    conv_weights = rest[:, 5 * columns : 8 * columns]
    second_weights = rest[:, 8 * columns :]

    tokens_all = both_halves(tokens)
    cotangent_all = both_halves(cotangent)

    entries1, pre1, hidden1, part1 = first_forward(tokens_all, norm_gains, first_weights)
    other1 = swap(part1)
    positions = position_forward(table, attention_weights, columns)
    after1, entries2, qc, qp, keys, values, prob, attended, part2 = attention_forward(
        tokens_all, part1, other1, norm_gains, attention_weights, positions, head_biases, local_heads
    )
    other2 = swap(part2)
    after2, entries3, value_pre, gate, convolved, sums = conv_forward(
        after1, part2, other2, norm_gains, conv_weights, depth_kernel
    )
    sums = sum_over(sums, "dp")
    activated, part3 = norm_forward(convolved, sums, batch, conv_weights, token_count)
    other3 = swap(part3)
    after3, entries4, pre4, hidden4, part4 = second_forward(
        after2, part3, other3, norm_gains, second_weights
    )
    other4 = swap(part4)
    out_all, grad4, branch4, slope4, part5, gain5 = second_back(
        after3, part4, other4, cotangent_all, pre4, norm_gains, second_weights
    )
    block_out = own_rows(out_all, own_count)
    other5 = swap(part5)
    grads_second = ff_weight_grads(entries4, slope4, branch4, hidden4, "second_weight_grads")
    grad3, branch3, grad_shifted, grad_sums, gain4 = norm_backward(
        grad4, part5, other5, after3, norm_gains, conv_weights, convolved, sums, batch, token_count
    )
    grad_sums = sum_over(grad_sums, "dp")
    grad_conv, joined3, part6 = conv_backward(
        grad_shifted,
        grad_sums,
        convolved,
        sums,
        batch,
        value_pre,
        gate,
        conv_weights,
        depth_kernel,
        token_count,
    )
    other6 = swap(part6)
    grads_conv, tap_grads = conv_weight_grads(
        entries3, joined3, branch3, activated, value_pre, gate, grad_conv, depth_kernel.shape[0]
    )
    grad2, branch2, joined2, table_grad, part7, gain3, bias_grads = attention_back(
        grad3,
        part6,
        other6,
        after2,
        norm_gains,
        attention_weights,
        positions,
        (qc, qp, keys, values, prob),
        local_heads,
    )
    other7 = swap(part7)
    grads_attention = attention_weight_grads(
        entries2, joined2, table, table_grad, branch2, attended
    )
    grad1, branch1, slope1, part8, gain2 = first_back(
        grad2, part7, other7, after1, pre1, norm_gains, first_weights
    )
    grads_first = ff_weight_grads(entries1, slope1, branch1, hidden1, "first_weight_grads")
    other_start = (1 - lax.axis_index("tensor")) * own_count
    other8 = swap(lax.dynamic_slice_in_dim(part8, other_start, own_count, 0))
    grad_start, gain1 = input_back(
        own_rows(grad1, own_count), own_rows(part8, own_count), other8, tokens, norm_gains
    )

    reduced_a = scatter_weights(jnp.concatenate([grads_second, grads_conv], 1))
    reduced_b = scatter_weights(jnp.concatenate([grads_attention, grads_first], 1))
    reduced_second = reduced_a[:, : 2 * hidden]
    reduced_conv = reduced_a[:, 2 * hidden :]
    reduced_attention = reduced_b[:, : 5 * columns]
    reduced_first = reduced_b[:, 5 * columns :]

    gains = jnp.concatenate([gain1, 0.5 * gain2, 0.5 * gain3, 0.5 * gain4, 0.5 * gain5], 0)
    packed = jnp.concatenate(
        [jnp.reshape(value, (-1, 128)) for value in (gains, tap_grads, bias_grads)], 0
    )
    packed = sum_over(packed, "dp")
    gain_rows = gains.size // 128
    tap_rows = tap_grads.size // 128
    gain_total = sum_over(packed[:gain_rows].reshape(gains.shape), "tensor")
    tap_total = packed[gain_rows : gain_rows + tap_rows].reshape(tap_grads.shape)
    bias_total = packed[gain_rows + tap_rows :].reshape(bias_grads.shape)
    return (
        block_out,
        grad_start,
        gain_total,
        reduced_first[:, :hidden],
        reduced_first[:, hidden:],
        stacked_columns(reduced_attention[:, : 4 * columns], 4),
        reduced_attention[:, 4 * columns :],
        bias_total,
        stacked_columns(reduced_conv[:, : 2 * columns], 2),
        reduced_conv[:, 2 * columns :],
        tap_total,
        grad_sums[1],
        grad_sums[0],
        reduced_second[:, :hidden],
        reduced_second[:, hidden:],
    )


def solution(mesh):
    placed = (
        P(("dp", "tensor"), None),
        P(),
        P("dp", "tensor"),
        P("dp", "tensor"),
        P(None, "dp", "tensor"),
        P("dp", "tensor"),
        P(None, "tensor"),
        P(None, "dp", "tensor"),
        P("dp", "tensor"),
        P(None, "tensor"),
        P("tensor"),
        P("tensor"),
        P("dp", "tensor"),
        P("dp", "tensor"),
        P(("dp", "tensor"), None),
    )
    return jax.shard_map(
        body,
        mesh=mesh,
        in_specs=placed,
        out_specs=(
            P(("dp", "tensor"), None),
            P(("dp", "tensor"), None),
            P(),
            P("dp", "tensor"),
            P("dp", "tensor"),
            P(None, "dp", "tensor"),
            P("dp", "tensor"),
            P(None, "tensor"),
            P(None, "dp", "tensor"),
            P("dp", "tensor"),
            P(None, "tensor"),
            P("tensor"),
            P("tensor"),
            P("dp", "tensor"),
            P("dp", "tensor"),
        ),
        check_vma=False,
    )
```

```python
import math

import jax
import jax.numpy as jnp
from jax import lax
from jax.experimental import pallas as pl
from jax.experimental.pallas import tpu as pltpu
from jax.sharding import PartitionSpec as P

HEAD_TOTAL = 8
EPSILON = 1e-05
BF16 = jnp.bfloat16
F32 = jnp.float32


def matmul(left_side, right_side):
    return jnp.dot(left_side, right_side, preferred_element_type=F32)


def right_transposed(left_side, right_side):
    return lax.dot_general(
        left_side, right_side, (((1,), (1,)), ((), ())), preferred_element_type=F32
    )


def left_transposed(left_side, right_side):
    return lax.dot_general(
        left_side, right_side, (((0,), (0,)), ((), ())), preferred_element_type=F32
    )


def swish_slope(pre_value, gate_sigma):
    return gate_sigma * (1.0 + pre_value * (1.0 - gate_sigma))


def norm_parts(residual):
    centred = residual - jnp.mean(residual, -1, keepdims=True)
    factor = lax.rsqrt(jnp.mean(centred * centred, -1, keepdims=True) + EPSILON)
    return centred * factor, factor


def norm_back(gradient, normed, factor, norm_gain):
    scaled = gradient * norm_gain
    inner_sum = (
        scaled
        - jnp.mean(scaled, -1, keepdims=True)
        - normed * jnp.mean(scaled * normed, -1, keepdims=True)
    )
    return factor * inner_sum, jnp.sum(gradient * normed, 0, keepdims=True)


def sinusoid(length, features):
    offsets = jnp.arange(2 * length, dtype=F32) - (length - 1)
    half_width = features // 2
    frequency = jnp.exp(jnp.arange(half_width, dtype=F32) * (-math.log(10000.0) / half_width))
    angles = offsets[:, None] * frequency[None, :]
    table = jnp.concatenate([jnp.sin(angles), jnp.cos(angles)], 1)
    return jnp.where(offsets[:, None] < length, table, 0.0)


def on_chip(function, name, operands, results, scratch=(), flops=300_000_000):
    count = len(operands)
    total = count + len(results)

    def kernel(*refs):
        function(refs[:count], refs[count:total], refs[total:])

    moved = sum(value.size * value.dtype.itemsize for value in operands)
    moved += sum(math.prod(shape) * jnp.dtype(kind).itemsize for shape, kind in results)
    return pl.pallas_call(
        kernel,
        out_shape=[jax.ShapeDtypeStruct(shape, kind) for shape, kind in results],
        in_specs=[pl.BlockSpec(memory_space=pltpu.VMEM)] * count,
        out_specs=[pl.BlockSpec(memory_space=pltpu.VMEM)] * len(results),
        scratch_shapes=list(scratch),
        compiler_params=pltpu.CompilerParams(vmem_limit_bytes=40 * 1024 * 1024),
        cost_estimate=pl.CostEstimate(flops=flops, bytes_accessed=moved, transcendentals=0),
        name=name,
    )(*operands)


def swap(value):
    return lax.ppermute(value, "tensor", [(0, 1), (1, 0)])


def both_halves(own):
    other = swap(own)
    first = lax.axis_index("tensor") == 0
    return jnp.concatenate([jnp.where(first, own, other), jnp.where(first, other, own)], 0)


def own_half(value):
    half = value.shape[0] // 2
    return jnp.where(lax.axis_index("tensor") == 0, value[:half], value[half:])


def other_half(value):
    half = value.shape[0] // 2
    return jnp.where(lax.axis_index("tensor") == 0, value[half:], value[:half])


def shift(value, axis, mask):
    return lax.ppermute(value, axis, [(k, k ^ mask) for k in range(lax.axis_size(axis))])


def sum_over(value, axis):
    size = lax.axis_size(axis)
    if size & (size - 1):
        return lax.psum(value, axis)
    step = 1
    while step < size:
        if step >= 4 and step * 4 <= size:
            near, far, both = (shift(value, axis, step * times) for times in (1, 2, 3))
            value = (value + near) + (far + both)
            step *= 4
        else:
            value = value + shift(value, axis, step)
            step *= 2
    return value


GATHER_ORDERS = ((8, 4, 2, 1), (8, 2, 4, 1))
SCATTER_ORDERS = ((1, 2, 4, 8), (1, 4, 2, 8))


def doubling():
    return lax.axis_size("dp") == 16


def distances(order):
    blocks = [0]
    for mask in order:
        blocks = blocks + [block ^ mask for block in blocks]
    return blocks


def halving(order):
    return distances(order[::-1])


def gather_stage(pair, stage):
    return tuple(
        jnp.concatenate([value, shift(value, "dp", order[stage])], 0)
        for value, order in zip(pair, GATHER_ORDERS)
    )


def gather_last(pair):
    return tuple((value, shift(value, "dp", 1)) for value in pair)


def tie(values, *others):
    return lax.optimization_barrier((values, others))[0]


def assemble(ref, target_ref, order, half, matrices, first_column):
    device = lax.axis_index("dp")
    blocks = distances(order)
    count = len(blocks) // 2
    rows = target_ref.shape[0] // len(blocks)
    columns = ref.shape[1]
    for place in range(count):
        owner = device ^ blocks[half * count + place]
        target = pl.ds(pl.multiple_of(owner * rows, rows), rows)
        for matrix in range(matrices):
            start = (place * matrices + matrix) * rows
            left = first_column + matrix * columns
            target_ref[target, left : left + columns] = ref[start : start + rows, :]


def scatter_split(total_ref, keep_ref, send_ref, order, matrices):
    device = lax.axis_index("dp")
    blocks = halving(order)
    count = len(blocks) // 2
    rows = total_ref.shape[0] // len(blocks)
    columns = keep_ref.shape[1]
    for place, block in enumerate(blocks):
        source = pl.ds(pl.multiple_of((device ^ block) * rows, rows), rows)
        for matrix in range(matrices):
            piece = total_ref[source, matrix * columns : (matrix + 1) * columns]
            start = ((place % count) * matrices + matrix) * rows
            if place < count:
                keep_ref[start : start + rows, :] = piece
            else:
                send_ref[start : start + rows, :] = piece.astype(BF16)


def scatter_stage(keeps, sends, stage, name):
    arrived = [
        shift(send, "dp", order[stage]) for send, order in zip(sends, SCATTER_ORDERS)
    ]
    groups = len(keeps)
    last = stage == len(SCATTER_ORDERS[0]) - 1
    results = []
    for keep in keeps:
        rows, columns = keep.shape
        if last:
            results.append(((rows, columns), F32))
        else:
            results.append(((rows // 2, columns), F32))
            results.append(((rows // 2, columns), BF16))

    def body(ins, outs, _):
        for group in range(groups):
            total = ins[group][...] + ins[groups + group][...].astype(F32)
            if last:
                outs[group][...] = total
            else:
                half = total.shape[0] // 2
                outs[2 * group][...] = total[:half]
                outs[2 * group + 1][...] = total[half:].astype(BF16)

    values = on_chip(body, name, tuple(keeps) + tuple(arrived), tuple(results), flops=1_000_000)
    if last:
        return values, None
    return values[0::2], values[1::2]


def ff_forward_body(row, residual, gain_ref, weight_ref, outs):
    entries_ref, pre_ref, hidden_ref, part_ref = outs
    half = weight_ref.shape[1] // 2
    normed, _ = norm_parts(residual)
    entries = (normed * gain_ref[row : row + 1, :]).astype(BF16)
    entries_ref[...] = entries
    pre = matmul(entries, weight_ref[:, :half])
    pre_ref[...] = pre
    hidden = (pre * jax.nn.sigmoid(pre)).astype(BF16)
    hidden_ref[...] = hidden
    part_ref[...] = right_transposed(hidden, weight_ref[:, half:]).astype(BF16)


def first_forward(tokens, gains, weights):
    rows, width = tokens.shape
    hidden = weights.shape[1] // 2

    def body(ins, outs, _):
        ff_forward_body(0, ins[0][...].astype(F32), ins[1], ins[2], outs)

    return on_chip(
        body,
        "first_forward",
        (tokens, gains, weights),
        (
            ((rows, width), BF16),
            ((rows, hidden), F32),
            ((rows, hidden), BF16),
            ((rows, width), BF16),
        ),
    )


def second_forward(residual, own, other, gains, weights):
    rows, width = residual.shape
    hidden = weights.shape[1] // 2

    def body(ins, outs, _):
        after = ins[0][...] + (ins[1][...].astype(F32) + ins[2][...].astype(F32))
        outs[0][...] = after
        ff_forward_body(3, after, ins[3], ins[4], outs[1:])

    return on_chip(
        body,
        "second_forward",
        (residual, own, other, gains, weights),
        (
            ((rows, width), F32),
            ((rows, width), BF16),
            ((rows, hidden), F32),
            ((rows, hidden), BF16),
            ((rows, width), BF16),
        ),
    )


def ff_back_body(gradient, pre_ref, weight_ref, branch_ref, slope_ref):
    half = weight_ref.shape[1] // 2
    branch = (0.5 * gradient).astype(BF16)
    branch_ref[...] = branch
    grad_hidden = matmul(branch, weight_ref[:, half:])
    pre = pre_ref[...]
    grad_pre = (grad_hidden * swish_slope(pre, jax.nn.sigmoid(pre))).astype(BF16)
    slope_ref[...] = grad_pre
    return right_transposed(grad_pre, weight_ref[:, :half])


def second_back(residual, own, other, cotangent, pre, gains, weights):
    rows, width = residual.shape
    hidden = weights.shape[1] // 2

    def body(ins, outs, _):
        x_ref, own_ref, other_ref, cot_ref, pre_ref, gain_ref, weight_ref = ins
        out_ref, grad_ref, branch_ref, slope_ref, part_ref, gain_grad_ref = outs
        after = x_ref[...] + 0.5 * (own_ref[...].astype(F32) + other_ref[...].astype(F32))
        normed, factor = norm_parts(after)
        gain = gain_ref[4:5, :]
        out_ref[...] = own_half(normed * gain).astype(BF16)
        gradient, gain_grad_ref[...] = norm_back(
            cot_ref[...].astype(F32), normed, factor, gain
        )
        grad_ref[...] = gradient
        part_ref[...] = ff_back_body(gradient, pre_ref, weight_ref, branch_ref, slope_ref).astype(
            BF16
        )

    return on_chip(
        body,
        "second_back",
        (residual, own, other, cotangent, pre, gains, weights),
        (
            ((rows // 2, width), BF16),
            ((rows, width), F32),
            ((rows, width), BF16),
            ((rows, hidden), BF16),
            ((rows, width), BF16),
            ((1, width), F32),
        ),
    )


def ff_weight_grads(entries, grad_pre, branch, hidden, name):
    width = entries.shape[1]
    half = hidden.shape[1]

    def body(ins, outs, _):
        outs[0][:, :half] = left_transposed(ins[0][...], ins[1][...]).astype(BF16)
        outs[0][:, half:] = left_transposed(ins[2][...], ins[3][...]).astype(BF16)

    return on_chip(
        body, name, (entries, grad_pre, branch, hidden), (((width, 2 * half), BF16),)
    )[0]


def ff_weight_split(entries, grad_pre, branch, hidden, name):
    width = entries.shape[1]
    half = hidden.shape[1]

    def body(ins, outs, scratch):
        for group in range(2):
            scratch[0][...] = left_transposed(ins[2 * group][...], ins[2 * group + 1][...])
            scatter_split(
                scratch[0], outs[2 * group], outs[2 * group + 1], SCATTER_ORDERS[group], 1
            )

    halves = (((width // 2, half), F32), ((width // 2, half), BF16))
    values = on_chip(
        body,
        name,
        (entries, grad_pre, branch, hidden),
        halves + halves,
        scratch=(pltpu.VMEM((width, half), F32),),
    )
    return values[0::2], values[1::2]


def ff_assemble(pairs, width):
    columns = pairs[0][0].shape[1]

    def body(ins, outs, _):
        for group in range(2):
            for half in range(2):
                assemble(
                    ins[2 * group + half],
                    outs[0],
                    GATHER_ORDERS[group],
                    half,
                    1,
                    group * columns,
                )

    return on_chip(
        body,
        "first_assemble",
        pairs[0] + pairs[1],
        (((width, 2 * columns), BF16),),
        flops=1_000_000,
    )[0]


def position_forward(table, weights, columns):
    def body(ins, outs, _):
        outs[0][...] = matmul(ins[0][...], ins[1][:, 3 * columns : 4 * columns]).astype(BF16)

    return on_chip(body, "position_forward", (table, weights), (((table.shape[0], columns), BF16),))[0]


def attention_forward(tokens, own, other, gains, weights, positions, biases, heads):
    rows, width = tokens.shape
    columns = biases.shape[1]
    features = columns // heads
    scale = features ** (-0.5)

    def body(ins, outs, _):
        x_ref, own_ref, other_ref, gain_ref, weight_ref, table_ref, bias_ref = ins
        after_ref, e_ref, qc_ref, qp_ref, k_ref, v_ref, prob_ref, mix_ref, part_ref = outs
        after = x_ref[...].astype(F32) + 0.5 * (
            own_ref[...].astype(F32) + other_ref[...].astype(F32)
        )
        after_ref[...] = after
        normed, _ = norm_parts(after)
        entries = (normed * gain_ref[1:2, :]).astype(BF16)
        e_ref[...] = entries
        joined = matmul(entries, weight_ref[:, : 3 * columns])
        queries = joined[:, :columns]
        content_q = (queries + bias_ref[0:1, :]).astype(BF16)
        position_q = (queries + bias_ref[1:2, :]).astype(BF16)
        keys = joined[:, columns : 2 * columns].astype(BF16)
        values = joined[:, 2 * columns :].astype(BF16)
        qc_ref[...] = content_q
        qp_ref[...] = position_q
        k_ref[...] = keys
        v_ref[...] = values
        mixed = []
        for head in range(heads):
            part = slice(head * features, (head + 1) * features)
            content = right_transposed(content_q[:, part], keys[:, part])
            raw = right_transposed(position_q[:, part], table_ref[:, part])
            shifted = pltpu.roll(raw, rows + 1, 1, stride=1, stride_axis=0)[:, :rows]
            scores = (content + shifted) * scale
            lifted = jnp.exp(scores - jnp.max(scores, -1, keepdims=True))
            probability = lifted / jnp.sum(lifted, -1, keepdims=True)
            prob_ref[head] = probability
            mixed.append(matmul(probability.astype(BF16), values[:, part]))
        attended = jnp.concatenate(mixed, 1).astype(BF16)
        mix_ref[...] = attended
        part_ref[...] = right_transposed(attended, weight_ref[:, 4 * columns : 5 * columns]).astype(BF16)

    local = ((rows, columns), BF16)
    return on_chip(
        body,
        "attention_forward",
        (tokens, own, other, gains, weights, positions, biases),
        (
            ((rows, width), F32),
            ((rows, width), BF16),
            local,
            local,
            local,
            local,
            ((heads, rows, rows), F32),
            local,
            ((rows, width), BF16),
        ),
    )


def attention_back(gradient, own, other, residual, gains, weights, positions, kept, heads):
    rows, width = residual.shape
    columns = positions.shape[1]
    features = columns // heads
    scale = features ** (-0.5)

    def body(ins, outs, _):
        (
            grad_ref,
            own_ref,
            other_ref,
            x_ref,
            gain_ref,
            weight_ref,
            table_ref,
            qc_ref,
            qp_ref,
            k_ref,
            v_ref,
            prob_ref,
        ) = ins
        total_ref, branch_ref, joined_ref, table_grad_ref, part_ref, gain_grad_ref, bias_ref = outs
        normed, factor = norm_parts(x_ref[...])
        passed, gain_grad_ref[...] = norm_back(
            own_ref[...].astype(F32) + other_ref[...].astype(F32), normed, factor, gain_ref[2:3, :]
        )
        total = grad_ref[...] + passed
        total_ref[...] = total
        branch = total.astype(BF16)
        branch_ref[...] = branch
        grad_mixed = matmul(branch, weight_ref[:, 4 * columns : 5 * columns]).astype(BF16)
        line = lax.broadcasted_iota(jnp.int32, (rows, rows), 0)
        place = lax.broadcasted_iota(jnp.int32, (rows, rows), 1)
        flip = (line + place == rows - 1).astype(F32).astype(BF16)
        content_q = qc_ref[...]
        keys = k_ref[...]
        values = v_ref[...]
        flipped_q = matmul(flip, qp_ref[...]).astype(BF16)
        zeros = jnp.zeros((rows, rows), F32)
        from_content, from_position, to_keys, to_values, to_table = [], [], [], [], []
        for head in range(heads):
            part = slice(head * features, (head + 1) * features)
            probability = prob_ref[head]
            grad_probability = right_transposed(grad_mixed[:, part], values[:, part])
            to_values.append(left_transposed(probability.astype(BF16), grad_mixed[:, part]))
            inner = jnp.sum(probability * grad_probability, -1, keepdims=True)
            grad_scores = (probability * (grad_probability - inner)).astype(BF16) * scale
            grad_scores = grad_scores.astype(BF16)
            from_content.append(matmul(grad_scores, keys[:, part]))
            to_keys.append(left_transposed(grad_scores, content_q[:, part]))
            flipped = jnp.concatenate([matmul(flip, grad_scores), zeros], 1)
            spread = pltpu.roll(flipped, 0, 1, stride=1, stride_axis=0).astype(BF16)
            from_position.append(matmul(spread, table_ref[:, part]))
            to_table.append(left_transposed(spread, flipped_q[:, part]))
        grad_content = jnp.concatenate(from_content, 1)
        grad_position = jnp.concatenate(from_position, 1)
        high = grad_position.astype(BF16)
        low = (grad_position - high.astype(F32)).astype(BF16)
        grad_position = matmul(flip, high) + matmul(flip, low)
        bias_ref[0:1, :] = jnp.sum(grad_content, 0, keepdims=True)
        bias_ref[1:2, :] = jnp.sum(grad_position, 0, keepdims=True)
        joined = jnp.concatenate(
            [grad_content + grad_position] + to_keys + to_values, 1
        ).astype(BF16)
        joined_ref[...] = joined
        table_grad_ref[...] = jnp.concatenate(to_table, 1).astype(BF16)
        part_ref[...] = right_transposed(joined, weight_ref[:, : 3 * columns]).astype(BF16)

    return on_chip(
        body,
        "attention_back",
        (gradient, own, other, residual, gains, weights, positions) + tuple(kept),
        (
            ((rows, width), F32),
            ((rows, width), BF16),
            ((rows, 3 * columns), BF16),
            ((2 * rows, columns), BF16),
            ((rows, width), BF16),
            ((1, width), F32),
            ((2, columns), F32),
        ),
    )


def mixed_assemble(pairs, width):
    columns = pairs[0][0].shape[1]

    def body(ins, outs, _):
        for group in range(2):
            for half in range(2):
                assemble(
                    ins[2 * group + half],
                    outs[0],
                    GATHER_ORDERS[group],
                    half,
                    4,
                    4 * group * columns,
                )

    return on_chip(
        body,
        "mixed_assemble",
        pairs[0] + pairs[1],
        (((width, 8 * columns), BF16),),
        flops=1_000_000,
    )[0]


def mixed_weight_grads(attention_parts, conv_parts, split):
    entries, joined, table, table_grad, branch, attended = attention_parts
    conv_entries, conv_joined, conv_branch, activated = conv_parts
    width = entries.shape[1]
    columns = attended.shape[1]

    def whole(ins, target_ref):
        target_ref[:, : 3 * columns] = left_transposed(ins[0][...], ins[1][...])
        target_ref[:, 3 * columns : 4 * columns] = left_transposed(ins[2][...], ins[3][...])
        target_ref[:, 4 * columns : 5 * columns] = left_transposed(ins[4][...], ins[5][...])
        target_ref[:, 5 * columns : 7 * columns] = left_transposed(ins[6][...], ins[7][...])
        target_ref[:, 7 * columns :] = left_transposed(ins[8][...], ins[9][...])

    def body(ins, outs, scratch):
        if not split:
            whole(ins, outs[0])
            return
        whole(ins, scratch[0])
        for group in range(2):
            part = scratch[0].at[:, 4 * group * columns : 4 * (group + 1) * columns]
            scatter_split(part, outs[2 * group], outs[2 * group + 1], SCATTER_ORDERS[group], 4)

    operands = (
        entries,
        joined,
        table,
        table_grad,
        branch,
        attended,
        conv_entries,
        conv_joined,
        conv_branch,
        activated,
    )
    if not split:
        return on_chip(body, "mixed_weight_grads", operands, (((width, 8 * columns), F32),))[0]
    halves = (((2 * width, columns), F32), ((2 * width, columns), BF16))
    values = on_chip(
        body,
        "mixed_weight_grads",
        operands,
        halves + halves,
        scratch=(pltpu.VMEM((width, 8 * columns), F32),),
    )
    return values[0::2], values[1::2]


PAD = 16


def conv_forward(residual, own, other, gains, weights, depth_kernel):
    rows, width = residual.shape
    taps, columns = depth_kernel.shape
    half_taps = (taps - 1) // 2

    def body(ins, outs, scratch):
        x_ref, own_ref, other_ref, gain_ref, weight_ref, tap_ref = ins
        after_ref, c_ref, value_ref, gate_ref, conv_ref, sums_ref = outs
        padded = scratch[0]
        after = x_ref[...] + (own_ref[...].astype(F32) + other_ref[...].astype(F32))
        after_ref[...] = after
        normed, _ = norm_parts(after)
        entries = (normed * gain_ref[2:3, :]).astype(BF16)
        c_ref[...] = entries
        joined = matmul(entries, weight_ref[:, 5 * columns : 7 * columns])
        value = joined[:, :columns]
        gate = jax.nn.sigmoid(joined[:, columns:])
        value_ref[...] = value
        gate_ref[...] = gate
        padded[:PAD, :] = jnp.zeros((PAD, columns), F32)
        padded[PAD + rows :, :] = jnp.zeros((PAD, columns), F32)
        padded[PAD : PAD + rows, :] = value * gate
        total = jnp.zeros((rows, columns), F32)
        for tap in range(taps):
            start = PAD - half_taps + tap
            total = total + tap_ref[tap : tap + 1, :] * padded[start : start + rows, :]
        conv_ref[...] = total
        sums_ref[0:1, :] = jnp.sum(total, 0, keepdims=True)
        sums_ref[1:2, :] = jnp.sum(total * total, 0, keepdims=True)

    local = ((rows, columns), F32)
    return on_chip(
        body,
        "conv_forward",
        (residual, own, other, gains, weights, depth_kernel),
        (((rows, width), F32), ((rows, width), BF16), local, local, local, ((2, columns), F32)),
        scratch=(pltpu.VMEM((rows + 2 * PAD, columns), F32),),
    )


def batch_norm(conv_ref, sums_ref, batch_ref, token_count):
    column_mean = sums_ref[0:1, :] / token_count
    inverse = lax.rsqrt(sums_ref[1:2, :] / token_count - column_mean * column_mean + EPSILON)
    standard = (conv_ref[...] - column_mean) * inverse
    return standard, inverse, standard * batch_ref[0:1, :] + batch_ref[1:2, :]


def norm_forward(convolved, sums, batch, weights, token_count):
    rows, columns = convolved.shape
    width = weights.shape[0]

    def body(ins, outs, _):
        conv_ref, sums_ref, batch_ref, weight_ref = ins
        _, _, shifted = batch_norm(conv_ref, sums_ref, batch_ref, token_count)
        activated = (shifted * jax.nn.sigmoid(shifted)).astype(BF16)
        outs[0][...] = activated
        outs[1][...] = right_transposed(activated, weight_ref[:, 7 * columns :]).astype(BF16)

    return on_chip(
        body,
        "norm_forward",
        (convolved, sums, batch, weights),
        (((rows, columns), BF16), ((rows, width), BF16)),
    )


def norm_backward(gradient, own, other, residual, gains, weights, convolved, sums, batch, count):
    rows, columns = convolved.shape
    width = weights.shape[0]

    def body(ins, outs, _):
        grad_ref, own_ref, other_ref, x_ref, gain_ref, weight_ref, conv_ref, sums_ref, batch_ref = (
            ins
        )
        total_ref, branch_ref, shifted_ref, grad_sums_ref, gain_grad_ref = outs
        normed, factor = norm_parts(x_ref[...])
        passed, gain_grad_ref[...] = norm_back(
            own_ref[...].astype(F32) + other_ref[...].astype(F32), normed, factor, gain_ref[3:4, :]
        )
        total = grad_ref[...] + passed
        total_ref[...] = total
        branch = total.astype(BF16)
        branch_ref[...] = branch
        standard, _, shifted = batch_norm(conv_ref, sums_ref, batch_ref, count)
        grad_shifted = matmul(branch, weight_ref[:, 7 * columns :]) * swish_slope(
            shifted, jax.nn.sigmoid(shifted)
        )
        shifted_ref[...] = grad_shifted
        grad_sums_ref[0:1, :] = jnp.sum(grad_shifted, 0, keepdims=True)
        grad_sums_ref[1:2, :] = jnp.sum(grad_shifted * standard, 0, keepdims=True)

    return on_chip(
        body,
        "norm_backward",
        (gradient, own, other, residual, gains, weights, convolved, sums, batch),
        (
            ((rows, width), F32),
            ((rows, width), BF16),
            ((rows, columns), F32),
            ((2, columns), F32),
            ((1, width), F32),
        ),
    )


def conv_backward(
    grad_shifted, grad_sums, convolved, sums, batch, value, gate, weights, depth_kernel, count
):
    rows, columns = convolved.shape
    width = weights.shape[0]
    taps = depth_kernel.shape[0]
    half_taps = (taps - 1) // 2

    def body(ins, outs, scratch):
        (
            shifted_ref,
            grad_sums_ref,
            conv_ref,
            sums_ref,
            batch_ref,
            value_ref,
            gate_ref,
            weight_ref,
            tap_ref,
        ) = ins
        grad_conv_ref, joined_ref, part_ref = outs
        padded = scratch[0]
        standard, inverse, _ = batch_norm(conv_ref, sums_ref, batch_ref, count)
        grad_conv = (inverse * batch_ref[0:1, :]) * (
            shifted_ref[...]
            - grad_sums_ref[0:1, :] / count
            - standard * (grad_sums_ref[1:2, :] / count)
        )
        grad_conv_ref[...] = grad_conv
        padded[:PAD, :] = jnp.zeros((PAD, columns), F32)
        padded[PAD + rows :, :] = jnp.zeros((PAD, columns), F32)
        padded[PAD : PAD + rows, :] = grad_conv
        total = jnp.zeros((rows, columns), F32)
        for tap in range(taps):
            start = PAD + half_taps - tap
            total = total + tap_ref[tap : tap + 1, :] * padded[start : start + rows, :]
        gate_sigma = gate_ref[...]
        grad_value = total * gate_sigma
        joined = jnp.concatenate(
            [grad_value, grad_value * value_ref[...] * (1.0 - gate_sigma)], 1
        ).astype(BF16)
        joined_ref[...] = joined
        part_ref[...] = right_transposed(joined, weight_ref[:, 5 * columns : 7 * columns]).astype(BF16)

    return on_chip(
        body,
        "conv_backward",
        (grad_shifted, grad_sums, convolved, sums, batch, value, gate, weights, depth_kernel),
        (((rows, columns), F32), ((rows, 2 * columns), BF16), ((rows, width), BF16)),
        scratch=(pltpu.VMEM((rows + 2 * PAD, columns), F32),),
    )


def tap_gradients(value, gate, grad_conv, taps):
    rows, columns = grad_conv.shape
    half_taps = (taps - 1) // 2

    def body(ins, outs, scratch):
        value_ref, gate_ref, grad_ref = ins
        padded = scratch[0]
        padded[:PAD, :] = jnp.zeros((PAD, columns), F32)
        padded[PAD + rows :, :] = jnp.zeros((PAD, columns), F32)
        padded[PAD : PAD + rows, :] = value_ref[...] * gate_ref[...]
        grad_conv_value = grad_ref[...]
        for tap in range(taps):
            start = PAD - half_taps + tap
            outs[0][tap : tap + 1, :] = jnp.sum(
                padded[start : start + rows, :] * grad_conv_value, 0, keepdims=True
            )

    return on_chip(
        body,
        "tap_gradients",
        (value, gate, grad_conv),
        (((taps, columns), F32),),
        scratch=(pltpu.VMEM((rows + 2 * PAD, columns), F32),),
        flops=10_000_000,
    )[0]


def first_back(gradient, own, other, residual, pre, gains, weights):
    rows, width = residual.shape
    hidden = weights.shape[1] // 2

    def body(ins, outs, _):
        grad_ref, own_ref, other_ref, x_ref, pre_ref, gain_ref, weight_ref = ins
        total_ref, branch_ref, slope_ref, keep_ref, send_ref, gain_grad_ref = outs
        normed, factor = norm_parts(x_ref[...])
        passed, gain_grad_ref[...] = norm_back(
            own_ref[...].astype(F32) + other_ref[...].astype(F32), normed, factor, gain_ref[1:2, :]
        )
        total = grad_ref[...] + passed
        total_ref[...] = own_half(total)
        part = ff_back_body(total, pre_ref, weight_ref, branch_ref, slope_ref)
        keep_ref[...] = own_half(part)
        send_ref[...] = other_half(part).astype(BF16)

    return on_chip(
        body,
        "first_back",
        (gradient, own, other, residual, pre, gains, weights),
        (
            ((rows // 2, width), F32),
            ((rows, width), BF16),
            ((rows, hidden), BF16),
            ((rows // 2, width), F32),
            ((rows // 2, width), BF16),
            ((1, width), F32),
        ),
    )


def input_back(gradient, own, other, tokens, gains):
    rows, width = tokens.shape

    def body(ins, outs, _):
        grad_ref, own_ref, other_ref, x_ref, gain_ref = ins
        normed, factor = norm_parts(x_ref[...].astype(F32))
        passed, outs[1][...] = norm_back(
            own_ref[...].astype(F32) + other_ref[...].astype(F32), normed, factor, gain_ref[0:1, :]
        )
        outs[0][...] = grad_ref[...] + passed

    return on_chip(
        body,
        "input_back",
        (gradient, own, other, tokens, gains),
        (((rows, width), F32), ((1, width), F32)),
        flops=1_000_000,
    )


def reduce_plain(grads):
    return lax.psum_scatter(grads.astype(BF16), "dp", scatter_dimension=0, tiled=True).astype(F32)


def stacked_columns(pieces, count):
    width = pieces.shape[1] // count
    return jnp.stack([pieces[:, index * width : (index + 1) * width] for index in range(count)])


def unstacked(stacked):
    return [stacked[index] for index in range(stacked.shape[0])]


def body(
    tokens,
    norm_gains,
    first_in,
    first_out,
    attention_in,
    attention_out,
    head_biases,
    gated_in,
    pointwise_out,
    depth_kernel,
    batch_scale,
    batch_shift,
    second_in,
    second_out,
    cotangent,
):
    local_heads = HEAD_TOTAL // lax.axis_size("tensor")
    length = tokens.shape[0] * lax.axis_size("tensor")
    token_count = float(length * lax.axis_size("dp"))
    columns = attention_out.shape[1]
    hidden = first_in.shape[1]
    width = tokens.shape[1]
    table = sinusoid(length, width).astype(BF16)
    batch = jnp.stack([batch_scale, batch_shift])
    split = doubling()

    def gather(pieces):
        return lax.all_gather(jnp.concatenate(pieces, 1), "dp", axis=0, tiled=True)

    tokens_all = both_halves(tokens)
    cotangent_all = both_halves(cotangent)

    if split:
        batch_one = (first_in, first_out)
        batch_two = (
            attention_in.reshape(-1, columns),
            jnp.concatenate([attention_out, gated_in.reshape(-1, columns), pointwise_out], 0),
        )
        for stage in range(3):
            batch_one = gather_stage(batch_one, stage)
            batch_two = gather_stage(tie(batch_two, batch_one), stage)
        second_pieces = tie((second_in, second_out), batch_one)
        batch_one = gather_last(batch_one)
        first_weights = ff_assemble(batch_one, width)
        batch_two = gather_last(tie(batch_two, batch_one))
        mixed_weights = mixed_assemble(batch_two, width)
        second_weights = gather(second_pieces)
    else:
        first_weights = gather([first_in, first_out])
        mixed_weights = gather(
            unstacked(attention_in) + [attention_out] + unstacked(gated_in) + [pointwise_out]
        )
        second_weights = gather([second_in, second_out])

    entries1, pre1, hidden1, part1 = first_forward(tokens_all, norm_gains, first_weights)
    other1 = swap(part1)
    positions = position_forward(table, mixed_weights, columns)
    after1, entries2, qc, qp, keys, values, prob, attended, part2 = attention_forward(
        tokens_all, part1, other1, norm_gains, mixed_weights, positions, head_biases, local_heads
    )
    other2 = swap(part2)
    after2, entries3, value_pre, gate, convolved, sums = conv_forward(
        after1, part2, other2, norm_gains, mixed_weights, depth_kernel
    )
    sums = sum_over(sums, "dp")
    activated, part3 = norm_forward(convolved, sums, batch, mixed_weights, token_count)
    other3 = swap(part3)
    after3, entries4, pre4, hidden4, part4 = second_forward(
        after2, part3, other3, norm_gains, second_weights
    )
    other4 = swap(part4)
    block_out, grad4, branch4, slope4, part5, gain5 = second_back(
        after3, part4, other4, cotangent_all, pre4, norm_gains, second_weights
    )
    other5 = swap(part5)
    grads_second = ff_weight_grads(entries4, slope4, branch4, hidden4, "second_weight_grads")
    other5 = tie(other5, grads_second)
    reduced_second = reduce_plain(grads_second)
    grad3, branch3, grad_shifted, grad_sums, gain4 = norm_backward(
        grad4, part5, other5, after3, norm_gains, mixed_weights, convolved, sums, batch, token_count
    )
    grad_sums = sum_over(grad_sums, "dp")
    grad_conv, joined3, part6 = conv_backward(
        grad_shifted,
        grad_sums,
        convolved,
        sums,
        batch,
        value_pre,
        gate,
        mixed_weights,
        depth_kernel,
        token_count,
    )
    other6 = swap(part6)
    tap_grads = tap_gradients(value_pre, gate, grad_conv, depth_kernel.shape[0])
    grad2, branch2, joined2, table_grad, part7, gain3, bias_grads = attention_back(
        grad3,
        part6,
        other6,
        after2,
        norm_gains,
        mixed_weights,
        positions,
        (qc, qp, keys, values, prob),
        local_heads,
    )
    other7 = swap(part7)
    mixed_grads = mixed_weight_grads(
        (entries2, joined2, table, table_grad, branch2, attended),
        (entries3, joined3, branch3, activated),
        split,
    )
    grad1, branch1, slope1, keep8, send8, gain2 = first_back(
        grad2, part7, other7, after1, pre1, norm_gains, first_weights
    )
    if split:
        first_grads = ff_weight_split(entries1, slope1, branch1, hidden1, "first_weight_grads")
        for stage in range(4):
            mixed_grads = scatter_stage(*mixed_grads, stage, "mixed_sum")
            first_grads = scatter_stage(*first_grads, stage, "first_sum")
        (mixed_a, mixed_b), (reduced_in, reduced_out) = mixed_grads[0], first_grads[0]
        rows = mixed_a.shape[0] // 4
        reduced_attention = mixed_a.reshape(4, rows, columns)
        reduced_mixing = mixed_b[:rows]
        reduced_gated = mixed_b[rows : 3 * rows].reshape(2, rows, columns)
        reduced_pointwise = mixed_b[3 * rows :]
    else:
        first_grads = reduce_plain(
            ff_weight_grads(entries1, slope1, branch1, hidden1, "first_weight_grads")
        )
        reduced_in, reduced_out = first_grads[:, :hidden], first_grads[:, hidden:]
        mixed = reduce_plain(mixed_grads)
        reduced_attention = stacked_columns(mixed[:, : 4 * columns], 4)
        reduced_mixing = mixed[:, 4 * columns : 5 * columns]
        reduced_gated = stacked_columns(mixed[:, 5 * columns : 7 * columns], 2)
        reduced_pointwise = mixed[:, 7 * columns :]
    other8 = swap(send8)
    grad_start, gain1 = input_back(grad1, keep8, other8, tokens, norm_gains)

    gains = jnp.concatenate([gain1, 0.5 * gain2, 0.5 * gain3, 0.5 * gain4, 0.5 * gain5], 0)
    packed = jnp.concatenate(
        [jnp.reshape(value, (-1, 128)) for value in (gains, tap_grads, bias_grads)], 0
    )
    packed = sum_over(packed, "dp")
    gain_rows = gains.size // 128
    tap_rows = tap_grads.size // 128
    gain_total = sum_over(packed[:gain_rows].reshape(gains.shape), "tensor")
    tap_total = packed[gain_rows : gain_rows + tap_rows].reshape(tap_grads.shape)
    bias_total = packed[gain_rows + tap_rows :].reshape(bias_grads.shape)
    return (
        block_out,
        grad_start,
        gain_total,
        reduced_in,
        reduced_out,
        reduced_attention,
        reduced_mixing,
        bias_total,
        reduced_gated,
        reduced_pointwise,
        tap_total,
        grad_sums[1],
        grad_sums[0],
        reduced_second[:, :hidden],
        reduced_second[:, hidden:],
    )


def solution(mesh):
    placed = (
        P(("dp", "tensor"), None),
        P(),
        P("dp", "tensor"),
        P("dp", "tensor"),
        P(None, "dp", "tensor"),
        P("dp", "tensor"),
        P(None, "tensor"),
        P(None, "dp", "tensor"),
        P("dp", "tensor"),
        P(None, "tensor"),
        P("tensor"),
        P("tensor"),
        P("dp", "tensor"),
        P("dp", "tensor"),
        P(("dp", "tensor"), None),
    )
    return jax.shard_map(
        body,
        mesh=mesh,
        in_specs=placed,
        out_specs=(
            P(("dp", "tensor"), None),
            P(("dp", "tensor"), None),
            P(),
            P("dp", "tensor"),
            P("dp", "tensor"),
            P(None, "dp", "tensor"),
            P("dp", "tensor"),
            P(None, "tensor"),
            P(None, "dp", "tensor"),
            P("dp", "tensor"),
            P(None, "tensor"),
            P("tensor"),
            P("tensor"),
            P("dp", "tensor"),
            P("dp", "tensor"),
        ),
        check_vma=False,
    )
```

```python
import math

import jax
import jax.numpy as jnp
from jax import lax
from jax.experimental import pallas as pl
from jax.experimental.pallas import tpu as pltpu
from jax.sharding import PartitionSpec as P

HEAD_TOTAL = 8
EPSILON = 1e-05
BF16 = jnp.bfloat16
F32 = jnp.float32


def matmul(left_side, right_side):
    return jnp.dot(left_side, right_side, preferred_element_type=F32)


def right_transposed(left_side, right_side):
    return lax.dot_general(
        left_side, right_side, (((1,), (1,)), ((), ())), preferred_element_type=F32
    )


def left_transposed(left_side, right_side):
    return lax.dot_general(
        left_side, right_side, (((0,), (0,)), ((), ())), preferred_element_type=F32
    )


def swish_slope(pre_value, gate_sigma):
    return gate_sigma * (1.0 + pre_value * (1.0 - gate_sigma))


def norm_parts(residual):
    centred = residual - jnp.mean(residual, -1, keepdims=True)
    factor = lax.rsqrt(jnp.mean(centred * centred, -1, keepdims=True) + EPSILON)
    return centred * factor, factor


def norm_back(gradient, normed, factor, norm_gain):
    scaled = gradient * norm_gain
    inner_sum = (
        scaled
        - jnp.mean(scaled, -1, keepdims=True)
        - normed * jnp.mean(scaled * normed, -1, keepdims=True)
    )
    return factor * inner_sum, jnp.sum(gradient * normed, 0, keepdims=True)


def sinusoid(length, features):
    offsets = jnp.arange(2 * length, dtype=F32) - (length - 1)
    half_width = features // 2
    frequency = jnp.exp(jnp.arange(half_width, dtype=F32) * (-math.log(10000.0) / half_width))
    angles = offsets[:, None] * frequency[None, :]
    table = jnp.concatenate([jnp.sin(angles), jnp.cos(angles)], 1)
    return jnp.where(offsets[:, None] < length, table, 0.0)


class Fetched:
    def __init__(self, source, buffer, semaphore):
        self.copy = pltpu.make_async_copy(source, buffer, semaphore)
        self.copy.start()
        self.buffer = buffer
        self.shape = buffer.shape
        self.pending = True

    def finish(self):
        if self.pending:
            self.copy.wait()
            self.pending = False

    def __getitem__(self, index):
        self.finish()
        return self.buffer[index]


class Stored:
    def __init__(self, target, buffer, semaphore):
        self.copy = pltpu.make_async_copy(buffer, target, semaphore)
        self.buffer = buffer
        self.shape = buffer.shape
        self.started = False

    def start(self):
        if not self.started:
            self.copy.start()
            self.started = True

    def finish(self):
        self.start()
        self.copy.wait()

    def __getitem__(self, index):
        return self.buffer[index]

    def __setitem__(self, index, value):
        self.buffer[index] = value
        if index is Ellipsis:
            self.start()


def far(shape, kind):
    return (shape, kind, True)


def on_chip(function, name, operands, results, scratch=(), flops=300_000_000, fetch=()):
    count = len(operands)
    total = count + len(results)
    fetch = tuple(sorted(fetch))
    distant = [index for index, result in enumerate(results) if len(result) == 3]
    buffers = [pltpu.VMEM(operands[index].shape, operands[index].dtype) for index in fetch]
    buffers += [pltpu.VMEM(results[index][0], results[index][1]) for index in distant]
    moves = len(buffers)
    semaphores = [pltpu.SemaphoreType.DMA((moves,))] if moves else []

    def kernel(*refs):
        ins, outs = list(refs[:count]), list(refs[count:total])
        spaces = refs[total : total + moves]
        if moves:
            semaphore = refs[total + moves]
        for place, index in enumerate(fetch):
            ins[index] = Fetched(ins[index], spaces[place], semaphore.at[place])
        for place, index in enumerate(distant, len(fetch)):
            outs[index] = Stored(outs[index], spaces[place], semaphore.at[place])
        function(ins, outs, refs[total + moves + len(semaphores) :])
        for index in fetch:
            ins[index].finish()
        for index in distant:
            outs[index].finish()

    def place(is_far):
        return pl.BlockSpec(memory_space=pltpu.HBM if is_far else pltpu.VMEM)

    moved = sum(value.size * value.dtype.itemsize for value in operands)
    moved += sum(math.prod(r[0]) * jnp.dtype(r[1]).itemsize for r in results)
    return pl.pallas_call(
        kernel,
        out_shape=[jax.ShapeDtypeStruct(r[0], r[1]) for r in results],
        in_specs=[place(index in fetch) for index in range(count)],
        out_specs=[place(index in distant) for index in range(len(results))],
        scratch_shapes=buffers + semaphores + list(scratch),
        compiler_params=pltpu.CompilerParams(vmem_limit_bytes=32 * 1024 * 1024),
        cost_estimate=pl.CostEstimate(flops=flops, bytes_accessed=moved, transcendentals=0),
        name=name,
    )(*operands)


def swap(value):
    return lax.ppermute(value, "tensor", [(0, 1), (1, 0)])


def both_halves(own):
    other = swap(own)
    first = lax.axis_index("tensor") == 0
    return jnp.concatenate([jnp.where(first, own, other), jnp.where(first, other, own)], 0)


def own_half(value):
    half = value.shape[0] // 2
    return jnp.where(lax.axis_index("tensor") == 0, value[:half], value[half:])


def other_half(value):
    half = value.shape[0] // 2
    return jnp.where(lax.axis_index("tensor") == 0, value[half:], value[:half])


def shift(value, axis, mask):
    return lax.ppermute(value, axis, [(k, k ^ mask) for k in range(lax.axis_size(axis))])


def sum_over(value, axis):
    size = lax.axis_size(axis)
    if size & (size - 1):
        return lax.psum(value, axis)
    step = 1
    while step < size:
        if step >= 4 and step * 4 <= size:
            near, far, both = (shift(value, axis, step * times) for times in (1, 2, 3))
            value = (value + near) + (far + both)
            step *= 4
        else:
            value = value + shift(value, axis, step)
            step *= 2
    return value


GATHER_ORDERS = ((8, 4, 2, 1), (8, 2, 4, 1))
SCATTER_ORDERS = ((1, 2, 4, 8), (1, 4, 2, 8))


def doubling():
    return lax.axis_size("dp") == 16


def distances(order):
    blocks = [0]
    for mask in order:
        blocks = blocks + [block ^ mask for block in blocks]
    return blocks


def halving(order):
    return distances(order[::-1])


def gather_stage(pair, stage):
    return tuple(
        jnp.concatenate([value, shift(value, "dp", order[stage])], 0)
        for value, order in zip(pair, GATHER_ORDERS)
    )


def gather_last(pair):
    return tuple((value, shift(value, "dp", 1)) for value in pair)


def tie(values, *others):
    return lax.optimization_barrier((values, others))[0]


def assemble(ref, target_ref, order, half, matrices, first_column):
    device = lax.axis_index("dp")
    blocks = distances(order)
    count = len(blocks) // 2
    rows = target_ref.shape[0] // len(blocks)
    columns = ref.shape[1]
    for place in range(count):
        owner = device ^ blocks[half * count + place]
        target = pl.ds(pl.multiple_of(owner * rows, rows), rows)
        for matrix in range(matrices):
            start = (place * matrices + matrix) * rows
            left = first_column + matrix * columns
            target_ref[target, left : left + columns] = ref[start : start + rows, :]


def scatter_split(total_ref, keep_ref, send_ref, order, matrices):
    device = lax.axis_index("dp")
    blocks = halving(order)
    count = len(blocks) // 2
    rows = total_ref.shape[0] // len(blocks)
    columns = keep_ref.shape[1]
    for place, block in enumerate(blocks):
        source = pl.ds(pl.multiple_of((device ^ block) * rows, rows), rows)
        for matrix in range(matrices):
            piece = total_ref[source, matrix * columns : (matrix + 1) * columns]
            start = ((place % count) * matrices + matrix) * rows
            if place < count:
                keep_ref[start : start + rows, :] = piece
            else:
                send_ref[start : start + rows, :] = piece.astype(BF16)


def scatter_stage(keeps, sends, stage, name, fetch=()):
    arrived = [
        shift(send, "dp", order[stage]) for send, order in zip(sends, SCATTER_ORDERS)
    ]
    groups = len(keeps)
    last = stage == len(SCATTER_ORDERS[0]) - 1
    results = []
    for keep in keeps:
        rows, columns = keep.shape
        if last:
            results.append(((rows, columns), F32))
        else:
            results.append(((rows // 2, columns), F32))
            results.append(((rows // 2, columns), BF16))

    def body(ins, outs, _):
        for group in range(groups):
            total = ins[group][...] + ins[groups + group][...].astype(F32)
            if last:
                outs[group][...] = total
            else:
                half = total.shape[0] // 2
                outs[2 * group][...] = total[:half]
                outs[2 * group + 1][...] = total[half:].astype(BF16)

    values = on_chip(body, name, tuple(keeps) + tuple(arrived), tuple(results), flops=1_000_000, fetch=fetch)
    if last:
        return values, None
    return values[0::2], values[1::2]


def ff_forward_body(row, residual, gain_ref, weight_ref, outs):
    entries_ref, pre_ref, hidden_ref, part_ref = outs
    half = weight_ref.shape[1] // 2
    normed, _ = norm_parts(residual)
    entries = (normed * gain_ref[row : row + 1, :]).astype(BF16)
    entries_ref[...] = entries
    pre = matmul(entries, weight_ref[:, :half])
    pre_ref[...] = pre
    hidden = (pre * jax.nn.sigmoid(pre)).astype(BF16)
    hidden_ref[...] = hidden
    part_ref[...] = right_transposed(hidden, weight_ref[:, half:]).astype(BF16)


def first_forward(tokens, gains, weights):
    rows, width = tokens.shape
    split = isinstance(weights, tuple)
    pieces = weights[0] + weights[1] if split else (weights,)
    hidden = pieces[0].shape[1] if split else weights.shape[1] // 2

    def body(ins, outs, scratch):
        weight_ref = ins[2]
        if split:
            weight_ref = outs[4]
            for group in range(2):
                for half in range(2):
                    piece = ins[2 + 2 * group + half]
                    assemble(
                        piece, weight_ref, GATHER_ORDERS[group], half, 1, group * hidden
                    )
            weight_ref.start()
        ff_forward_body(0, ins[0][...].astype(F32), ins[1], weight_ref, outs[:4])

    results = (
        far((rows, width), BF16),
        far((rows, hidden), F32),
        far((rows, hidden), BF16),
        ((rows, width), BF16),
    )
    if split:
        results += (far((width, 2 * hidden), BF16),)
    values = on_chip(body, "first_forward", (tokens, gains) + pieces, results)
    return values if split else tuple(values) + (weights,)


def second_forward(residual, own, other, gains, weights):
    rows, width = residual.shape
    hidden = weights.shape[1] // 2

    def body(ins, outs, _):
        after = ins[0][...] + (ins[1][...].astype(F32) + ins[2][...].astype(F32))
        outs[0][...] = after
        outs[5][...] = after
        ff_forward_body(3, after, ins[3], ins[4], outs[1:5])

    return on_chip(
        body,
        "second_forward",
        (residual, own, other, gains, weights),
        (
            ((rows, width), F32),
            far((rows, width), BF16),
            ((rows, hidden), F32),
            far((rows, hidden), BF16),
            ((rows, width), BF16),
            far((rows, width), F32),
        ),
        fetch=(4,),
    )


def ff_back_body(gradient, pre_ref, weight_ref, branch_ref, slope_ref):
    half = weight_ref.shape[1] // 2
    branch = (0.5 * gradient).astype(BF16)
    branch_ref[...] = branch
    grad_hidden = matmul(branch, weight_ref[:, half:])
    pre = pre_ref[...]
    grad_pre = (grad_hidden * swish_slope(pre, jax.nn.sigmoid(pre))).astype(BF16)
    slope_ref[...] = grad_pre
    return right_transposed(grad_pre, weight_ref[:, :half])


def second_back(residual, own, other, cotangent, pre, gains, weights):
    rows, width = residual.shape
    hidden = weights.shape[1] // 2

    def body(ins, outs, _):
        x_ref, own_ref, other_ref, cot_ref, pre_ref, gain_ref, weight_ref = ins
        out_ref, grad_ref, branch_ref, slope_ref, part_ref, gain_grad_ref = outs
        after = x_ref[...] + 0.5 * (own_ref[...].astype(F32) + other_ref[...].astype(F32))
        normed, factor = norm_parts(after)
        gain = gain_ref[4:5, :]
        out_ref[...] = own_half(normed * gain).astype(BF16)
        gradient, gain_grad = norm_back(cot_ref[...].astype(F32), normed, factor, gain)
        gain_grad_ref[...] = 0.5 * gain_grad
        grad_ref[...] = gradient
        part_ref[...] = ff_back_body(gradient, pre_ref, weight_ref, branch_ref, slope_ref).astype(
            BF16
        )

    return on_chip(
        body,
        "second_back",
        (residual, own, other, cotangent, pre, gains, weights),
        (
            ((rows // 2, width), BF16),
            ((rows, width), F32),
            ((rows, width), BF16),
            ((rows, hidden), BF16),
            ((rows, width), BF16),
            far((1, width), F32),
        ),
        fetch=(3, 6),
    )


def ff_weight_grads(entries, grad_pre, branch, hidden, name):
    width = entries.shape[1]
    half = hidden.shape[1]

    def body(ins, outs, _):
        outs[0][:, :half] = left_transposed(ins[0][...], ins[1][...]).astype(BF16)
        outs[0][:, half:] = left_transposed(ins[2][...], ins[3][...]).astype(BF16)

    return on_chip(
        body,
        name,
        (entries, grad_pre, branch, hidden),
        (far((width, 2 * half), BF16),),
        fetch=(0, 3),
    )[0]


def ff_weight_split(entries, grad_pre, branch, hidden, name):
    width = entries.shape[1]
    half = hidden.shape[1]

    def body(ins, outs, scratch):
        for group in range(2):
            scratch[0][...] = left_transposed(ins[2 * group][...], ins[2 * group + 1][...])
            scatter_split(
                scratch[0], outs[2 * group], outs[2 * group + 1], SCATTER_ORDERS[group], 1
            )

    halves = (((width // 2, half), F32), ((width // 2, half), BF16))
    values = on_chip(
        body,
        name,
        (entries, grad_pre, branch, hidden),
        halves + halves,
        scratch=(pltpu.VMEM((width, half), F32),),
        fetch=(0, 3),
    )
    return values[0::2], values[1::2]


def position_forward(table, weights, columns):
    def body(ins, outs, _):
        outs[0][...] = matmul(ins[0][...], ins[1][:, 3 * columns : 4 * columns]).astype(BF16)

    return on_chip(
        body, "position_forward", (table, weights), (((table.shape[0], columns), BF16),)
    )[0]


def attention_forward(tokens, own, other, gains, weights, positions, biases, heads):
    rows, width = tokens.shape
    columns = biases.shape[1]
    features = columns // heads
    scale = features ** (-0.5)

    def body(ins, outs, _):
        x_ref, own_ref, other_ref, gain_ref, weight_ref, table_ref, bias_ref = ins
        after_ref, e_ref, kept_ref, prob_ref, mix_ref, part_ref, after_far_ref = outs
        after = x_ref[...].astype(F32) + 0.5 * (
            own_ref[...].astype(F32) + other_ref[...].astype(F32)
        )
        after_ref[...] = after
        after_far_ref[...] = after
        normed, _ = norm_parts(after)
        entries = (normed * gain_ref[1:2, :]).astype(BF16)
        e_ref[...] = entries
        joined = matmul(entries, weight_ref[:, : 3 * columns])
        queries = joined[:, :columns]
        content_q = (queries + bias_ref[0:1, :]).astype(BF16)
        position_q = (queries + bias_ref[1:2, :]).astype(BF16)
        keys = joined[:, columns : 2 * columns].astype(BF16)
        values = joined[:, 2 * columns :].astype(BF16)
        kept_ref[...] = jnp.concatenate([content_q, position_q, keys, values], 1)
        mixed = []
        for head in range(heads):
            part = slice(head * features, (head + 1) * features)
            content = right_transposed(content_q[:, part], keys[:, part])
            raw = right_transposed(position_q[:, part], table_ref[:, part])
            shifted = pltpu.roll(raw, rows + 1, 1, stride=1, stride_axis=0)[:, :rows]
            scores = (content + shifted) * scale
            lifted = jnp.exp(scores - jnp.max(scores, -1, keepdims=True))
            probability = lifted / jnp.sum(lifted, -1, keepdims=True)
            prob_ref[head] = probability
            mixed.append(matmul(probability.astype(BF16), values[:, part]))
        attended = jnp.concatenate(mixed, 1).astype(BF16)
        mix_ref[...] = attended
        part_ref[...] = right_transposed(attended, weight_ref[:, 4 * columns : 5 * columns]).astype(BF16)

    return on_chip(
        body,
        "attention_forward",
        (tokens, own, other, gains, weights, positions, biases),
        (
            ((rows, width), F32),
            far((rows, width), BF16),
            far((rows, 4 * columns), BF16),
            far((heads, rows, rows), F32),
            far((rows, columns), BF16),
            ((rows, width), BF16),
            far((rows, width), F32),
        ),
    )


def attention_back(gradient, own, other, residual, gains, weights, positions, kept, heads):
    rows, width = residual.shape
    columns = positions.shape[1]
    features = columns // heads
    scale = features ** (-0.5)

    def body(ins, outs, _):
        (
            grad_ref,
            own_ref,
            other_ref,
            x_ref,
            gain_ref,
            weight_ref,
            table_ref,
            kept_ref,
            prob_ref,
        ) = ins
        total_ref, branch_ref, joined_ref, table_grad_ref, part_ref, gain_grad_ref, bias_ref = outs
        normed, factor = norm_parts(x_ref[...])
        passed, gain_grad = norm_back(
            own_ref[...].astype(F32) + other_ref[...].astype(F32), normed, factor, gain_ref[2:3, :]
        )
        gain_grad_ref[...] = 0.5 * gain_grad
        total = grad_ref[...] + passed
        total_ref[...] = total
        branch = total.astype(BF16)
        branch_ref[...] = branch
        grad_mixed = matmul(branch, weight_ref[:, 4 * columns : 5 * columns]).astype(BF16)
        line = lax.broadcasted_iota(jnp.int32, (rows, rows), 0)
        place = lax.broadcasted_iota(jnp.int32, (rows, rows), 1)
        flip = (line + place == rows - 1).astype(F32).astype(BF16)
        content_q = kept_ref[:, :columns]
        keys = kept_ref[:, 2 * columns : 3 * columns]
        values = kept_ref[:, 3 * columns :]
        flipped_q = matmul(flip, kept_ref[:, columns : 2 * columns]).astype(BF16)
        zeros = jnp.zeros((rows, rows), F32)
        from_content, from_position, to_keys, to_values, to_table = [], [], [], [], []
        for head in range(heads):
            part = slice(head * features, (head + 1) * features)
            probability = prob_ref[head]
            grad_probability = right_transposed(grad_mixed[:, part], values[:, part])
            to_values.append(left_transposed(probability.astype(BF16), grad_mixed[:, part]))
            inner = jnp.sum(probability * grad_probability, -1, keepdims=True)
            grad_scores = (probability * (grad_probability - inner)).astype(BF16) * scale
            grad_scores = grad_scores.astype(BF16)
            from_content.append(matmul(grad_scores, keys[:, part]))
            to_keys.append(left_transposed(grad_scores, content_q[:, part]))
            flipped = jnp.concatenate([matmul(flip, grad_scores), zeros], 1)
            spread = pltpu.roll(flipped, 0, 1, stride=1, stride_axis=0).astype(BF16)
            from_position.append(matmul(spread, table_ref[:, part]))
            to_table.append(left_transposed(spread, flipped_q[:, part]))
        grad_content = jnp.concatenate(from_content, 1)
        grad_position = jnp.concatenate(from_position, 1)
        high = grad_position.astype(BF16)
        low = (grad_position - high.astype(F32)).astype(BF16)
        grad_position = matmul(flip, high) + matmul(flip, low)
        bias_ref[0:1, :] = jnp.sum(grad_content, 0, keepdims=True)
        bias_ref[1:2, :] = jnp.sum(grad_position, 0, keepdims=True)
        joined = jnp.concatenate(
            [grad_content + grad_position] + to_keys + to_values, 1
        ).astype(BF16)
        joined_ref[...] = joined
        table_grad_ref[...] = jnp.concatenate(to_table, 1).astype(BF16)
        part_ref[...] = right_transposed(joined, weight_ref[:, : 3 * columns]).astype(BF16)

    return on_chip(
        body,
        "attention_back",
        (gradient, own, other, residual, gains, weights, positions) + tuple(kept),
        (
            ((rows, width), F32),
            ((rows, width), BF16),
            ((rows, 3 * columns), BF16),
            ((2 * rows, columns), BF16),
            ((rows, width), BF16),
            far((1, width), F32),
            far((2, columns), F32),
        ),
        fetch=(0, 3, 7, 8),
    )


def mixed_assemble(pairs, table, width):
    columns = pairs[0][0].shape[1]

    def body(ins, outs, _):
        for group in range(2):
            for half in range(2):
                assemble(
                    ins[2 * group + half],
                    outs[0],
                    GATHER_ORDERS[group],
                    half,
                    4,
                    4 * group * columns,
                )
        outs[1][...] = matmul(ins[4][...], outs[0][:, 3 * columns : 4 * columns]).astype(BF16)

    return on_chip(
        body,
        "mixed_assemble",
        pairs[0] + pairs[1] + (table,),
        (((width, 8 * columns), BF16), ((table.shape[0], columns), BF16)),
    )


def mixed_weight_grads(attention_parts, conv_parts, split):
    entries, joined, table, table_grad, branch, attended = attention_parts
    conv_entries, conv_joined, conv_branch, activated = conv_parts
    width = entries.shape[1]
    columns = attended.shape[1]

    def whole(ins, target_ref):
        target_ref[:, : 3 * columns] = left_transposed(ins[0][...], ins[1][...])
        target_ref[:, 3 * columns : 4 * columns] = left_transposed(ins[2][...], ins[3][...])
        target_ref[:, 4 * columns : 5 * columns] = left_transposed(ins[4][...], ins[5][...])
        target_ref[:, 5 * columns : 7 * columns] = left_transposed(ins[6][...], ins[7][...])
        target_ref[:, 7 * columns :] = left_transposed(ins[8][...], ins[9][...])

    def body(ins, outs, scratch):
        if not split:
            whole(ins, outs[0])
            return
        whole(ins, scratch[0])
        for group in range(2):
            part = scratch[0].at[:, 4 * group * columns : 4 * (group + 1) * columns]
            scatter_split(part, outs[2 * group], outs[2 * group + 1], SCATTER_ORDERS[group], 4)

    operands = (
        entries,
        joined,
        table,
        table_grad,
        branch,
        attended,
        conv_entries,
        conv_joined,
        conv_branch,
        activated,
    )
    fetch = (0, 5, 6, 7, 8, 9)
    if not split:
        results = (((width, 8 * columns), F32),)
        return on_chip(body, "mixed_weight_grads", operands, results, fetch=fetch)[0]
    halves = (far((2 * width, columns), F32), ((2 * width, columns), BF16))
    values = on_chip(
        body,
        "mixed_weight_grads",
        operands,
        halves + halves,
        scratch=(pltpu.VMEM((width, 8 * columns), F32),),
        fetch=fetch,
    )
    return values[0::2], values[1::2]


PAD = 16


def conv_forward(residual, own, other, gains, weights, depth_kernel):
    rows, width = residual.shape
    taps, columns = depth_kernel.shape
    half_taps = (taps - 1) // 2

    def body(ins, outs, scratch):
        x_ref, own_ref, other_ref, gain_ref, weight_ref, tap_ref = ins
        after_ref, c_ref, value_ref, gate_ref, conv_ref, sums_ref, after_far_ref, conv_far_ref = outs
        padded = scratch[0]
        after = x_ref[...] + (own_ref[...].astype(F32) + other_ref[...].astype(F32))
        after_ref[...] = after
        after_far_ref[...] = after
        normed, _ = norm_parts(after)
        entries = (normed * gain_ref[2:3, :]).astype(BF16)
        c_ref[...] = entries
        joined = matmul(entries, weight_ref[:, 5 * columns : 7 * columns])
        value = joined[:, :columns]
        gate = jax.nn.sigmoid(joined[:, columns:])
        value_ref[...] = value
        gate_ref[...] = gate
        padded[:PAD, :] = jnp.zeros((PAD, columns), F32)
        padded[PAD + rows :, :] = jnp.zeros((PAD, columns), F32)
        padded[PAD : PAD + rows, :] = value * gate
        total = jnp.zeros((rows, columns), F32)
        for tap in range(taps):
            start = PAD - half_taps + tap
            total = total + tap_ref[tap : tap + 1, :] * padded[start : start + rows, :]
        conv_ref[...] = total
        conv_far_ref[...] = total
        sums_ref[0:1, :] = jnp.sum(total, 0, keepdims=True)
        sums_ref[1:2, :] = jnp.sum(total * total, 0, keepdims=True)

    local = far((rows, columns), F32)
    return on_chip(
        body,
        "conv_forward",
        (residual, own, other, gains, weights, depth_kernel),
        (
            ((rows, width), F32),
            far((rows, width), BF16),
            local,
            local,
            ((rows, columns), F32),
            ((2, columns), F32),
            far((rows, width), F32),
            local,
        ),
        scratch=(pltpu.VMEM((rows + 2 * PAD, columns), F32),),
    )


def batch_norm(conv_ref, sums_ref, batch_ref, token_count):
    column_mean = sums_ref[0:1, :] / token_count
    inverse = lax.rsqrt(sums_ref[1:2, :] / token_count - column_mean * column_mean + EPSILON)
    standard = (conv_ref[...] - column_mean) * inverse
    return standard, inverse, standard * batch_ref[0:1, :] + batch_ref[1:2, :]


def norm_forward(convolved, sums, batch, weights, token_count):
    rows, columns = convolved.shape
    width = weights.shape[0]

    def body(ins, outs, _):
        conv_ref, sums_ref, batch_ref, weight_ref = ins
        _, _, shifted = batch_norm(conv_ref, sums_ref, batch_ref, token_count)
        activated = (shifted * jax.nn.sigmoid(shifted)).astype(BF16)
        outs[0][...] = activated
        outs[1][...] = right_transposed(activated, weight_ref[:, 7 * columns :]).astype(BF16)

    return on_chip(
        body,
        "norm_forward",
        (convolved, sums, batch, weights),
        (far((rows, columns), BF16), ((rows, width), BF16)),
    )


def norm_backward(gradient, own, other, residual, gains, weights, convolved, sums, batch, count):
    rows, columns = convolved.shape
    width = weights.shape[0]

    def body(ins, outs, _):
        grad_ref, own_ref, other_ref, x_ref, gain_ref, weight_ref, conv_ref, sums_ref, batch_ref = (
            ins
        )
        total_ref, branch_ref, shifted_ref, grad_sums_ref, gain_grad_ref = outs
        normed, factor = norm_parts(x_ref[...])
        passed, gain_grad = norm_back(
            own_ref[...].astype(F32) + other_ref[...].astype(F32), normed, factor, gain_ref[3:4, :]
        )
        gain_grad_ref[...] = 0.5 * gain_grad
        total = grad_ref[...] + passed
        total_ref[...] = total
        branch = total.astype(BF16)
        branch_ref[...] = branch
        standard, _, shifted = batch_norm(conv_ref, sums_ref, batch_ref, count)
        grad_shifted = matmul(branch, weight_ref[:, 7 * columns :]) * swish_slope(
            shifted, jax.nn.sigmoid(shifted)
        )
        shifted_ref[...] = grad_shifted
        grad_sums_ref[0:1, :] = jnp.sum(grad_shifted, 0, keepdims=True)
        grad_sums_ref[1:2, :] = jnp.sum(grad_shifted * standard, 0, keepdims=True)

    return on_chip(
        body,
        "norm_backward",
        (gradient, own, other, residual, gains, weights, convolved, sums, batch),
        (
            far((rows, width), F32),
            far((rows, width), BF16),
            ((rows, columns), F32),
            ((2, columns), F32),
            far((1, width), F32),
        ),
        fetch=(3, 6),
    )


def conv_backward(
    grad_shifted, grad_sums, convolved, sums, batch, value, gate, weights, depth_kernel, count
):
    rows, columns = convolved.shape
    width = weights.shape[0]
    taps = depth_kernel.shape[0]
    half_taps = (taps - 1) // 2

    def body(ins, outs, scratch):
        (
            shifted_ref,
            grad_sums_ref,
            conv_ref,
            sums_ref,
            batch_ref,
            value_ref,
            gate_ref,
            weight_ref,
            tap_ref,
        ) = ins
        grad_conv_ref, joined_ref, part_ref = outs
        padded = scratch[0]
        standard, inverse, _ = batch_norm(conv_ref, sums_ref, batch_ref, count)
        grad_conv = (inverse * batch_ref[0:1, :]) * (
            shifted_ref[...]
            - grad_sums_ref[0:1, :] / count
            - standard * (grad_sums_ref[1:2, :] / count)
        )
        grad_conv_ref[...] = grad_conv
        padded[:PAD, :] = jnp.zeros((PAD, columns), F32)
        padded[PAD + rows :, :] = jnp.zeros((PAD, columns), F32)
        padded[PAD : PAD + rows, :] = grad_conv
        total = jnp.zeros((rows, columns), F32)
        for tap in range(taps):
            start = PAD + half_taps - tap
            total = total + tap_ref[tap : tap + 1, :] * padded[start : start + rows, :]
        gate_sigma = gate_ref[...]
        grad_value = total * gate_sigma
        joined = jnp.concatenate(
            [grad_value, grad_value * value_ref[...] * (1.0 - gate_sigma)], 1
        ).astype(BF16)
        joined_ref[...] = joined
        part_ref[...] = right_transposed(joined, weight_ref[:, 5 * columns : 7 * columns]).astype(BF16)

    return on_chip(
        body,
        "conv_backward",
        (grad_shifted, grad_sums, convolved, sums, batch, value, gate, weights, depth_kernel),
        (((rows, columns), F32), far((rows, 2 * columns), BF16), ((rows, width), BF16)),
        scratch=(pltpu.VMEM((rows + 2 * PAD, columns), F32),),
        fetch=(2, 5, 6),
    )


def tap_gradients(value, gate, grad_conv, taps):
    rows, columns = grad_conv.shape
    half_taps = (taps - 1) // 2

    def body(ins, outs, scratch):
        value_ref, gate_ref, grad_ref = ins
        padded = scratch[0]
        padded[:PAD, :] = jnp.zeros((PAD, columns), F32)
        padded[PAD + rows :, :] = jnp.zeros((PAD, columns), F32)
        padded[PAD : PAD + rows, :] = value_ref[...] * gate_ref[...]
        grad_conv_value = grad_ref[...]
        for tap in range(taps):
            start = PAD - half_taps + tap
            outs[0][tap : tap + 1, :] = jnp.sum(
                padded[start : start + rows, :] * grad_conv_value, 0, keepdims=True
            )

    return on_chip(
        body,
        "tap_gradients",
        (value, gate, grad_conv),
        (far((taps, columns), F32),),
        scratch=(pltpu.VMEM((rows + 2 * PAD, columns), F32),),
        flops=10_000_000,
        fetch=(0, 1),
    )[0]


def first_back(gradient, own, other, residual, pre, gains, weights):
    rows, width = residual.shape
    hidden = weights.shape[1] // 2

    def body(ins, outs, _):
        grad_ref, own_ref, other_ref, x_ref, pre_ref, gain_ref, weight_ref = ins
        total_ref, branch_ref, slope_ref, keep_ref, send_ref, gain_grad_ref = outs
        normed, factor = norm_parts(x_ref[...])
        passed, gain_grad = norm_back(
            own_ref[...].astype(F32) + other_ref[...].astype(F32), normed, factor, gain_ref[1:2, :]
        )
        gain_grad_ref[...] = 0.5 * gain_grad
        total = grad_ref[...] + passed
        total_ref[...] = own_half(total)
        part = ff_back_body(total, pre_ref, weight_ref, branch_ref, slope_ref)
        keep_ref[...] = own_half(part)
        send_ref[...] = other_half(part).astype(BF16)

    return on_chip(
        body,
        "first_back",
        (gradient, own, other, residual, pre, gains, weights),
        (
            ((rows // 2, width), F32),
            ((rows, width), BF16),
            ((rows, hidden), BF16),
            ((rows // 2, width), F32),
            ((rows // 2, width), BF16),
            far((1, width), F32),
        ),
        fetch=(3, 4, 6),
    )


def input_back(gradient, own, other, tokens, gains, gain_grads, tap_grads, bias_grads):
    rows, width = tokens.shape
    taps, columns = tap_grads.shape
    upper = (taps + 1) // 2
    packed_rows = -(-(6 + upper) // 8) * 8

    def body(ins, outs, _):
        grad_ref, own_ref, other_ref, x_ref, gain_ref = ins[:5]
        tap_ref, bias_ref = ins[9:]
        packed = outs[1]
        normed, factor = norm_parts(x_ref[...].astype(F32))
        passed, gain_grad = norm_back(
            own_ref[...].astype(F32) + other_ref[...].astype(F32), normed, factor, gain_ref[0:1, :]
        )
        outs[0][...] = grad_ref[...] + passed
        packed[...] = jnp.zeros((packed_rows, 2 * columns), F32)
        packed[0:1, :] = gain_grad
        for place in range(4):
            packed[place + 1 : place + 2, :] = ins[5 + place][...]
        packed[5:6, :columns] = bias_ref[0:1, :]
        packed[5:6, columns:] = bias_ref[1:2, :]
        packed[6 : 6 + upper, :columns] = tap_ref[:upper, :]
        packed[6 : 6 + taps - upper, columns:] = tap_ref[upper:, :]

    return on_chip(
        body,
        "input_back",
        (gradient, own, other, tokens, gains) + tuple(gain_grads) + (tap_grads, bias_grads),
        (((rows, width), F32), ((packed_rows, 2 * columns), F32)),
        flops=1_000_000,
        fetch=(5, 6, 7, 8, 9, 10),
    )


def reduce_plain(grads):
    return lax.psum_scatter(grads.astype(BF16), "dp", scatter_dimension=0, tiled=True).astype(F32)


def stacked_columns(pieces, count):
    width = pieces.shape[1] // count
    return jnp.stack([pieces[:, index * width : (index + 1) * width] for index in range(count)])


def unstacked(stacked):
    return [stacked[index] for index in range(stacked.shape[0])]


def body(
    tokens,
    norm_gains,
    first_in,
    first_out,
    attention_in,
    attention_out,
    head_biases,
    gated_in,
    pointwise_out,
    depth_kernel,
    batch_scale,
    batch_shift,
    second_in,
    second_out,
    cotangent,
):
    local_heads = HEAD_TOTAL // lax.axis_size("tensor")
    length = tokens.shape[0] * lax.axis_size("tensor")
    token_count = float(length * lax.axis_size("dp"))
    columns = attention_out.shape[1]
    hidden = first_in.shape[1]
    width = tokens.shape[1]
    table = sinusoid(length, width).astype(BF16)
    batch = jnp.stack([batch_scale, batch_shift])
    split = doubling()

    def gather(pieces):
        return lax.all_gather(jnp.concatenate(pieces, 1), "dp", axis=0, tiled=True)

    tokens_all = both_halves(tokens)
    cotangent_all = both_halves(cotangent)

    if split:
        batch_one = (first_in, first_out)
        batch_two = (
            attention_in.reshape(-1, columns),
            jnp.concatenate([attention_out, gated_in.reshape(-1, columns), pointwise_out], 0),
        )
        batch_one = gather_stage(batch_one, 0)
        batch_one = gather_stage(tie(batch_one, tokens_all), 1)
        batch_two = gather_stage(tie(batch_two, batch_one), 0)
        batch_one = gather_stage(batch_one, 2)
        second_pieces = tie((second_in, second_out), batch_one)
        batch_two = gather_stage(tie(batch_two, batch_one), 1)
        batch_one = gather_last(batch_one)
        batch_two = gather_stage(tie(batch_two, batch_one), 2)
        second_weights = gather(second_pieces)
    else:
        batch_one = gather([first_in, first_out])
        mixed_weights = gather(
            unstacked(attention_in) + [attention_out] + unstacked(gated_in) + [pointwise_out]
        )
        second_weights = gather([second_in, second_out])
        positions = position_forward(table, mixed_weights, columns)

    entries1, pre1, hidden1, part1, first_weights = first_forward(
        tokens_all, norm_gains, batch_one
    )
    other1 = swap(part1)
    if split:
        batch_two = gather_last(tie(batch_two, part1))
        mixed_weights, positions = mixed_assemble(batch_two, table, width)
    after1, entries2, kept, prob, attended, part2, after1_far = attention_forward(
        tokens_all, part1, other1, norm_gains, mixed_weights, positions, head_biases, local_heads
    )
    other2 = swap(part2)
    after2, entries3, value_pre, gate, convolved, sums, after2_far, conv_far = conv_forward(
        after1, part2, other2, norm_gains, mixed_weights, depth_kernel
    )
    sums = sum_over(sums, "dp")
    activated, part3 = norm_forward(convolved, sums, batch, mixed_weights, token_count)
    other3 = swap(part3)
    after3, entries4, pre4, hidden4, part4, after3_far = second_forward(
        after2, part3, other3, norm_gains, second_weights
    )
    other4 = swap(part4)
    block_out, grad4, branch4, slope4, part5, gain5 = second_back(
        after3, part4, other4, cotangent_all, pre4, norm_gains, second_weights
    )
    other5 = swap(part5)
    grads_second = ff_weight_grads(entries4, slope4, branch4, hidden4, "second_weight_grads")
    other5 = tie(other5, grads_second)
    reduced_second = reduce_plain(grads_second)
    grad3, branch3, grad_shifted, grad_sums, gain4 = norm_backward(
        grad4,
        part5,
        other5,
        after3_far,
        norm_gains,
        mixed_weights,
        conv_far,
        sums,
        batch,
        token_count,
    )
    grad_sums = sum_over(grad_sums, "dp")
    grad_conv, joined3, part6 = conv_backward(
        grad_shifted,
        grad_sums,
        conv_far,
        sums,
        batch,
        value_pre,
        gate,
        mixed_weights,
        depth_kernel,
        token_count,
    )
    other6 = swap(part6)
    tap_grads = tap_gradients(value_pre, gate, grad_conv, depth_kernel.shape[0])
    grad2, branch2, joined2, table_grad, part7, gain3, bias_grads = attention_back(
        grad3,
        part6,
        other6,
        after2_far,
        norm_gains,
        mixed_weights,
        positions,
        (kept, prob),
        local_heads,
    )
    other7 = swap(part7)
    mixed_grads = mixed_weight_grads(
        (entries2, joined2, table, table_grad, branch2, attended),
        (entries3, joined3, branch3, activated),
        split,
    )
    grad1, branch1, slope1, keep8, send8, gain2 = first_back(
        grad2, part7, other7, after1_far, pre1, norm_gains, first_weights
    )
    if split:
        first_grads = ff_weight_split(entries1, slope1, branch1, hidden1, "first_weight_grads")
        for stage in range(4):
            mixed_grads = scatter_stage(
                *mixed_grads, stage, "mixed_sum", (0, 1) if stage == 0 else ()
            )
            first_grads = scatter_stage(*first_grads, stage, "first_sum")
        (mixed_a, mixed_b), (reduced_in, reduced_out) = mixed_grads[0], first_grads[0]
        rows = mixed_a.shape[0] // 4
        reduced_attention = mixed_a.reshape(4, rows, columns)
        reduced_mixing = mixed_b[:rows]
        reduced_gated = mixed_b[rows : 3 * rows].reshape(2, rows, columns)
        reduced_pointwise = mixed_b[3 * rows :]
    else:
        first_grads = reduce_plain(
            ff_weight_grads(entries1, slope1, branch1, hidden1, "first_weight_grads")
        )
        reduced_in, reduced_out = first_grads[:, :hidden], first_grads[:, hidden:]
        mixed = reduce_plain(mixed_grads)
        reduced_attention = stacked_columns(mixed[:, : 4 * columns], 4)
        reduced_mixing = mixed[:, 4 * columns : 5 * columns]
        reduced_gated = stacked_columns(mixed[:, 5 * columns : 7 * columns], 2)
        reduced_pointwise = mixed[:, 7 * columns :]
    other8 = swap(send8)
    grad_start, packed = input_back(
        grad1,
        keep8,
        other8,
        tokens,
        norm_gains,
        (gain2, gain3, gain4, gain5),
        tap_grads,
        bias_grads,
    )
    packed = sum_over(packed, "dp")
    gain_total = sum_over(packed[:5], "tensor")
    bias_total = packed[5].reshape(bias_grads.shape)
    taps = tap_grads.shape[0]
    upper = (taps + 1) // 2
    tap_total = jnp.concatenate(
        [packed[6 : 6 + upper, :columns], packed[6 : 6 + taps - upper, columns:]], 0
    )
    return (
        block_out,
        grad_start,
        gain_total,
        reduced_in,
        reduced_out,
        reduced_attention,
        reduced_mixing,
        bias_total,
        reduced_gated,
        reduced_pointwise,
        tap_total,
        grad_sums[1],
        grad_sums[0],
        reduced_second[:, :hidden],
        reduced_second[:, hidden:],
    )


def solution(mesh):
    placed = (
        P(("dp", "tensor"), None),
        P(),
        P("dp", "tensor"),
        P("dp", "tensor"),
        P(None, "dp", "tensor"),
        P("dp", "tensor"),
        P(None, "tensor"),
        P(None, "dp", "tensor"),
        P("dp", "tensor"),
        P(None, "tensor"),
        P("tensor"),
        P("tensor"),
        P("dp", "tensor"),
        P("dp", "tensor"),
        P(("dp", "tensor"), None),
    )
    return jax.shard_map(
        body,
        mesh=mesh,
        in_specs=placed,
        out_specs=(
            P(("dp", "tensor"), None),
            P(("dp", "tensor"), None),
            P(),
            P("dp", "tensor"),
            P("dp", "tensor"),
            P(None, "dp", "tensor"),
            P("dp", "tensor"),
            P(None, "tensor"),
            P(None, "dp", "tensor"),
            P("dp", "tensor"),
            P(None, "tensor"),
            P("tensor"),
            P("tensor"),
            P("dp", "tensor"),
            P("dp", "tensor"),
        ),
        check_vma=False,
    )
```

```python
import math

import jax
import jax.numpy as jnp
from jax import lax
from jax.experimental import pallas as pl
from jax.experimental.pallas import tpu as pltpu
from jax.sharding import PartitionSpec as P

HEAD_TOTAL = 8
EPSILON = 1e-05
BF16 = jnp.bfloat16
F32 = jnp.float32


def matmul(left_side, right_side):
    return jnp.dot(left_side, right_side, preferred_element_type=F32)


def right_transposed(left_side, right_side):
    return lax.dot_general(
        left_side, right_side, (((1,), (1,)), ((), ())), preferred_element_type=F32
    )


def left_transposed(left_side, right_side):
    return lax.dot_general(
        left_side, right_side, (((0,), (0,)), ((), ())), preferred_element_type=F32
    )


def swish_slope(pre_value, gate_sigma):
    return gate_sigma * (1.0 + pre_value * (1.0 - gate_sigma))


def norm_parts(residual):
    centred = residual - jnp.mean(residual, -1, keepdims=True)
    factor = lax.rsqrt(jnp.mean(centred * centred, -1, keepdims=True) + EPSILON)
    return centred * factor, factor


def norm_back(gradient, normed, factor, norm_gain):
    scaled = gradient * norm_gain
    inner_sum = (
        scaled
        - jnp.mean(scaled, -1, keepdims=True)
        - normed * jnp.mean(scaled * normed, -1, keepdims=True)
    )
    return factor * inner_sum, jnp.sum(gradient * normed, 0, keepdims=True)


def sinusoid(length, features):
    offsets = jnp.arange(2 * length, dtype=F32) - (length - 1)
    half_width = features // 2
    frequency = jnp.exp(jnp.arange(half_width, dtype=F32) * (-math.log(10000.0) / half_width))
    angles = offsets[:, None] * frequency[None, :]
    table = jnp.concatenate([jnp.sin(angles), jnp.cos(angles)], 1)
    return jnp.where(offsets[:, None] < length, table, 0.0)


def on_chip(function, name, operands, results, scratch=(), flops=300_000_000):
    count = len(operands)
    total = count + len(results)

    def kernel(*refs):
        function(refs[:count], refs[count:total], refs[total:])

    moved = sum(value.size * value.dtype.itemsize for value in operands)
    moved += sum(math.prod(shape) * jnp.dtype(kind).itemsize for shape, kind in results)
    return pl.pallas_call(
        kernel,
        out_shape=[jax.ShapeDtypeStruct(shape, kind) for shape, kind in results],
        in_specs=[pl.BlockSpec(memory_space=pltpu.VMEM)] * count,
        out_specs=[pl.BlockSpec(memory_space=pltpu.VMEM)] * len(results),
        scratch_shapes=list(scratch),
        compiler_params=pltpu.CompilerParams(vmem_limit_bytes=24 * 1024 * 1024),
        cost_estimate=pl.CostEstimate(flops=flops, bytes_accessed=moved, transcendentals=0),
        name=name,
    )(*operands)


def swap(value):
    return lax.ppermute(value, "tensor", [(0, 1), (1, 0)])


def both_halves(own):
    other = swap(own)
    first = lax.axis_index("tensor") == 0
    return jnp.concatenate([jnp.where(first, own, other), jnp.where(first, other, own)], 0)


def own_half(value):
    half = value.shape[0] // 2
    return jnp.where(lax.axis_index("tensor") == 0, value[:half], value[half:])


def other_half(value):
    half = value.shape[0] // 2
    return jnp.where(lax.axis_index("tensor") == 0, value[half:], value[:half])


def shift(value, axis, mask):
    return lax.ppermute(value, axis, [(k, k ^ mask) for k in range(lax.axis_size(axis))])


def sum_over(value, axis):
    size = lax.axis_size(axis)
    if size & (size - 1):
        return lax.psum(value, axis)
    step = 1
    while step < size:
        if step >= 4 and step * 4 <= size:
            near, far, both = (shift(value, axis, step * times) for times in (1, 2, 3))
            value = (value + near) + (far + both)
            step *= 4
        else:
            value = value + shift(value, axis, step)
            step *= 2
    return value


GATHER_ORDERS = ((8, 4, 2, 1), (8, 2, 4, 1))
SCATTER_ORDERS = ((1, 2, 4, 8), (1, 4, 2, 8))


def doubling():
    return lax.axis_size("dp") == 16


def distances(order):
    blocks = [0]
    for mask in order:
        blocks = blocks + [block ^ mask for block in blocks]
    return blocks


def halving(order):
    return distances(order[::-1])


def gather_send(pair, stage):
    return tuple(shift(value, "dp", order[stage]) for value, order in zip(pair, GATHER_ORDERS))


def gather_join(pair, arrived):
    def body(ins, outs, _):
        for group in range(2):
            rows = ins[group].shape[0]
            outs[group][:rows, :] = ins[group][...]
            outs[group][rows:, :] = ins[2 + group][...]

    results = tuple(((2 * value.shape[0], value.shape[1]), value.dtype) for value in pair)
    return tuple(on_chip(body, "gather_join", tuple(pair) + arrived, results, flops=1_000))


def gather_last(pair):
    return tuple((value, shift(value, "dp", 1)) for value in pair)


def tie(values, *others):
    return lax.optimization_barrier((values, others))[0]


def assemble(ref, target_ref, order, half, matrices, first_column):
    device = lax.axis_index("dp")
    blocks = distances(order)
    count = len(blocks) // 2
    rows = target_ref.shape[0] // len(blocks)
    columns = ref.shape[1]
    for place in range(count):
        owner = device ^ blocks[half * count + place]
        target = pl.ds(pl.multiple_of(owner * rows, rows), rows)
        for matrix in range(matrices):
            start = (place * matrices + matrix) * rows
            left = first_column + matrix * columns
            target_ref[target, left : left + columns] = ref[start : start + rows, :]


def scatter_split(total_ref, keep_ref, send_ref, order, matrices):
    device = lax.axis_index("dp")
    blocks = halving(order)
    count = len(blocks) // 2
    rows = total_ref.shape[0] // len(blocks)
    columns = keep_ref.shape[1]
    for place, block in enumerate(blocks):
        source = pl.ds(pl.multiple_of((device ^ block) * rows, rows), rows)
        for matrix in range(matrices):
            piece = total_ref[source, matrix * columns : (matrix + 1) * columns]
            start = ((place % count) * matrices + matrix) * rows
            if place < count:
                keep_ref[start : start + rows, :] = piece
            else:
                send_ref[start : start + rows, :] = piece.astype(BF16)


def scatter_send(sends, stage):
    return tuple(shift(send, "dp", order[stage]) for send, order in zip(sends, SCATTER_ORDERS))


def scatter_add(keeps, arrived, stage, name):
    groups = len(keeps)
    last = stage == len(SCATTER_ORDERS[0]) - 1
    results = []
    for keep in keeps:
        rows, columns = keep.shape
        if last:
            results.append(((rows, columns), F32))
        else:
            results.append(((rows // 2, columns), F32))
            results.append(((rows // 2, columns), BF16))

    def body(ins, outs, _):
        for group in range(groups):
            total = ins[group][...] + ins[groups + group][...].astype(F32)
            if last:
                outs[group][...] = total
            else:
                half = total.shape[0] // 2
                outs[2 * group][...] = total[:half]
                outs[2 * group + 1][...] = total[half:].astype(BF16)

    values = on_chip(body, name, tuple(keeps) + tuple(arrived), tuple(results), flops=1_000)
    if last:
        return values, ()
    return values[0::2], values[1::2]


def entries_of(residual, gain):
    return (norm_parts(residual)[0] * gain).astype(BF16)


def ff_forward_body(entries, weight_ref, part_ref):
    half = weight_ref.shape[1] // 2
    pre = matmul(entries, weight_ref[:, :half])
    hidden = (pre * jax.nn.sigmoid(pre)).astype(BF16)
    part_ref[...] = right_transposed(hidden, weight_ref[:, half:]).astype(BF16)
    return pre


def both_parts(own_ref, other_ref):
    return own_ref[...].astype(F32) + other_ref[...].astype(F32)


def first_forward(tokens, gains, weights):
    rows, width = tokens.shape
    split = isinstance(weights, tuple)
    pieces = weights[0] + weights[1] if split else (weights,)
    hidden = pieces[0].shape[1] if split else weights.shape[1] // 2

    def body(ins, outs, _):
        weight_ref = ins[2]
        if split:
            weight_ref = outs[2]
            for group in range(2):
                for half in range(2):
                    piece = ins[2 + 2 * group + half]
                    assemble(piece, weight_ref, GATHER_ORDERS[group], half, 1, group * hidden)
        entries = entries_of(ins[0][...].astype(F32), ins[1][0:1, :])
        outs[0][...] = ff_forward_body(entries, weight_ref, outs[1])

    results = (((rows, hidden), F32), ((rows, width), BF16))
    if split:
        results += (((width, 2 * hidden), BF16),)
    values = on_chip(body, "first_forward", (tokens, gains) + pieces, results)
    return values if split else tuple(values) + (weights,)


def ff_back_body(gradient, pre, weight_ref, grads_ref):
    width = gradient.shape[1]
    half = weight_ref.shape[1] // 2
    branch = (0.5 * gradient).astype(BF16)
    grads_ref[:, :width] = branch
    grad_hidden = matmul(branch, weight_ref[:, half:])
    sigma = jax.nn.sigmoid(pre)
    grad_pre = (grad_hidden * swish_slope(pre, sigma)).astype(BF16)
    grads_ref[:, width : width + half] = grad_pre
    grads_ref[:, width + half : width + 2 * half] = (pre * sigma).astype(BF16)
    return right_transposed(grad_pre, weight_ref[:, :half])


def second_weight_grads(rows_kept, width):
    half = (rows_kept.shape[1] - 2 * width) // 2

    def body(ins, outs, _):
        rows_ref = ins[0]
        outs[0][:, :half] = left_transposed(
            rows_ref[:, width : 2 * width], rows_ref[:, 2 * width : 2 * width + half]
        ).astype(BF16)
        outs[0][:, half:] = left_transposed(
            rows_ref[:, :width], rows_ref[:, 2 * width + half :]
        ).astype(BF16)

    return on_chip(body, "second_weight_grads", (rows_kept,), (((width, 2 * half), BF16),))[0]


def ff_weight_grads(grads, residual, gains, row, name):
    width = gains.shape[1]
    half = (grads.shape[1] - width) // 2

    def body(ins, outs, _):
        grads_ref, x_ref, gain_ref = ins
        entries = entries_of(x_ref[:, :width].astype(F32), gain_ref[row : row + 1, :])
        outs[0][:, :half] = left_transposed(entries, grads_ref[:, width : width + half]).astype(
            BF16
        )
        outs[0][:, half:] = left_transposed(
            grads_ref[:, :width], grads_ref[:, width + half :]
        ).astype(BF16)

    return on_chip(body, name, (grads, residual, gains), (((width, 2 * half), BF16),))[0]


def ff_weight_split(grads, residual, gains, row, name):
    width = gains.shape[1]
    half = (grads.shape[1] - width) // 2

    def body(ins, outs, scratch):
        grads_ref, x_ref, gain_ref = ins
        entries = entries_of(x_ref[:, :width].astype(F32), gain_ref[row : row + 1, :])
        scratch[0][...] = left_transposed(entries, grads_ref[:, width : width + half])
        scatter_split(scratch[0], outs[0], outs[1], SCATTER_ORDERS[0], 1)
        scratch[0][...] = left_transposed(grads_ref[:, :width], grads_ref[:, width + half :])
        scatter_split(scratch[0], outs[2], outs[3], SCATTER_ORDERS[1], 1)

    halves = (((width // 2, half), F32), ((width // 2, half), BF16))
    values = on_chip(
        body,
        name,
        (grads, residual, gains),
        halves + halves,
        scratch=(pltpu.VMEM((width, half), F32),),
    )
    return values[0::2], values[1::2]


def kept_residual(kept_ref, width):
    return kept_ref[:, :width].astype(F32) + kept_ref[:, width : 2 * width].astype(F32)


def position_forward(table, weights, columns):
    def body(ins, outs, _):
        outs[0][...] = matmul(ins[0][...], ins[1][:, 3 * columns : 4 * columns]).astype(BF16)

    return on_chip(
        body, "position_forward", (table, weights), (((table.shape[0], columns), BF16),)
    )[0]


def attention_forward(tokens, own, other, gains, weights, positions, biases, heads):
    rows, width = tokens.shape
    columns = biases.shape[1]
    features = columns // heads
    scale = features ** (-0.5)
    start = 2 * width

    def body(ins, outs, _):
        x_ref, own_ref, other_ref, gain_ref, weight_ref, table_ref, bias_ref = ins
        kept_ref, part_ref = outs
        after = x_ref[...].astype(F32) + 0.5 * both_parts(own_ref, other_ref)
        high = after.astype(BF16)
        kept_ref[:, :width] = high
        kept_ref[:, width : 2 * width] = (after - high.astype(F32)).astype(BF16)
        entries = entries_of(after, gain_ref[1:2, :])
        joined = matmul(entries, weight_ref[:, : 3 * columns])
        queries = joined[:, :columns]
        content_q = (queries + bias_ref[0:1, :]).astype(BF16)
        position_q = (queries + bias_ref[1:2, :]).astype(BF16)
        keys = joined[:, columns : 2 * columns].astype(BF16)
        values = joined[:, 2 * columns :].astype(BF16)
        kept_ref[:, start : start + columns] = content_q
        kept_ref[:, start + columns : start + 2 * columns] = position_q
        kept_ref[:, start + 2 * columns : start + 3 * columns] = keys
        kept_ref[:, start + 3 * columns : start + 4 * columns] = values
        mixed = []
        for head in range(heads):
            part = slice(head * features, (head + 1) * features)
            content = right_transposed(content_q[:, part], keys[:, part])
            raw = right_transposed(position_q[:, part], table_ref[:, part])
            shifted = pltpu.roll(raw, rows + 1, 1, stride=1, stride_axis=0)[:, :rows]
            scores = (content + shifted) * scale
            lifted = jnp.exp(scores - jnp.max(scores, -1, keepdims=True))
            probability = (lifted / jnp.sum(lifted, -1, keepdims=True)).astype(BF16)
            place = start + 5 * columns + head * rows
            kept_ref[:, place : place + rows] = probability
            mixed.append(matmul(probability, values[:, part]))
        attended = jnp.concatenate(mixed, 1).astype(BF16)
        kept_ref[:, start + 4 * columns : start + 5 * columns] = attended
        part_ref[...] = right_transposed(
            attended, weight_ref[:, 4 * columns : 5 * columns]
        ).astype(BF16)

    return on_chip(
        body,
        "attention_forward",
        (tokens, own, other, gains, weights, positions, biases),
        (((rows, start + 5 * columns + heads * rows), BF16), ((rows, width), BF16)),
    )


def attention_back(norm_grads, own, other, conv_kept, gains, weights, positions, kept, heads):
    rows, width = own.shape
    columns = positions.shape[1]
    features = columns // heads
    scale = features ** (-0.5)
    start = 2 * width

    def body(ins, outs, _):
        grad_ref, own_ref, other_ref, x_ref, gain_ref, weight_ref, table_ref, kept_ref = ins
        total_ref, joined_ref, table_grad_ref, part_ref, gain_grad_ref, bias_ref = outs
        normed, factor = norm_parts(x_ref[:, :width])
        passed, gain_grad = norm_back(
            both_parts(own_ref, other_ref), normed, factor, gain_ref[2:3, :]
        )
        gain_grad_ref[...] = 0.5 * gain_grad
        total = grad_ref[:, :width] + passed
        total_ref[...] = total
        grad_mixed = matmul(
            total.astype(BF16), weight_ref[:, 4 * columns : 5 * columns]
        ).astype(BF16)
        line = lax.broadcasted_iota(jnp.int32, (rows, rows), 0)
        place = lax.broadcasted_iota(jnp.int32, (rows, rows), 1)
        flip = (line + place == rows - 1).astype(F32).astype(BF16)
        content_q = kept_ref[:, start : start + columns]
        flipped_q = matmul(flip, kept_ref[:, start + columns : start + 2 * columns]).astype(BF16)
        keys = kept_ref[:, start + 2 * columns : start + 3 * columns]
        values = kept_ref[:, start + 3 * columns : start + 4 * columns]
        zeros = jnp.zeros((rows, rows), F32)
        from_content, from_position, to_keys, to_values, to_table = [], [], [], [], []
        for head in range(heads):
            part = slice(head * features, (head + 1) * features)
            left = start + 5 * columns + head * rows
            rounded = kept_ref[:, left : left + rows]
            probability = rounded.astype(F32)
            grad_probability = right_transposed(grad_mixed[:, part], values[:, part])
            to_values.append(left_transposed(rounded, grad_mixed[:, part]))
            inner = jnp.sum(probability * grad_probability, -1, keepdims=True)
            grad_scores = (probability * (grad_probability - inner)).astype(BF16) * scale
            grad_scores = grad_scores.astype(BF16)
            from_content.append(matmul(grad_scores, keys[:, part]))
            to_keys.append(left_transposed(grad_scores, content_q[:, part]))
            flipped = jnp.concatenate([matmul(flip, grad_scores), zeros], 1)
            spread = pltpu.roll(flipped, 0, 1, stride=1, stride_axis=0).astype(BF16)
            from_position.append(matmul(spread, table_ref[:, part]))
            to_table.append(left_transposed(spread, flipped_q[:, part]))
        grad_content = jnp.concatenate(from_content, 1)
        grad_position = jnp.concatenate(from_position, 1)
        high = grad_position.astype(BF16)
        low = (grad_position - high.astype(F32)).astype(BF16)
        grad_position = matmul(flip, high) + matmul(flip, low)
        bias_ref[0:1, :] = jnp.sum(grad_content, 0, keepdims=True)
        bias_ref[1:2, :] = jnp.sum(grad_position, 0, keepdims=True)
        joined = jnp.concatenate(
            [grad_content + grad_position] + to_keys + to_values, 1
        ).astype(BF16)
        joined_ref[...] = joined
        table_grad_ref[...] = jnp.concatenate(to_table, 1).astype(BF16)
        part_ref[...] = right_transposed(joined, weight_ref[:, : 3 * columns]).astype(BF16)

    return on_chip(
        body,
        "attention_back",
        (norm_grads, own, other, conv_kept, gains, weights, positions, kept),
        (
            ((rows, width), F32),
            ((rows, 3 * columns), BF16),
            ((2 * rows, columns), BF16),
            ((rows, width), BF16),
            ((1, width), F32),
            ((2, columns), F32),
        ),
    )


def mixed_assemble(pairs, table, width):
    columns = pairs[0][0].shape[1]

    def body(ins, outs, _):
        for group in range(2):
            for half in range(2):
                assemble(
                    ins[2 * group + half],
                    outs[0],
                    GATHER_ORDERS[group],
                    half,
                    4,
                    4 * group * columns,
                )
        outs[1][...] = matmul(ins[4][...], outs[0][:, 3 * columns : 4 * columns]).astype(BF16)

    return on_chip(
        body,
        "mixed_assemble",
        pairs[0] + pairs[1] + (table,),
        (((width, 8 * columns), BF16), ((table.shape[0], columns), BF16)),
    )


def mixed_weight_grads(joined, table, table_grad, total, kept, gains, conv_grads, split):
    width = gains.shape[1]
    columns = table_grad.shape[1]

    def whole(ins, target_ref):
        joined_ref, table_ref, table_grad_ref, total_ref, kept_ref, gain_ref, conv_ref = ins
        entries = entries_of(kept_residual(kept_ref, width), gain_ref[1:2, :])
        attended = kept_ref[:, 2 * width + 4 * columns : 2 * width + 5 * columns]
        target_ref[:, : 3 * columns] = left_transposed(entries, joined_ref[...])
        target_ref[:, 3 * columns : 4 * columns] = left_transposed(
            table_ref[...], table_grad_ref[...]
        )
        target_ref[:, 4 * columns : 5 * columns] = left_transposed(
            total_ref[...].astype(BF16), attended
        )
        target_ref[:, 5 * columns :] = conv_ref[...].astype(F32)

    def body(ins, outs, scratch):
        if not split:
            whole(ins, outs[0])
            return
        whole(ins, scratch[0])
        for group in range(2):
            part = scratch[0].at[:, 4 * group * columns : 4 * (group + 1) * columns]
            scatter_split(part, outs[2 * group], outs[2 * group + 1], SCATTER_ORDERS[group], 4)

    operands = (joined, table, table_grad, total, kept, gains, conv_grads)
    if not split:
        results = (((width, 8 * columns), F32),)
        return on_chip(body, "mixed_weight_grads", operands, results)[0]
    halves = (((2 * width, columns), F32), ((2 * width, columns), BF16))
    values = on_chip(
        body,
        "mixed_weight_grads",
        operands,
        halves + halves,
        scratch=(pltpu.VMEM((width, 8 * columns), F32),),
    )
    return values[0::2], values[1::2]


PAD = 16


def pad_rows(padded, rows, columns, value):
    padded[:PAD, :] = jnp.zeros((PAD, columns), F32)
    padded[PAD + rows :, :] = jnp.zeros((PAD, columns), F32)
    padded[PAD : PAD + rows, :] = value


def conv_forward(kept, own, other, gains, weights, depth_kernel):
    rows, width = own.shape
    taps, columns = depth_kernel.shape
    half_taps = (taps - 1) // 2

    def body(ins, outs, scratch):
        kept_ref, own_ref, other_ref, gain_ref, weight_ref, tap_ref = ins
        conv_ref, sums_ref = outs
        padded = scratch[0]
        after = kept_residual(kept_ref, width) + both_parts(own_ref, other_ref)
        conv_ref[:, :width] = after
        entries = entries_of(after, gain_ref[2:3, :])
        joined = matmul(entries, weight_ref[:, 5 * columns : 7 * columns])
        value = joined[:, :columns]
        gate = jax.nn.sigmoid(joined[:, columns:])
        conv_ref[:, width : width + columns] = value
        conv_ref[:, width + columns : width + 2 * columns] = gate
        pad_rows(padded, rows, columns, value * gate)
        total = jnp.zeros((rows, columns), F32)
        for tap in range(taps):
            start = PAD - half_taps + tap
            total = total + tap_ref[tap : tap + 1, :] * padded[start : start + rows, :]
        conv_ref[:, width + 2 * columns :] = total
        sums_ref[0:1, :] = jnp.sum(total, 0, keepdims=True)
        sums_ref[1:2, :] = jnp.sum(total * total, 0, keepdims=True)

    return on_chip(
        body,
        "conv_forward",
        (kept, own, other, gains, weights, depth_kernel),
        (((rows, width + 3 * columns), F32), ((2, columns), F32)),
        scratch=(pltpu.VMEM((rows + 2 * PAD, columns), F32),),
    )


def batch_norm(conv_ref, sums_ref, batch_ref, token_count):
    columns = sums_ref.shape[1]
    column_mean = sums_ref[0:1, :] / token_count
    inverse = lax.rsqrt(sums_ref[1:2, :] / token_count - column_mean * column_mean + EPSILON)
    standard = (conv_ref[:, conv_ref.shape[1] - columns :] - column_mean) * inverse
    return standard, inverse, standard * batch_ref[0:1, :] + batch_ref[1:2, :]


def norm_forward(conv_kept, sums, batch, weights, token_count):
    rows = conv_kept.shape[0]
    columns = sums.shape[1]
    width = weights.shape[0]

    def body(ins, outs, _):
        conv_ref, sums_ref, batch_ref, weight_ref = ins
        _, _, shifted = batch_norm(conv_ref, sums_ref, batch_ref, token_count)
        activated = (shifted * jax.nn.sigmoid(shifted)).astype(BF16)
        outs[0][...] = right_transposed(activated, weight_ref[:, 7 * columns :]).astype(BF16)

    return on_chip(
        body, "norm_forward", (conv_kept, sums, batch, weights), (((rows, width), BF16),)
    )[0]


def second_block(conv_kept, own, other, cotangent, gains, weights, mixed, sums, batch, count):
    rows, width = own.shape
    columns = sums.shape[1]
    half = weights.shape[1] // 4

    def body(ins, outs, _):
        conv_ref, own_ref, other_ref, cot_ref, gain_ref, weight_ref, mixed_ref = ins[:7]
        sums_ref, batch_ref = ins[7:]
        out_ref, grads_ref, rows_ref, grad_sums_ref, last_gain_ref, gain_grad_ref = outs
        residual = conv_ref[:, :width] + both_parts(own_ref, other_ref)
        normed, factor = norm_parts(residual)
        entries = (normed * gain_ref[3:4, :]).astype(BF16)
        rows_ref[:, width : 2 * width] = entries
        inner, branch_sum = [], 0.0
        for part in range(2):
            left = 2 * part * half
            pre = matmul(entries, weight_ref[:, left : left + half])
            sigma = jax.nn.sigmoid(pre)
            hidden = (pre * sigma).astype(BF16)
            inner.append(swish_slope(pre, sigma))
            if part == 0:
                rows_ref[:, 2 * width + half :] = hidden
            branch_sum += right_transposed(hidden, weight_ref[:, left + half : left + 2 * half])
        after = residual + 0.5 * branch_sum
        last_normed, last_factor = norm_parts(after)
        last_gain = gain_ref[4:5, :]
        out_ref[...] = own_half(last_normed * last_gain).astype(BF16)
        gradient, last_grad = norm_back(
            cot_ref[...].astype(F32), last_normed, last_factor, last_gain
        )
        last_gain_ref[...] = 0.5 * last_grad
        branch = (0.5 * gradient).astype(BF16)
        rows_ref[:, :width] = branch
        entry_grad = 0.0
        for part in range(2):
            left = 2 * part * half
            grad_hidden = matmul(branch, weight_ref[:, left + half : left + 2 * half])
            grad_pre = (grad_hidden * inner[part]).astype(BF16)
            if part == 0:
                rows_ref[:, 2 * width : 2 * width + half] = grad_pre
            entry_grad += right_transposed(grad_pre, weight_ref[:, left : left + half])
        passed, gain_grad = norm_back(entry_grad, normed, factor, gain_ref[3:4, :])
        gain_grad_ref[...] = 0.5 * gain_grad
        total = gradient + passed
        grads_ref[:, :width] = total
        standard, _, shifted = batch_norm(conv_ref, sums_ref, batch_ref, count)
        grad_shifted = matmul(total.astype(BF16), mixed_ref[:, 7 * columns :]) * swish_slope(
            shifted, jax.nn.sigmoid(shifted)
        )
        grads_ref[:, width:] = grad_shifted
        grad_sums_ref[0:1, :] = jnp.sum(grad_shifted, 0, keepdims=True)
        grad_sums_ref[1:2, :] = jnp.sum(grad_shifted * standard, 0, keepdims=True)

    return on_chip(
        body,
        "second_block",
        (conv_kept, own, other, cotangent, gains, weights, mixed, sums, batch),
        (
            ((rows // 2, width), BF16),
            ((rows, width + columns), F32),
            ((rows, 2 * width + 2 * half), BF16),
            ((2, columns), F32),
            ((1, width), F32),
            ((1, width), F32),
        ),
    )


def conv_backward(norm_grads, grad_sums, conv_kept, sums, batch, weights, depth_kernel, count):
    rows = conv_kept.shape[0]
    columns = sums.shape[1]
    width = weights.shape[0]
    taps = depth_kernel.shape[0]
    half_taps = (taps - 1) // 2

    def body(ins, outs, scratch):
        grads_ref, grad_sums_ref, conv_ref, sums_ref, batch_ref, weight_ref, tap_ref = ins
        grad_conv_ref, joined_ref, part_ref = outs
        padded = scratch[0]
        standard, inverse, _ = batch_norm(conv_ref, sums_ref, batch_ref, count)
        grad_conv = (inverse * batch_ref[0:1, :]) * (
            grads_ref[:, width:]
            - grad_sums_ref[0:1, :] / count
            - standard * (grad_sums_ref[1:2, :] / count)
        )
        grad_conv_ref[...] = grad_conv
        pad_rows(padded, rows, columns, grad_conv)
        total = jnp.zeros((rows, columns), F32)
        for tap in range(taps):
            start = PAD + half_taps - tap
            total = total + tap_ref[tap : tap + 1, :] * padded[start : start + rows, :]
        gate_sigma = conv_ref[:, width + columns : width + 2 * columns]
        grad_value = total * gate_sigma
        grad_gate = grad_value * conv_ref[:, width : width + columns] * (1.0 - gate_sigma)
        joined = jnp.concatenate([grad_value, grad_gate], 1).astype(BF16)
        joined_ref[...] = joined
        part_ref[...] = right_transposed(
            joined, weight_ref[:, 5 * columns : 7 * columns]
        ).astype(BF16)

    return on_chip(
        body,
        "conv_backward",
        (norm_grads, grad_sums, conv_kept, sums, batch, weights, depth_kernel),
        (((rows, columns), F32), ((rows, 2 * columns), BF16), ((rows, width), BF16)),
        scratch=(pltpu.VMEM((rows + 2 * PAD, columns), F32),),
    )


def conv_weight_grads(norm_grads, grad_conv, joined, conv_kept, sums, batch, gains, taps, count):
    rows, columns = grad_conv.shape
    width = gains.shape[1]
    half_taps = (taps - 1) // 2

    def body(ins, outs, scratch):
        grads_ref, grad_ref, joined_ref, conv_ref, sums_ref, batch_ref, gain_ref = ins
        padded = scratch[0]
        entries = entries_of(conv_ref[:, :width], gain_ref[2:3, :])
        outs[0][:, : 2 * columns] = left_transposed(entries, joined_ref[...]).astype(BF16)
        _, _, shifted = batch_norm(conv_ref, sums_ref, batch_ref, count)
        activated = (shifted * jax.nn.sigmoid(shifted)).astype(BF16)
        outs[0][:, 2 * columns :] = left_transposed(
            grads_ref[:, :width].astype(BF16), activated
        ).astype(BF16)
        value = conv_ref[:, width : width + columns]
        gate = conv_ref[:, width + columns : width + 2 * columns]
        pad_rows(padded, rows, columns, value * gate)
        grad_conv_value = grad_ref[...]
        for tap in range(taps):
            start = PAD - half_taps + tap
            outs[1][tap : tap + 1, :] = jnp.sum(
                padded[start : start + rows, :] * grad_conv_value, 0, keepdims=True
            )

    return on_chip(
        body,
        "conv_weight_grads",
        (norm_grads, grad_conv, joined, conv_kept, sums, batch, gains),
        (((width, 3 * columns), BF16), ((taps, columns), F32)),
        scratch=(pltpu.VMEM((rows + 2 * PAD, columns), F32),),
    )


def first_back(gradient, own, other, kept, pre, gains, weights):
    rows, width = gradient.shape
    hidden = weights.shape[1] // 2

    def body(ins, outs, _):
        grad_ref, own_ref, other_ref, kept_ref, pre_ref, gain_ref, weight_ref = ins
        grads_ref, keep_ref, send_ref, gain_grad_ref = outs
        normed, factor = norm_parts(kept_residual(kept_ref, width))
        passed, gain_grad = norm_back(
            both_parts(own_ref, other_ref), normed, factor, gain_ref[1:2, :]
        )
        gain_grad_ref[...] = 0.5 * gain_grad
        total = grad_ref[...] + passed
        keep_ref[:, :width] = own_half(total)
        part = ff_back_body(total, pre_ref[...], weight_ref, grads_ref)
        keep_ref[:, width:] = own_half(part)
        send_ref[...] = other_half(part).astype(BF16)

    return on_chip(
        body,
        "first_back",
        (gradient, own, other, kept, pre, gains, weights),
        (
            ((rows, width + 2 * hidden), BF16),
            ((rows // 2, 2 * width), F32),
            ((rows // 2, width), BF16),
            ((1, width), F32),
        ),
    )


def input_back(keep, other, tokens, gains, gain_grads, tap_grads, bias_grads):
    rows, width = tokens.shape
    taps, columns = tap_grads.shape
    upper = (taps + 1) // 2
    packed_rows = -(-(6 + upper) // 8) * 8

    def body(ins, outs, _):
        keep_ref, other_ref, x_ref, gain_ref = ins[:4]
        tap_ref, bias_ref = ins[8:]
        packed = outs[1]
        normed, factor = norm_parts(x_ref[...].astype(F32))
        passed, gain_grad = norm_back(
            keep_ref[:, width:] + other_ref[...].astype(F32), normed, factor, gain_ref[0:1, :]
        )
        outs[0][...] = keep_ref[:, :width] + passed
        packed[...] = jnp.zeros((packed_rows, 2 * columns), F32)
        packed[0:1, :] = gain_grad
        for place in range(4):
            packed[place + 1 : place + 2, :] = ins[4 + place][...]
        packed[5:6, :columns] = bias_ref[0:1, :]
        packed[5:6, columns:] = bias_ref[1:2, :]
        packed[6 : 6 + upper, :columns] = tap_ref[:upper, :]
        packed[6 : 6 + taps - upper, columns:] = tap_ref[upper:, :]

    return on_chip(
        body,
        "input_back",
        (keep, other, tokens, gains) + tuple(gain_grads) + (tap_grads, bias_grads),
        (((rows, width), F32), ((packed_rows, 2 * columns), F32)),
        flops=1_000_000,
    )


def reduce_plain(grads):
    return lax.psum_scatter(grads.astype(BF16), "dp", scatter_dimension=0, tiled=True).astype(F32)


def stacked_columns(pieces, count):
    width = pieces.shape[1] // count
    return jnp.stack([pieces[:, index * width : (index + 1) * width] for index in range(count)])


def unstacked(stacked):
    return [stacked[index] for index in range(stacked.shape[0])]


def body(
    tokens,
    norm_gains,
    first_in,
    first_out,
    attention_in,
    attention_out,
    head_biases,
    gated_in,
    pointwise_out,
    depth_kernel,
    batch_scale,
    batch_shift,
    second_in,
    second_out,
    cotangent,
):
    local_heads = HEAD_TOTAL // lax.axis_size("tensor")
    length = tokens.shape[0] * lax.axis_size("tensor")
    token_count = float(length * lax.axis_size("dp"))
    columns = attention_out.shape[1]
    hidden = first_in.shape[1]
    width = tokens.shape[1]
    table = sinusoid(length, width).astype(BF16)
    batch = jnp.stack([batch_scale, batch_shift])
    split = doubling()

    def gather(pieces):
        return lax.all_gather(jnp.concatenate(pieces, 1), "dp", axis=0, tiled=True)

    tokens_all = both_halves(tokens)
    cotangent_all = both_halves(cotangent)

    second_own = jnp.concatenate([second_in, second_out], 1)
    second_pair = jnp.concatenate([second_own, swap(second_own)], 1)
    if split:
        batch_one = (first_in, first_out)
        batch_two = (
            attention_in.reshape(-1, columns),
            jnp.concatenate([attention_out, gated_in.reshape(-1, columns), pointwise_out], 0),
        )
        batch_one = gather_join(batch_one, gather_send(batch_one, 0))
        arrived_one = gather_send(batch_one, 1)
        arrived_two = gather_send(tie(batch_two, batch_one), 0)
        batch_one = gather_join(batch_one, arrived_one)
        arrived_one = gather_send(batch_one, 2)
        batch_two = gather_join(batch_two, tie(arrived_two, batch_one))
        arrived_two = gather_send(batch_two, 1)
        batch_one = gather_join(batch_one, tie(arrived_one, batch_two))
        second_pair = tie(second_pair, batch_one)
        batch_two = gather_join(batch_two, tie(arrived_two, batch_one))
        arrived_two = gather_send(batch_two, 2)
        batch_one = gather_last(batch_one)
    else:
        batch_one = gather([first_in, first_out])
        mixed_weights = gather(
            unstacked(attention_in) + [attention_out] + unstacked(gated_in) + [pointwise_out]
        )
        positions = position_forward(table, mixed_weights, columns)
    second_weights = gather([second_pair])

    pre1, part1, first_weights = first_forward(tokens_all, norm_gains, batch_one)
    other1 = swap(part1)
    if split:
        batch_two = gather_last(gather_join(batch_two, tie(arrived_two, other1)))
        mixed_weights, positions = mixed_assemble(batch_two, table, width)
    kept, part2 = attention_forward(
        tokens_all, part1, other1, norm_gains, mixed_weights, positions, head_biases, local_heads
    )
    other2 = swap(part2)
    conv_kept, sums = conv_forward(
        kept, part2, other2, norm_gains, mixed_weights, depth_kernel
    )
    sums = tie(sum_over(sums, "dp"), second_weights)
    part3 = norm_forward(conv_kept, sums, batch, mixed_weights, token_count)
    other3 = swap(part3)
    block_out, norm_grads, second_rows, grad_sums, gain5, gain4 = second_block(
        conv_kept,
        part3,
        other3,
        cotangent_all,
        norm_gains,
        second_weights,
        mixed_weights,
        sums,
        batch,
        token_count,
    )
    second_grads = second_weight_grads(second_rows, width)
    reduced_second = reduce_plain(second_grads)
    grad_sums = sum_over(grad_sums, "dp")
    grad_sums = tie(grad_sums, second_grads)
    grad_conv, joined3, part6 = conv_backward(
        norm_grads, grad_sums, conv_kept, sums, batch, mixed_weights, depth_kernel, token_count
    )
    other6 = swap(part6)
    conv_grads, tap_grads = conv_weight_grads(
        norm_grads,
        grad_conv,
        joined3,
        conv_kept,
        sums,
        batch,
        norm_gains,
        depth_kernel.shape[0],
        token_count,
    )
    other6 = tie(other6, conv_grads)
    grad2, joined2, table_grad, part7, gain3, bias_grads = attention_back(
        norm_grads,
        part6,
        other6,
        conv_kept,
        norm_gains,
        mixed_weights,
        positions,
        kept,
        local_heads,
    )
    other7 = swap(part7)
    mixed_grads = mixed_weight_grads(
        joined2, table, table_grad, grad2, kept, norm_gains, conv_grads, split
    )
    if split:
        keeps, sends = mixed_grads
        mixed_keeps, sends = scatter_add(keeps, scatter_send(sends, 0), 0, "mixed_sum")
        mixed_arrived = scatter_send(sends, 1)
        other7 = tie(other7, mixed_arrived)
    first_rows, keep8, send8, gain2 = first_back(
        grad2, part7, other7, kept, pre1, norm_gains, first_weights
    )
    other8 = swap(send8)
    small = ((gain2, gain3, gain4, gain5), tap_grads, bias_grads)
    if split:
        mixed_keeps, sends = scatter_add(mixed_keeps, mixed_arrived, 1, "mixed_sum")
        mixed_arrived = scatter_send(sends, 2)
        keeps, sends = ff_weight_split(
            tie(first_rows, mixed_keeps), tokens_all, norm_gains, 0, "first_weight_grads"
        )
        first_arrived = scatter_send(sends, 0)
        first_arrived = tie(first_arrived, mixed_arrived)
        first_keeps, sends = scatter_add(keeps, first_arrived, 0, "first_sum")
        first_arrived = scatter_send(sends, 1)
        mixed_keeps, sends = scatter_add(
            mixed_keeps, tie(mixed_arrived, first_keeps), 2, "mixed_sum"
        )
        mixed_arrived = scatter_send(sends, 3)
        first_arrived = tie(first_arrived, mixed_arrived)
        first_keeps, sends = scatter_add(first_keeps, first_arrived, 1, "first_sum")
        first_arrived = scatter_send(sends, 2)
        (mixed_a, mixed_b), _ = scatter_add(
            mixed_keeps, tie(mixed_arrived, first_keeps), 3, "mixed_sum"
        )
        other8 = tie(other8, mixed_a)
        grad_start, packed = input_back(keep8, other8, tokens, norm_gains, *small)
        first_arrived = tie(first_arrived, packed)
        first_keeps, sends = scatter_add(first_keeps, first_arrived, 2, "first_sum")
        first_arrived = scatter_send(sends, 3)
        (reduced_in, reduced_out), _ = scatter_add(first_keeps, first_arrived, 3, "first_sum")
        rows = mixed_a.shape[0] // 4
        reduced_attention = mixed_a.reshape(4, rows, columns)
        reduced_mixing = mixed_b[:rows]
        reduced_gated = mixed_b[rows : 3 * rows].reshape(2, rows, columns)
        reduced_pointwise = mixed_b[3 * rows :]
    else:
        grad_start, packed = input_back(keep8, other8, tokens, norm_gains, *small)
        first_grads = reduce_plain(
            ff_weight_grads(first_rows, tokens_all, norm_gains, 0, "first_weight_grads")
        )
        reduced_in, reduced_out = first_grads[:, :hidden], first_grads[:, hidden:]
        mixed = reduce_plain(mixed_grads)
        reduced_attention = stacked_columns(mixed[:, : 4 * columns], 4)
        reduced_mixing = mixed[:, 4 * columns : 5 * columns]
        reduced_gated = stacked_columns(mixed[:, 5 * columns : 7 * columns], 2)
        reduced_pointwise = mixed[:, 7 * columns :]
    packed = sum_over(packed, "dp")
    gain_total = sum_over(packed[:5], "tensor")
    bias_total = packed[5].reshape(bias_grads.shape)
    taps = tap_grads.shape[0]
    upper = (taps + 1) // 2
    tap_total = jnp.concatenate(
        [packed[6 : 6 + upper, :columns], packed[6 : 6 + taps - upper, columns:]], 0
    )
    return (
        block_out,
        grad_start,
        gain_total,
        reduced_in,
        reduced_out,
        reduced_attention,
        reduced_mixing,
        bias_total,
        reduced_gated,
        reduced_pointwise,
        tap_total,
        grad_sums[1],
        grad_sums[0],
        reduced_second[:, :hidden],
        reduced_second[:, hidden:],
    )


def solution(mesh):
    placed = (
        P(("dp", "tensor"), None),
        P(),
        P("dp", "tensor"),
        P("dp", "tensor"),
        P(None, "dp", "tensor"),
        P("dp", "tensor"),
        P(None, "tensor"),
        P(None, "dp", "tensor"),
        P("dp", "tensor"),
        P(None, "tensor"),
        P("tensor"),
        P("tensor"),
        P("dp", "tensor"),
        P("dp", "tensor"),
        P(("dp", "tensor"), None),
    )
    return jax.shard_map(
        body,
        mesh=mesh,
        in_specs=placed,
        out_specs=(
            P(("dp", "tensor"), None),
            P(("dp", "tensor"), None),
            P(),
            P("dp", "tensor"),
            P("dp", "tensor"),
            P(None, "dp", "tensor"),
            P("dp", "tensor"),
            P(None, "tensor"),
            P(None, "dp", "tensor"),
            P("dp", "tensor"),
            P(None, "tensor"),
            P("tensor"),
            P("tensor"),
            P("dp", "tensor"),
            P("dp", "tensor"),
        ),
        check_vma=False,
    )
```

```python
import math

import jax
import jax.numpy as jnp
from jax import lax
from jax.experimental import pallas as pl
from jax.experimental.pallas import tpu as pltpu
from jax.sharding import PartitionSpec as P

HEAD_TOTAL = 8
EPSILON = 1e-05
BF16 = jnp.bfloat16
F32 = jnp.float32


def matmul(left_side, right_side):
    return jnp.dot(left_side, right_side, preferred_element_type=F32)


def right_transposed(left_side, right_side):
    return lax.dot_general(
        left_side, right_side, (((1,), (1,)), ((), ())), preferred_element_type=F32
    )


def left_transposed(left_side, right_side):
    return lax.dot_general(
        left_side, right_side, (((0,), (0,)), ((), ())), preferred_element_type=F32
    )


def swish_slope(pre_value, gate_sigma):
    return gate_sigma * (1.0 + pre_value * (1.0 - gate_sigma))


def norm_parts(residual):
    centred = residual - jnp.mean(residual, -1, keepdims=True)
    factor = lax.rsqrt(jnp.mean(centred * centred, -1, keepdims=True) + EPSILON)
    return centred * factor, factor


def norm_back(gradient, normed, factor, norm_gain):
    scaled = gradient * norm_gain
    inner_sum = (
        scaled
        - jnp.mean(scaled, -1, keepdims=True)
        - normed * jnp.mean(scaled * normed, -1, keepdims=True)
    )
    return factor * inner_sum, jnp.sum(gradient * normed, 0, keepdims=True)


def sinusoid(length, features):
    offsets = jnp.arange(2 * length, dtype=F32) - (length - 1)
    half_width = features // 2
    frequency = jnp.exp(jnp.arange(half_width, dtype=F32) * (-math.log(10000.0) / half_width))
    angles = offsets[:, None] * frequency[None, :]
    table = jnp.concatenate([jnp.sin(angles), jnp.cos(angles)], 1)
    return jnp.where(offsets[:, None] < length, table, 0.0)


def on_chip(function, name, operands, results, scratch=(), flops=300_000_000):
    count = len(operands)
    total = count + len(results)

    def kernel(*refs):
        function(refs[:count], refs[count:total], refs[total:])

    moved = sum(value.size * value.dtype.itemsize for value in operands)
    moved += sum(math.prod(shape) * jnp.dtype(kind).itemsize for shape, kind in results)
    return pl.pallas_call(
        kernel,
        out_shape=[jax.ShapeDtypeStruct(shape, kind) for shape, kind in results],
        in_specs=[pl.BlockSpec(memory_space=pltpu.VMEM)] * count,
        out_specs=[pl.BlockSpec(memory_space=pltpu.VMEM)] * len(results),
        scratch_shapes=list(scratch),
        compiler_params=pltpu.CompilerParams(vmem_limit_bytes=24 * 1024 * 1024),
        cost_estimate=pl.CostEstimate(flops=flops, bytes_accessed=moved, transcendentals=0),
        name=name,
    )(*operands)


def swap(value):
    return lax.ppermute(value, "tensor", [(0, 1), (1, 0)])


def both_halves(own):
    other = swap(own)
    first = lax.axis_index("tensor") == 0
    return jnp.concatenate([jnp.where(first, own, other), jnp.where(first, other, own)], 0)


def own_half(value):
    half = value.shape[0] // 2
    return jnp.where(lax.axis_index("tensor") == 0, value[:half], value[half:])


def other_half(value):
    half = value.shape[0] // 2
    return jnp.where(lax.axis_index("tensor") == 0, value[half:], value[:half])


def shift(value, axis, mask):
    return lax.ppermute(value, axis, [(k, k ^ mask) for k in range(lax.axis_size(axis))])


def sum_over(value, axis, step=1, stop=None):
    size = lax.axis_size(axis)
    if size & (size - 1):
        return lax.psum(value, axis)
    stop = stop or size
    while step < stop:
        if step >= 4 and step * 4 <= stop:
            near, far, both = (shift(value, axis, step * times) for times in (1, 2, 3))
            value = (value + near) + (far + both)
            step *= 4
        else:
            value = value + shift(value, axis, step)
            step *= 2
    return value


GATHER_ORDERS = ((8, 4, 2, 1), (8, 2, 4, 1))
SCATTER_ORDERS = ((1, 2, 4, 8), (1, 4, 2, 8))


def doubling():
    return lax.axis_size("dp") == 16


def distances(order):
    blocks = [0]
    for mask in order:
        blocks = blocks + [block ^ mask for block in blocks]
    return blocks


def halving(order):
    return distances(order[::-1])


def gather_send(values, stage):
    return tuple(shift(value, "dp", order[stage]) for value, order in zip(values, GATHER_ORDERS))


def gather_join(pair, arrived, joint=False):
    sizes = [value.shape[0] for value in pair]

    def body(ins, outs, _):
        for group in range(2):
            rows = sizes[group]
            target, start = (outs[0], 2 * rows * group) if joint else (outs[group], 0)
            source, begin = (ins[2], rows * group) if len(arrived) == 1 else (ins[2 + group], 0)
            target[start : start + rows, :] = ins[group][...]
            target[start + rows : start + 2 * rows, :] = source[begin : begin + rows, :]

    columns, kind = pair[0].shape[1], pair[0].dtype
    if joint:
        results = (((2 * sum(sizes), columns), kind),)
    else:
        results = tuple(((2 * rows, columns), kind) for rows in sizes)
    return tuple(on_chip(body, "gather_join", tuple(pair) + arrived, results, flops=1_000))


def tie(values, *others):
    return lax.optimization_barrier((values, others))[0]


def assemble(ref, target_ref, group, half, matrices, first_column):
    device = lax.axis_index("dp")
    blocks = distances(GATHER_ORDERS[group])
    count = len(blocks) // 2
    rows = target_ref.shape[0] // len(blocks)
    columns = ref.shape[1]
    for place in range(count):
        owner = device ^ blocks[half * count + place]
        target = pl.ds(pl.multiple_of(owner * rows, rows), rows)
        for matrix in range(matrices):
            start = ((group * count + place) * matrices + matrix) * rows
            left = first_column + matrix * columns
            target_ref[target, left : left + columns] = ref[start : start + rows, :]


def scatter_split(total_ref, keep_ref, send_ref, group, matrices):
    device = lax.axis_index("dp")
    blocks = halving(SCATTER_ORDERS[group])
    count = len(blocks) // 2
    rows = total_ref.shape[0] // len(blocks)
    columns = keep_ref.shape[1]
    first = group * keep_ref.shape[0]
    for place, block in enumerate(blocks):
        source = pl.ds(pl.multiple_of((device ^ block) * rows, rows), rows)
        for matrix in range(matrices):
            piece = total_ref[source, matrix * columns : (matrix + 1) * columns]
            start = ((place % count) * matrices + matrix) * rows
            if place < count:
                keep_ref[start : start + rows, :] = piece
            else:
                send_ref[first + start : first + start + rows, :] = piece.astype(BF16)


def scatter_send(sends, stage):
    return tuple(shift(send, "dp", order[stage]) for send, order in zip(sends, SCATTER_ORDERS))


def arrived_part(refs, group, rows):
    if len(refs) == 1:
        return refs[0][group * rows : (group + 1) * rows, :].astype(F32)
    return refs[group][...].astype(F32)


def scatter_add(keeps, arrived, stage, name):
    rows, columns = keeps[0].shape
    half = rows // 2
    last = stage == len(SCATTER_ORDERS[0]) - 1
    joint = stage == len(SCATTER_ORDERS[0]) - 2
    results = (((rows if last else half, columns), F32),) * 2
    if not last:
        results += (((rows, columns), BF16),) if joint else (((half, columns), BF16),) * 2

    def body(ins, outs, _):
        for group in range(2):
            total = ins[group][...] + arrived_part(ins[2:], group, rows)
            if last:
                outs[group][...] = total
                continue
            outs[group][...] = total[:half]
            if joint:
                outs[2][group * half : (group + 1) * half, :] = total[half:].astype(BF16)
            else:
                outs[2 + group][...] = total[half:].astype(BF16)

    values = on_chip(body, name, tuple(keeps) + tuple(arrived), results, flops=1_000)
    return values[:2], values[2:]


def entries_of(residual, gain):
    return (norm_parts(residual)[0] * gain).astype(BF16)


def ff_forward_body(entries, weight_ref, part_ref):
    half = weight_ref.shape[1] // 2
    pre = matmul(entries, weight_ref[:, :half])
    hidden = (pre * jax.nn.sigmoid(pre)).astype(BF16)
    part_ref[...] = right_transposed(hidden, weight_ref[:, half:]).astype(BF16)
    return pre


def both_parts(own_ref, other_ref):
    return own_ref[...].astype(F32) + other_ref[...].astype(F32)


def first_forward(tokens, gains, weights):
    rows, width = tokens.shape
    split = isinstance(weights, tuple)
    pieces = weights if split else (weights,)
    hidden = pieces[0].shape[1] if split else weights.shape[1] // 2

    def body(ins, outs, _):
        weight_ref = ins[2]
        if split:
            weight_ref = outs[2]
            for group in range(2):
                for half in range(2):
                    assemble(ins[2 + half], weight_ref, group, half, 1, group * hidden)
        entries = entries_of(ins[0][...].astype(F32), ins[1][0:1, :])
        outs[0][...] = ff_forward_body(entries, weight_ref, outs[1])

    results = (((rows, hidden), F32), ((rows, width), BF16))
    if split:
        results += (((width, 2 * hidden), BF16),)
    values = on_chip(body, "first_forward", (tokens, gains) + pieces, results)
    return values if split else tuple(values) + (weights,)


def second_forward(conv_kept, own, other, gains, weights):
    rows, width = own.shape
    hidden = weights.shape[1] // 2

    def body(ins, outs, _):
        kept_ref, part_ref = outs
        after = ins[0][:, :width] + both_parts(ins[1], ins[2])
        kept_ref[:, :width] = after
        kept_ref[:, width:] = ff_forward_body(
            entries_of(after, ins[3][3:4, :]), ins[4], part_ref
        )

    return on_chip(
        body,
        "second_forward",
        (conv_kept, own, other, gains, weights),
        (((rows, width + hidden), F32), ((rows, width), BF16)),
    )


def ff_back_body(gradient, pre, weight_ref, grads_ref):
    width = gradient.shape[1]
    half = weight_ref.shape[1] // 2
    branch = (0.5 * gradient).astype(BF16)
    grads_ref[:, :width] = branch
    grad_hidden = matmul(branch, weight_ref[:, half:])
    sigma = jax.nn.sigmoid(pre)
    grad_pre = (grad_hidden * swish_slope(pre, sigma)).astype(BF16)
    grads_ref[:, width : width + half] = grad_pre
    grads_ref[:, width + half : width + 2 * half] = (pre * sigma).astype(BF16)
    return right_transposed(grad_pre, weight_ref[:, :half])


def second_back(kept, own, other, cotangent, gains, weights):
    rows, width = own.shape
    hidden = weights.shape[1] // 2

    def body(ins, outs, _):
        kept_ref, own_ref, other_ref, cot_ref, gain_ref, weight_ref = ins
        out_ref, grad_ref, grads_ref, part_ref, gain_grad_ref = outs
        after = kept_ref[:, :width] + 0.5 * both_parts(own_ref, other_ref)
        normed, factor = norm_parts(after)
        gain = gain_ref[4:5, :]
        out_ref[...] = own_half(normed * gain).astype(BF16)
        gradient, gain_grad = norm_back(cot_ref[...].astype(F32), normed, factor, gain)
        gain_grad_ref[...] = 0.5 * gain_grad
        grad_ref[...] = gradient
        part_ref[...] = ff_back_body(
            gradient, kept_ref[:, width:], weight_ref, grads_ref
        ).astype(BF16)

    return on_chip(
        body,
        "second_back",
        (kept, own, other, cotangent, gains, weights),
        (
            ((rows // 2, width), BF16),
            ((rows, width), F32),
            ((rows, width + 2 * hidden), BF16),
            ((rows, width), BF16),
            ((1, width), F32),
        ),
    )


def ff_weight_grads(grads, residual, gains, row, name):
    width = gains.shape[1]
    half = (grads.shape[1] - width) // 2

    def body(ins, outs, _):
        grads_ref, x_ref, gain_ref = ins
        entries = entries_of(x_ref[:, :width].astype(F32), gain_ref[row : row + 1, :])
        outs[0][:, :half] = left_transposed(entries, grads_ref[:, width : width + half]).astype(
            BF16
        )
        outs[0][:, half:] = left_transposed(
            grads_ref[:, :width], grads_ref[:, width + half :]
        ).astype(BF16)

    return on_chip(body, name, (grads, residual, gains), (((width, 2 * half), BF16),))[0]


def ff_weight_split(grads, residual, gains, row, name):
    width = gains.shape[1]
    half = (grads.shape[1] - width) // 2

    def body(ins, outs, scratch):
        grads_ref, x_ref, gain_ref = ins
        entries = entries_of(x_ref[:, :width].astype(F32), gain_ref[row : row + 1, :])
        scratch[0][...] = left_transposed(entries, grads_ref[:, width : width + half])
        scatter_split(scratch[0], outs[0], outs[2], 0, 1)
        scratch[0][...] = left_transposed(grads_ref[:, :width], grads_ref[:, width + half :])
        scatter_split(scratch[0], outs[1], outs[2], 1, 1)

    values = on_chip(
        body,
        name,
        (grads, residual, gains),
        (((width // 2, half), F32),) * 2 + (((width, half), BF16),),
        scratch=(pltpu.VMEM((width, half), F32),),
    )
    return values[:2], values[2:]


def kept_residual(kept_ref, width):
    return kept_ref[:, :width].astype(F32) + kept_ref[:, width : 2 * width].astype(F32)


def position_forward(table, weights, columns):
    def body(ins, outs, _):
        outs[0][...] = matmul(ins[0][...], ins[1][:, 3 * columns : 4 * columns]).astype(BF16)

    return on_chip(
        body, "position_forward", (table, weights), (((table.shape[0], columns), BF16),)
    )[0]


def attention_forward(tokens, own, other, gains, weights, positions, biases, heads):
    rows, width = tokens.shape
    columns = biases.shape[1]
    features = columns // heads
    scale = features ** (-0.5)
    start = 2 * width

    def body(ins, outs, _):
        x_ref, own_ref, other_ref, gain_ref, weight_ref, table_ref, bias_ref = ins
        kept_ref, part_ref = outs
        after = x_ref[...].astype(F32) + 0.5 * both_parts(own_ref, other_ref)
        high = after.astype(BF16)
        kept_ref[:, :width] = high
        kept_ref[:, width : 2 * width] = (after - high.astype(F32)).astype(BF16)
        entries = entries_of(after, gain_ref[1:2, :])
        joined = matmul(entries, weight_ref[:, : 3 * columns])
        queries = joined[:, :columns]
        content_q = (queries + bias_ref[0:1, :]).astype(BF16)
        position_q = (queries + bias_ref[1:2, :]).astype(BF16)
        keys = joined[:, columns : 2 * columns].astype(BF16)
        values = joined[:, 2 * columns :].astype(BF16)
        kept_ref[:, start : start + columns] = content_q
        kept_ref[:, start + columns : start + 2 * columns] = position_q
        kept_ref[:, start + 2 * columns : start + 3 * columns] = keys
        kept_ref[:, start + 3 * columns : start + 4 * columns] = values
        mixed = []
        for head in range(heads):
            part = slice(head * features, (head + 1) * features)
            content = right_transposed(content_q[:, part], keys[:, part])
            raw = right_transposed(position_q[:, part], table_ref[:, part])
            shifted = pltpu.roll(raw, rows + 1, 1, stride=1, stride_axis=0)[:, :rows]
            scores = (content + shifted) * scale
            lifted = jnp.exp(scores - jnp.max(scores, -1, keepdims=True))
            probability = (lifted / jnp.sum(lifted, -1, keepdims=True)).astype(BF16)
            place = start + 5 * columns + head * rows
            kept_ref[:, place : place + rows] = probability
            mixed.append(matmul(probability, values[:, part]))
        attended = jnp.concatenate(mixed, 1).astype(BF16)
        kept_ref[:, start + 4 * columns : start + 5 * columns] = attended
        part_ref[...] = right_transposed(
            attended, weight_ref[:, 4 * columns : 5 * columns]
        ).astype(BF16)

    return on_chip(
        body,
        "attention_forward",
        (tokens, own, other, gains, weights, positions, biases),
        (((rows, start + 5 * columns + heads * rows), BF16), ((rows, width), BF16)),
    )


def attention_back(norm_grads, own, other, conv_kept, gains, weights, positions, kept, heads):
    rows, width = own.shape
    columns = positions.shape[1]
    features = columns // heads
    scale = features ** (-0.5)
    start = 2 * width

    def body(ins, outs, _):
        grad_ref, own_ref, other_ref, x_ref, gain_ref, weight_ref, table_ref, kept_ref = ins
        total_ref, joined_ref, table_grad_ref, part_ref, gain_grad_ref, bias_ref = outs
        normed, factor = norm_parts(x_ref[:, :width])
        passed, gain_grad = norm_back(
            both_parts(own_ref, other_ref), normed, factor, gain_ref[2:3, :]
        )
        gain_grad_ref[...] = 0.5 * gain_grad
        total = grad_ref[:, :width] + passed
        total_ref[...] = total
        grad_mixed = matmul(
            total.astype(BF16), weight_ref[:, 4 * columns : 5 * columns]
        ).astype(BF16)
        line = lax.broadcasted_iota(jnp.int32, (rows, rows), 0)
        place = lax.broadcasted_iota(jnp.int32, (rows, rows), 1)
        flip = (line + place == rows - 1).astype(F32).astype(BF16)
        content_q = kept_ref[:, start : start + columns]
        flipped_q = matmul(flip, kept_ref[:, start + columns : start + 2 * columns]).astype(BF16)
        keys = kept_ref[:, start + 2 * columns : start + 3 * columns]
        values = kept_ref[:, start + 3 * columns : start + 4 * columns]
        zeros = jnp.zeros((rows, rows), F32)
        from_content, from_position, to_keys, to_values, to_table = [], [], [], [], []
        for head in range(heads):
            part = slice(head * features, (head + 1) * features)
            left = start + 5 * columns + head * rows
            rounded = kept_ref[:, left : left + rows]
            probability = rounded.astype(F32)
            grad_probability = right_transposed(grad_mixed[:, part], values[:, part])
            to_values.append(left_transposed(rounded, grad_mixed[:, part]))
            inner = jnp.sum(probability * grad_probability, -1, keepdims=True)
            grad_scores = (probability * (grad_probability - inner)).astype(BF16) * scale
            grad_scores = grad_scores.astype(BF16)
            from_content.append(matmul(grad_scores, keys[:, part]))
            to_keys.append(left_transposed(grad_scores, content_q[:, part]))
            flipped = jnp.concatenate([matmul(flip, grad_scores), zeros], 1)
            spread = pltpu.roll(flipped, 0, 1, stride=1, stride_axis=0).astype(BF16)
            from_position.append(matmul(spread, table_ref[:, part]))
            to_table.append(left_transposed(spread, flipped_q[:, part]))
        grad_content = jnp.concatenate(from_content, 1)
        grad_position = jnp.concatenate(from_position, 1)
        high = grad_position.astype(BF16)
        low = (grad_position - high.astype(F32)).astype(BF16)
        grad_position = matmul(flip, high) + matmul(flip, low)
        bias_ref[0:1, :] = jnp.sum(grad_content, 0, keepdims=True)
        bias_ref[1:2, :] = jnp.sum(grad_position, 0, keepdims=True)
        joined = jnp.concatenate(
            [grad_content + grad_position] + to_keys + to_values, 1
        ).astype(BF16)
        joined_ref[...] = joined
        table_grad_ref[...] = jnp.concatenate(to_table, 1).astype(BF16)
        part_ref[...] = right_transposed(joined, weight_ref[:, : 3 * columns]).astype(BF16)

    return on_chip(
        body,
        "attention_back",
        (norm_grads, own, other, conv_kept, gains, weights, positions, kept),
        (
            ((rows, width), F32),
            ((rows, 3 * columns), BF16),
            ((2 * rows, columns), BF16),
            ((rows, width), BF16),
            ((1, width), F32),
            ((2, columns), F32),
        ),
    )


def second_assemble(halves, width):
    columns = halves[0].shape[1]

    def body(ins, outs, _):
        for group in range(2):
            for half in range(2):
                assemble(ins[half], outs[0], group, half, 1, group * columns)

    return on_chip(
        body, "second_assemble", halves, (((width, 2 * columns), BF16),), flops=1_000
    )[0]


def mixed_assemble(halves, table, width):
    columns = halves[0].shape[1]

    def body(ins, outs, _):
        for group in range(2):
            for half in range(2):
                assemble(ins[half], outs[0], group, half, 4, 4 * group * columns)
        outs[1][...] = matmul(ins[2][...], outs[0][:, 3 * columns : 4 * columns]).astype(BF16)

    return on_chip(
        body,
        "mixed_assemble",
        halves + (table,),
        (((width, 8 * columns), BF16), ((table.shape[0], columns), BF16)),
    )


def mixed_weight_grads(joined, table, table_grad, total, kept, gains, conv_grads, split):
    width = gains.shape[1]
    columns = table_grad.shape[1]

    def whole(ins, target_ref):
        joined_ref, table_ref, table_grad_ref, total_ref, kept_ref, gain_ref, conv_ref = ins
        entries = entries_of(kept_residual(kept_ref, width), gain_ref[1:2, :])
        attended = kept_ref[:, 2 * width + 4 * columns : 2 * width + 5 * columns]
        target_ref[:, : 3 * columns] = left_transposed(entries, joined_ref[...])
        target_ref[:, 3 * columns : 4 * columns] = left_transposed(
            table_ref[...], table_grad_ref[...]
        )
        target_ref[:, 4 * columns : 5 * columns] = left_transposed(
            total_ref[...].astype(BF16), attended
        )
        target_ref[:, 5 * columns :] = conv_ref[...].astype(F32)

    def body(ins, outs, scratch):
        if not split:
            whole(ins, outs[0])
            return
        whole(ins, scratch[0])
        for group in range(2):
            part = scratch[0].at[:, 4 * group * columns : 4 * (group + 1) * columns]
            scatter_split(part, outs[group], outs[2], group, 4)

    operands = (joined, table, table_grad, total, kept, gains, conv_grads)
    if not split:
        results = (((width, 8 * columns), F32),)
        return on_chip(body, "mixed_weight_grads", operands, results)[0]
    values = on_chip(
        body,
        "mixed_weight_grads",
        operands,
        (((2 * width, columns), F32),) * 2 + (((4 * width, columns), BF16),),
        scratch=(pltpu.VMEM((width, 8 * columns), F32),),
    )
    return values[:2], values[2:]


def mixed_finish(keeps, arrived):
    rows, columns = keeps[0].shape
    one = rows // 4

    def body(ins, outs, _):
        first = ins[0][...] + arrived_part(ins[2:], 0, rows)
        for matrix in range(4):
            outs[0][matrix] = first[matrix * one : (matrix + 1) * one]
        second = ins[1][...] + arrived_part(ins[2:], 1, rows)
        outs[1][...] = second[:one]
        outs[2][0] = second[one : 2 * one]
        outs[2][1] = second[2 * one : 3 * one]
        outs[3][...] = second[3 * one :]

    return on_chip(
        body,
        "mixed_finish",
        tuple(keeps) + tuple(arrived),
        (
            ((4, one, columns), F32),
            ((one, columns), F32),
            ((2, one, columns), F32),
            ((one, columns), F32),
        ),
        flops=1_000,
    )


def unpack_small(parts, taps, columns):
    upper = (taps + 1) // 2
    width = parts[0].shape[1]

    def body(ins, outs, scratch):
        total = scratch[0]
        total[...] = (ins[0][...] + ins[1][...]) + (ins[2][...] + ins[3][...])
        outs[0][...] = total[:5, :]
        outs[1][:upper, :] = total[9 : 9 + upper, :columns]
        outs[1][upper:, :] = total[9 : 9 + taps - upper, columns:]
        outs[2][0:1, :] = total[8:9, :columns]
        outs[2][1:2, :] = total[8:9, columns:]

    return on_chip(
        body,
        "unpack_small",
        parts,
        (((5, width), F32), ((taps, columns), F32), ((2, columns), F32)),
        scratch=(pltpu.VMEM(parts[0].shape, F32),),
        flops=1_000,
    )


PAD = 16


def pad_rows(padded, rows, columns, value):
    padded[:PAD, :] = jnp.zeros((PAD, columns), F32)
    padded[PAD + rows :, :] = jnp.zeros((PAD, columns), F32)
    padded[PAD : PAD + rows, :] = value


def conv_forward(kept, own, other, gains, weights, depth_kernel):
    rows, width = own.shape
    taps, columns = depth_kernel.shape
    half_taps = (taps - 1) // 2

    def body(ins, outs, scratch):
        kept_ref, own_ref, other_ref, gain_ref, weight_ref, tap_ref = ins
        conv_ref, sums_ref = outs
        padded = scratch[0]
        after = kept_residual(kept_ref, width) + both_parts(own_ref, other_ref)
        conv_ref[:, :width] = after
        entries = entries_of(after, gain_ref[2:3, :])
        joined = matmul(entries, weight_ref[:, 5 * columns : 7 * columns])
        value = joined[:, :columns]
        gate = jax.nn.sigmoid(joined[:, columns:])
        conv_ref[:, width : width + columns] = value
        conv_ref[:, width + columns : width + 2 * columns] = gate
        pad_rows(padded, rows, columns, value * gate)
        total = jnp.zeros((rows, columns), F32)
        for tap in range(taps):
            start = PAD - half_taps + tap
            total = total + tap_ref[tap : tap + 1, :] * padded[start : start + rows, :]
        conv_ref[:, width + 2 * columns :] = total
        sums_ref[0:1, :] = jnp.sum(total, 0, keepdims=True)
        sums_ref[1:2, :] = jnp.sum(total * total, 0, keepdims=True)

    return on_chip(
        body,
        "conv_forward",
        (kept, own, other, gains, weights, depth_kernel),
        (((rows, width + 3 * columns), F32), ((2, columns), F32)),
        scratch=(pltpu.VMEM((rows + 2 * PAD, columns), F32),),
    )


def batch_norm(conv_ref, sums_ref, batch_ref, token_count):
    columns = sums_ref.shape[1]
    column_mean = sums_ref[0:1, :] / token_count
    inverse = lax.rsqrt(sums_ref[1:2, :] / token_count - column_mean * column_mean + EPSILON)
    standard = (conv_ref[:, conv_ref.shape[1] - columns :] - column_mean) * inverse
    return standard, inverse, standard * batch_ref[0:1, :] + batch_ref[1:2, :]


def norm_forward(conv_kept, sums, batch, weights, token_count):
    rows = conv_kept.shape[0]
    columns = sums.shape[1]
    width = weights.shape[0]

    def body(ins, outs, _):
        conv_ref, sums_ref, batch_ref, weight_ref = ins
        _, _, shifted = batch_norm(conv_ref, sums_ref, batch_ref, token_count)
        activated = (shifted * jax.nn.sigmoid(shifted)).astype(BF16)
        outs[0][...] = right_transposed(activated, weight_ref[:, 7 * columns :]).astype(BF16)

    return on_chip(
        body, "norm_forward", (conv_kept, sums, batch, weights), (((rows, width), BF16),)
    )[0]


def norm_backward(gradient, own, other, kept, gains, weights, conv_kept, sums, batch, count):
    rows, width = gradient.shape
    columns = sums.shape[1]

    def body(ins, outs, _):
        grad_ref, own_ref, other_ref, x_ref, gain_ref, weight_ref, conv_ref, sums_ref, batch_ref = (
            ins
        )
        grads_ref, grad_sums_ref, gain_grad_ref = outs
        normed, factor = norm_parts(x_ref[:, :width])
        passed, gain_grad = norm_back(
            both_parts(own_ref, other_ref), normed, factor, gain_ref[3:4, :]
        )
        gain_grad_ref[...] = 0.5 * gain_grad
        total = grad_ref[...] + passed
        grads_ref[:, :width] = total
        standard, _, shifted = batch_norm(conv_ref, sums_ref, batch_ref, count)
        grad_shifted = matmul(
            total.astype(BF16), weight_ref[:, 7 * columns :]
        ) * swish_slope(shifted, jax.nn.sigmoid(shifted))
        grads_ref[:, width:] = grad_shifted
        grad_sums_ref[0:1, :] = jnp.sum(grad_shifted, 0, keepdims=True)
        grad_sums_ref[1:2, :] = jnp.sum(grad_shifted * standard, 0, keepdims=True)

    return on_chip(
        body,
        "norm_backward",
        (gradient, own, other, kept, gains, weights, conv_kept, sums, batch),
        (((rows, width + columns), F32), ((2, columns), F32), ((1, width), F32)),
    )


def conv_backward(norm_grads, grad_sums, conv_kept, sums, batch, weights, depth_kernel, count):
    rows = conv_kept.shape[0]
    columns = sums.shape[1]
    width = weights.shape[0]
    taps = depth_kernel.shape[0]
    half_taps = (taps - 1) // 2

    def body(ins, outs, scratch):
        grads_ref, grad_sums_ref, conv_ref, sums_ref, batch_ref, weight_ref, tap_ref = ins
        grad_conv_ref, joined_ref, part_ref = outs
        padded = scratch[0]
        standard, inverse, _ = batch_norm(conv_ref, sums_ref, batch_ref, count)
        grad_conv = (inverse * batch_ref[0:1, :]) * (
            grads_ref[:, width:]
            - grad_sums_ref[0:1, :] / count
            - standard * (grad_sums_ref[1:2, :] / count)
        )
        grad_conv_ref[...] = grad_conv
        pad_rows(padded, rows, columns, grad_conv)
        total = jnp.zeros((rows, columns), F32)
        for tap in range(taps):
            start = PAD + half_taps - tap
            total = total + tap_ref[tap : tap + 1, :] * padded[start : start + rows, :]
        gate_sigma = conv_ref[:, width + columns : width + 2 * columns]
        grad_value = total * gate_sigma
        grad_gate = grad_value * conv_ref[:, width : width + columns] * (1.0 - gate_sigma)
        joined = jnp.concatenate([grad_value, grad_gate], 1).astype(BF16)
        joined_ref[...] = joined
        part_ref[...] = right_transposed(
            joined, weight_ref[:, 5 * columns : 7 * columns]
        ).astype(BF16)

    return on_chip(
        body,
        "conv_backward",
        (norm_grads, grad_sums, conv_kept, sums, batch, weights, depth_kernel),
        (((rows, columns), F32), ((rows, 2 * columns), BF16), ((rows, width), BF16)),
        scratch=(pltpu.VMEM((rows + 2 * PAD, columns), F32),),
    )


def conv_weight_grads(norm_grads, grad_conv, joined, conv_kept, sums, batch, gains, taps, count):
    rows, columns = grad_conv.shape
    width = gains.shape[1]
    half_taps = (taps - 1) // 2

    def body(ins, outs, scratch):
        grads_ref, grad_ref, joined_ref, conv_ref, sums_ref, batch_ref, gain_ref = ins
        padded = scratch[0]
        entries = entries_of(conv_ref[:, :width], gain_ref[2:3, :])
        outs[0][:, : 2 * columns] = left_transposed(entries, joined_ref[...]).astype(BF16)
        _, _, shifted = batch_norm(conv_ref, sums_ref, batch_ref, count)
        activated = (shifted * jax.nn.sigmoid(shifted)).astype(BF16)
        outs[0][:, 2 * columns :] = left_transposed(
            grads_ref[:, :width].astype(BF16), activated
        ).astype(BF16)
        value = conv_ref[:, width : width + columns]
        gate = conv_ref[:, width + columns : width + 2 * columns]
        pad_rows(padded, rows, columns, value * gate)
        grad_conv_value = grad_ref[...]
        for tap in range(taps):
            start = PAD - half_taps + tap
            outs[1][tap : tap + 1, :] = jnp.sum(
                padded[start : start + rows, :] * grad_conv_value, 0, keepdims=True
            )

    return on_chip(
        body,
        "conv_weight_grads",
        (norm_grads, grad_conv, joined, conv_kept, sums, batch, gains),
        (((width, 3 * columns), BF16), ((taps, columns), F32)),
        scratch=(pltpu.VMEM((rows + 2 * PAD, columns), F32),),
    )


def first_back(gradient, own, other, kept, pre, gains, weights):
    rows, width = gradient.shape
    hidden = weights.shape[1] // 2

    def body(ins, outs, _):
        grad_ref, own_ref, other_ref, kept_ref, pre_ref, gain_ref, weight_ref = ins
        grads_ref, keep_ref, send_ref, gain_grad_ref = outs
        normed, factor = norm_parts(kept_residual(kept_ref, width))
        passed, gain_grad = norm_back(
            both_parts(own_ref, other_ref), normed, factor, gain_ref[1:2, :]
        )
        gain_grad_ref[...] = 0.5 * gain_grad
        total = grad_ref[...] + passed
        keep_ref[:, :width] = own_half(total)
        part = ff_back_body(total, pre_ref[...], weight_ref, grads_ref)
        keep_ref[:, width:] = own_half(part)
        send_ref[...] = other_half(part).astype(BF16)

    return on_chip(
        body,
        "first_back",
        (gradient, own, other, kept, pre, gains, weights),
        (
            ((rows, width + 2 * hidden), BF16),
            ((rows // 2, 2 * width), F32),
            ((rows // 2, width), BF16),
            ((1, width), F32),
        ),
    )


def input_back(keep, other, tokens, gains, gain_grads, tap_grads, bias_grads):
    rows, width = tokens.shape
    taps, columns = tap_grads.shape
    upper = (taps + 1) // 2
    packed_rows = 8 + -(-(1 + upper) // 8) * 8

    def body(ins, outs, _):
        keep_ref, other_ref, x_ref, gain_ref = ins[:4]
        tap_ref, bias_ref = ins[8:]
        packed = outs[1]
        normed, factor = norm_parts(x_ref[...].astype(F32))
        passed, gain_grad = norm_back(
            keep_ref[:, width:] + other_ref[...].astype(F32), normed, factor, gain_ref[0:1, :]
        )
        outs[0][...] = keep_ref[:, :width] + passed
        packed[...] = jnp.zeros((packed_rows, 2 * columns), F32)
        packed[0:1, :] = gain_grad
        for place in range(4):
            packed[place + 1 : place + 2, :] = ins[4 + place][...]
        packed[8:9, :columns] = bias_ref[0:1, :]
        packed[8:9, columns:] = bias_ref[1:2, :]
        packed[9 : 9 + upper, :columns] = tap_ref[:upper, :]
        packed[9 : 9 + taps - upper, columns:] = tap_ref[upper:, :]

    return on_chip(
        body,
        "input_back",
        (keep, other, tokens, gains) + tuple(gain_grads) + (tap_grads, bias_grads),
        (((rows, width), F32), ((packed_rows, 2 * columns), F32)),
        flops=1_000_000,
    )


def reduce_plain(grads):
    return lax.psum_scatter(grads.astype(BF16), "dp", scatter_dimension=0, tiled=True).astype(F32)


def stacked_columns(pieces, count):
    width = pieces.shape[1] // count
    return jnp.stack([pieces[:, index * width : (index + 1) * width] for index in range(count)])


def unstacked(stacked):
    return [stacked[index] for index in range(stacked.shape[0])]


def body(
    tokens,
    norm_gains,
    first_in,
    first_out,
    attention_in,
    attention_out,
    head_biases,
    gated_in,
    pointwise_out,
    depth_kernel,
    batch_scale,
    batch_shift,
    second_in,
    second_out,
    cotangent,
):
    local_heads = HEAD_TOTAL // lax.axis_size("tensor")
    length = tokens.shape[0] * lax.axis_size("tensor")
    token_count = float(length * lax.axis_size("dp"))
    columns = attention_out.shape[1]
    hidden = first_in.shape[1]
    width = tokens.shape[1]
    table = sinusoid(length, width).astype(BF16)
    batch = jnp.stack([batch_scale, batch_shift])
    split = doubling()

    def gather(pieces):
        return lax.all_gather(jnp.concatenate(pieces, 1), "dp", axis=0, tiled=True)

    tokens_all = both_halves(tokens)
    cotangent_all = both_halves(cotangent)

    if split:
        batch_one = (first_in, first_out)
        joint_two = jnp.concatenate(
            [
                attention_in.reshape(-1, columns),
                attention_out,
                gated_in.reshape(-1, columns),
                pointwise_out,
            ],
            0,
        )
        batch_two = (joint_two[: joint_two.shape[0] // 2], joint_two[joint_two.shape[0] // 2 :])
        batch_three = (second_in, second_out)
        joint_three = jnp.concatenate(batch_three, 0)
        arrived_one = gather_send(batch_one, 0)
        batch_one = on_chip(
            lambda ins, outs, _: (
                outs[0].__setitem__(..., ins[0][...]),
                outs[1].__setitem__(..., ins[1][...]),
            ),
            "first_copy",
            batch_one,
            tuple((value.shape, value.dtype) for value in batch_one),
            flops=1_000,
        )
        arrived_one = tie(arrived_one, (batch_one, table))
        arrived_two = gather_send((tie(joint_two, arrived_one),), 0)
        batch_one = gather_join(tuple(batch_one), tuple(arrived_one))
        arrived_one = gather_send(batch_one, 1)
        batch_one = gather_join(batch_one, tie(arrived_one, tokens_all))
        arrived_one = gather_send(batch_one, 2)
        batch_two = gather_join(batch_two, tie(arrived_two, batch_one))
        arrived_two = gather_send(batch_two, 1)
        batch_one = gather_join(
            batch_one, tie(arrived_one, (batch_two, cotangent_all)), joint=True
        )
        arrived_three = gather_send((tie(joint_three, batch_one),), 0)
        batch_one += (shift(batch_one[0], "dp", 1),)
    else:
        batch_one = gather([first_in, first_out])
        mixed_weights = gather(
            unstacked(attention_in) + [attention_out] + unstacked(gated_in) + [pointwise_out]
        )
        positions = position_forward(table, mixed_weights, columns)
        second_weights = gather([second_in, second_out])

    pre1, part1, first_weights = first_forward(tokens_all, norm_gains, batch_one)
    other1 = swap(part1)
    if split:
        batch_two = gather_join(batch_two, tie(arrived_two, part1))
        arrived_two = gather_send(batch_two, 2)
        batch_three = gather_join(batch_three, tie(arrived_three, batch_two))
        arrived_three = gather_send(batch_three, 1)
        batch_two = gather_join(batch_two, tie(arrived_two, (other1, batch_three)), joint=True)
        batch_two += (shift(batch_two[0], "dp", 1),)
        mixed_weights, positions = mixed_assemble(batch_two, table, width)
    kept, part2 = attention_forward(
        tokens_all, part1, other1, norm_gains, mixed_weights, positions, head_biases, local_heads
    )
    other2 = swap(part2)
    if split:
        batch_three = gather_join(batch_three, tie(arrived_three, part2))
        arrived_three = gather_send(batch_three, 2)
    conv_kept, sums = conv_forward(
        kept, part2, other2, norm_gains, mixed_weights, depth_kernel
    )
    if split:
        batch_three = gather_join(batch_three, tie(arrived_three, sums), joint=True)
        batch_three += (shift(batch_three[0], "dp", 1),)
        second_weights = second_assemble(batch_three, width)
    sums = sum_over(sums, "dp")
    part3 = norm_forward(conv_kept, sums, batch, mixed_weights, token_count)
    other3 = swap(part3)
    other3 = tie(other3, second_weights)
    second_kept, part4 = second_forward(conv_kept, part3, other3, norm_gains, second_weights)
    other4 = swap(part4)
    block_out, grad4, second_rows, part5, gain5 = second_back(
        second_kept, part4, other4, cotangent_all, norm_gains, second_weights
    )
    other5 = swap(part5)
    second_name = "second_weight_grads"
    if split:
        keeps, sends = ff_weight_split(second_rows, second_kept, norm_gains, 3, second_name)
        second_keeps, sends = scatter_add(keeps, scatter_send(sends, 0), 0, "second_sum")
        second_arrived = scatter_send(sends, 1)
        other5 = tie(other5, second_keeps)
    else:
        second_grads = reduce_plain(
            ff_weight_grads(second_rows, second_kept, norm_gains, 3, second_name)
        )
        second_reduced = (second_grads[:, :hidden], second_grads[:, hidden:])
    norm_grads, grad_sums, gain4 = norm_backward(
        grad4,
        part5,
        other5,
        second_kept,
        norm_gains,
        mixed_weights,
        conv_kept,
        sums,
        batch,
        token_count,
    )
    grad_sums = sum_over(grad_sums, "dp")
    if split:
        second_keeps, sends = scatter_add(second_keeps, second_arrived, 1, "second_sum")
        grad_sums = tie(grad_sums, second_keeps)
    grad_conv, joined3, part6 = conv_backward(
        norm_grads, grad_sums, conv_kept, sums, batch, mixed_weights, depth_kernel, token_count
    )
    other6 = swap(part6)
    conv_grads, tap_grads = conv_weight_grads(
        norm_grads,
        grad_conv,
        joined3,
        conv_kept,
        sums,
        batch,
        norm_gains,
        depth_kernel.shape[0],
        token_count,
    )
    other6 = tie(other6, conv_grads)
    if split:
        second_arrived = scatter_send(tie(sends, part6), 2)
        second_arrived = tie(second_arrived, conv_grads)
        second_keeps, sends = scatter_add(second_keeps, second_arrived, 2, "second_sum")
        second_arrived = scatter_send(sends, 3)
        other6 = tie(other6, second_keeps)
    grad2, joined2, table_grad, part7, gain3, bias_grads = attention_back(
        norm_grads,
        part6,
        other6,
        conv_kept,
        norm_gains,
        mixed_weights,
        positions,
        kept,
        local_heads,
    )
    other7 = swap(part7)
    mixed_grads = mixed_weight_grads(
        joined2, table, table_grad, grad2, kept, norm_gains, conv_grads, split
    )
    if split:
        keeps, sends = mixed_grads
        mixed_keeps, sends = scatter_add(keeps, scatter_send(sends, 0), 0, "mixed_sum")
        mixed_arrived = scatter_send(sends, 1)
        other7 = tie(other7, mixed_keeps)
    first_rows, keep8, send8, gain2 = first_back(
        grad2, part7, other7, kept, pre1, norm_gains, first_weights
    )
    other8 = swap(send8)
    small = ((gain2, gain3, gain4, gain5), tap_grads, bias_grads)
    if split:
        mixed_keeps, sends = scatter_add(mixed_keeps, mixed_arrived, 1, "mixed_sum")
        mixed_arrived = scatter_send(sends, 2)
        keeps, sends = ff_weight_split(
            tie(first_rows, mixed_keeps), tokens_all, norm_gains, 0, "first_weight_grads"
        )
        first_arrived = scatter_send(sends, 0)
        first_keeps, sends = scatter_add(keeps, first_arrived, 0, "first_sum")
        first_arrived = scatter_send(sends, 1)
        second_reduced, _ = scatter_add(
            second_keeps, tie(second_arrived, first_keeps), 3, "second_sum"
        )
        mixed_keeps, sends = scatter_add(
            mixed_keeps, tie(mixed_arrived, first_keeps), 2, "mixed_sum"
        )
        mixed_arrived = scatter_send(sends, 3)
        other8 = tie(other8, mixed_keeps)
        grad_start, packed = input_back(keep8, other8, tokens, norm_gains, *small)
        first_arrived = tie(first_arrived, packed)
        first_keeps, sends = scatter_add(first_keeps, first_arrived, 1, "first_sum")
        first_arrived = scatter_send(sends, 2)
        packed = jnp.concatenate([sum_over(packed[:8], "tensor"), packed[8:]], 0)
        packed = sum_over(tie(packed, first_keeps), "dp", 1, 4)
        reduced_attention, reduced_mixing, reduced_gated, reduced_pointwise = mixed_finish(
            mixed_keeps, tie(mixed_arrived, first_keeps)
        )
        first_arrived = tie(first_arrived, (reduced_mixing, packed))
        first_keeps, sends = scatter_add(first_keeps, first_arrived, 2, "first_sum")
        first_arrived = scatter_send(sends, 3)
        packed = tie(packed, first_keeps)
        parts = (packed,) + tuple(shift(packed, "dp", mask) for mask in (4, 8, 12))
        (reduced_in, reduced_out), _ = scatter_add(first_keeps, first_arrived, 3, "first_sum")
    else:
        grad_start, packed = input_back(keep8, other8, tokens, norm_gains, *small)
        first_grads = reduce_plain(
            ff_weight_grads(first_rows, tokens_all, norm_gains, 0, "first_weight_grads")
        )
        reduced_in, reduced_out = first_grads[:, :hidden], first_grads[:, hidden:]
        mixed = reduce_plain(mixed_grads)
        reduced_attention = stacked_columns(mixed[:, : 4 * columns], 4)
        reduced_mixing = mixed[:, 4 * columns : 5 * columns]
        reduced_gated = stacked_columns(mixed[:, 5 * columns : 7 * columns], 2)
        reduced_pointwise = mixed[:, 7 * columns :]
        packed = jnp.concatenate([sum_over(packed[:8], "tensor"), packed[8:]], 0)
        packed = sum_over(packed, "dp")
        parts = (packed,) + (jnp.zeros_like(packed),) * 3
    gain_total, tap_total, bias_total = unpack_small(parts, depth_kernel.shape[0], columns)
    return (
        block_out,
        grad_start,
        gain_total,
        reduced_in,
        reduced_out,
        reduced_attention,
        reduced_mixing,
        bias_total,
        reduced_gated,
        reduced_pointwise,
        tap_total,
        grad_sums[1],
        grad_sums[0],
        *second_reduced,
    )


def solution(mesh):
    placed = (
        P(("dp", "tensor"), None),
        P(),
        P("dp", "tensor"),
        P("dp", "tensor"),
        P(None, "dp", "tensor"),
        P("dp", "tensor"),
        P(None, "tensor"),
        P(None, "dp", "tensor"),
        P("dp", "tensor"),
        P(None, "tensor"),
        P("tensor"),
        P("tensor"),
        P("dp", "tensor"),
        P("dp", "tensor"),
        P(("dp", "tensor"), None),
    )
    return jax.shard_map(
        body,
        mesh=mesh,
        in_specs=placed,
        out_specs=(
            P(("dp", "tensor"), None),
            P(("dp", "tensor"), None),
            P(),
            P("dp", "tensor"),
            P("dp", "tensor"),
            P(None, "dp", "tensor"),
            P("dp", "tensor"),
            P(None, "tensor"),
            P(None, "dp", "tensor"),
            P("dp", "tensor"),
            P(None, "tensor"),
            P("tensor"),
            P("tensor"),
            P("dp", "tensor"),
            P("dp", "tensor"),
        ),
        check_vma=False,
    )
```

```python
import math

import jax
import jax.numpy as jnp
from jax import lax
from jax.experimental import pallas as pl
from jax.experimental.pallas import tpu as pltpu
from jax.sharding import PartitionSpec as P

HEAD_TOTAL = 8
EPSILON = 1e-05
BF16 = jnp.bfloat16
F32 = jnp.float32


def matmul(left_side, right_side):
    return jnp.dot(left_side, right_side, preferred_element_type=F32)


def right_transposed(left_side, right_side):
    return lax.dot_general(
        left_side, right_side, (((1,), (1,)), ((), ())), preferred_element_type=F32
    )


def left_transposed(left_side, right_side):
    return lax.dot_general(
        left_side, right_side, (((0,), (0,)), ((), ())), preferred_element_type=F32
    )


def swish_slope(pre_value, gate_sigma):
    return gate_sigma * (1.0 + pre_value * (1.0 - gate_sigma))


def norm_parts(residual):
    centred = residual - jnp.mean(residual, -1, keepdims=True)
    factor = lax.rsqrt(jnp.mean(centred * centred, -1, keepdims=True) + EPSILON)
    return centred * factor, factor


def norm_back(gradient, normed, factor, norm_gain):
    scaled = gradient * norm_gain
    inner_sum = (
        scaled
        - jnp.mean(scaled, -1, keepdims=True)
        - normed * jnp.mean(scaled * normed, -1, keepdims=True)
    )
    return factor * inner_sum, jnp.sum(gradient * normed, 0, keepdims=True)


def sinusoid(length, features):
    offsets = jnp.arange(2 * length, dtype=F32) - (length - 1)
    half_width = features // 2
    frequency = jnp.exp(jnp.arange(half_width, dtype=F32) * (-math.log(10000.0) / half_width))
    angles = offsets[:, None] * frequency[None, :]
    table = jnp.concatenate([jnp.sin(angles), jnp.cos(angles)], 1)
    return jnp.where(offsets[:, None] < length, table, 0.0)


def on_chip(function, name, operands, results, scratch=(), flops=300_000_000):
    count = len(operands)
    total = count + len(results)

    def kernel(*refs):
        function(refs[:count], refs[count:total], refs[total:])

    moved = sum(value.size * value.dtype.itemsize for value in operands)
    moved += sum(math.prod(shape) * jnp.dtype(kind).itemsize for shape, kind in results)
    return pl.pallas_call(
        kernel,
        out_shape=[jax.ShapeDtypeStruct(shape, kind) for shape, kind in results],
        in_specs=[pl.BlockSpec(memory_space=pltpu.VMEM)] * count,
        out_specs=[pl.BlockSpec(memory_space=pltpu.VMEM)] * len(results),
        scratch_shapes=list(scratch),
        compiler_params=pltpu.CompilerParams(vmem_limit_bytes=24 * 1024 * 1024),
        cost_estimate=pl.CostEstimate(flops=flops, bytes_accessed=moved, transcendentals=0),
        name=name,
    )(*operands)


def swap(value):
    return lax.ppermute(value, "tensor", [(0, 1), (1, 0)])


def both_halves(own):
    other = swap(own)
    first = lax.axis_index("tensor") == 0
    return jnp.concatenate([jnp.where(first, own, other), jnp.where(first, other, own)], 0)


def own_half(value):
    half = value.shape[0] // 2
    return jnp.where(lax.axis_index("tensor") == 0, value[:half], value[half:])


def shift(value, axis, mask):
    return lax.ppermute(value, axis, [(k, k ^ mask) for k in range(lax.axis_size(axis))])


def sum_over(value, axis, step=1, stop=None):
    size = lax.axis_size(axis)
    if size & (size - 1):
        return lax.psum(value, axis)
    stop = stop or size
    while step < stop:
        if step * 4 <= stop:
            near, far, both = (shift(value, axis, step * times) for times in (1, 2, 3))
            value = (value + near) + (far + both)
            step *= 4
        else:
            value = value + shift(value, axis, step)
            step *= 2
    return value


GATHER_ORDERS = ((8, 4, 2, 1), (8, 2, 4, 1))
SCATTER_ORDERS = ((1, 2, 4, 8), (1, 4, 2, 8))


def doubling():
    return lax.axis_size("dp") == 16


def distances(order):
    blocks = [0]
    for mask in order:
        blocks = blocks + [block ^ mask for block in blocks]
    return blocks


def halving(order):
    return distances(order[::-1])


def gather_send(values, stage):
    return tuple(shift(value, "dp", order[stage]) for value, order in zip(values, GATHER_ORDERS))


def gather_join(pair, arrived, joint=False):
    sizes = [value.shape[0] for value in pair]

    def body(ins, outs, _):
        for group in range(2):
            rows = sizes[group]
            target, start = (outs[0], 2 * rows * group) if joint else (outs[group], 0)
            source, begin = (ins[2], rows * group) if len(arrived) == 1 else (ins[2 + group], 0)
            target[start : start + rows, :] = ins[group][...]
            target[start + rows : start + 2 * rows, :] = source[begin : begin + rows, :]

    columns, kind = pair[0].shape[1], pair[0].dtype
    if joint:
        results = (((2 * sum(sizes), columns), kind),)
    else:
        results = tuple(((2 * rows, columns), kind) for rows in sizes)
    return tuple(on_chip(body, "gather_join", tuple(pair) + arrived, results, flops=1_000))


def tie(values, *others):
    return lax.optimization_barrier((values, others))[0]


def assemble(ref, target_ref, group, half, matrices, first_column):
    device = lax.axis_index("dp")
    blocks = distances(GATHER_ORDERS[group])
    count = len(blocks) // 2
    rows = target_ref.shape[0] // len(blocks)
    columns = ref.shape[1]
    for place in range(count):
        owner = device ^ blocks[half * count + place]
        target = pl.ds(pl.multiple_of(owner * rows, rows), rows)
        for matrix in range(matrices):
            start = ((group * count + place) * matrices + matrix) * rows
            left = first_column + matrix * columns
            target_ref[target, left : left + columns] = ref[start : start + rows, :]


def scatter_split(total_ref, keep_ref, send_ref, group, matrices):
    device = lax.axis_index("dp")
    blocks = halving(SCATTER_ORDERS[group])
    count = len(blocks) // 2
    rows = total_ref.shape[0] // len(blocks)
    columns = keep_ref.shape[1]
    first = group * keep_ref.shape[0]
    for place, block in enumerate(blocks):
        source = pl.ds(pl.multiple_of((device ^ block) * rows, rows), rows)
        for matrix in range(matrices):
            piece = total_ref[source, matrix * columns : (matrix + 1) * columns]
            start = ((place % count) * matrices + matrix) * rows
            if place < count:
                keep_ref[start : start + rows, :] = piece
            else:
                send_ref[first + start : first + start + rows, :] = piece.astype(BF16)


def scatter_send(sends, stage):
    return tuple(shift(send, "dp", order[stage]) for send, order in zip(sends, SCATTER_ORDERS))


def arrived_part(refs, group, rows):
    if len(refs) == 1:
        return refs[0][group * rows : (group + 1) * rows, :].astype(F32)
    return refs[group][...].astype(F32)


def scatter_add(keeps, arrived, stage, name):
    rows, columns = keeps[0].shape
    half = rows // 2
    last = stage == len(SCATTER_ORDERS[0]) - 1
    joint = stage == len(SCATTER_ORDERS[0]) - 2
    results = (((rows if last else half, columns), F32),) * 2
    if not last:
        results += (((rows, columns), BF16),) if joint else (((half, columns), BF16),) * 2

    def body(ins, outs, _):
        for group in range(2):
            total = ins[group][...] + arrived_part(ins[2:], group, rows)
            if last:
                outs[group][...] = total
                continue
            outs[group][...] = total[:half]
            if joint:
                outs[2][group * half : (group + 1) * half, :] = total[half:].astype(BF16)
            else:
                outs[2 + group][...] = total[half:].astype(BF16)

    values = on_chip(body, name, tuple(keeps) + tuple(arrived), results, flops=1_000)
    return values[:2], values[2:]


def entries_of(residual, gain):
    return (norm_parts(residual)[0] * gain).astype(BF16)


def ff_forward_body(entries, weight_ref, part_ref):
    half = weight_ref.shape[1] // 2
    pre = matmul(entries, weight_ref[:, :half])
    hidden = (pre * jax.nn.sigmoid(pre)).astype(BF16)
    part_ref[...] = right_transposed(hidden, weight_ref[:, half:]).astype(BF16)
    return pre


def both_parts(own_ref, other_ref):
    return own_ref[...].astype(F32) + other_ref[...].astype(F32)


def first_forward(tokens, gains, weights):
    rows, width = tokens.shape
    split = isinstance(weights, tuple)
    pieces = weights if split else (weights,)
    hidden = pieces[0].shape[1] if split else weights.shape[1] // 2

    def body(ins, outs, _):
        weight_ref = ins[2]
        if split:
            weight_ref = outs[2]
            for group in range(2):
                for half in range(2):
                    assemble(ins[2 + half], weight_ref, group, half, 1, group * hidden)
        entries = entries_of(ins[0][...].astype(F32), ins[1][0:1, :])
        outs[0][...] = ff_forward_body(entries, weight_ref, outs[1])

    results = (((rows, hidden), F32), ((rows, width), BF16))
    if split:
        results += (((width, 2 * hidden), BF16),)
    values = on_chip(body, "first_forward", (tokens, gains) + pieces, results)
    return values if split else tuple(values) + (weights,)


def second_forward(conv_kept, own, other, gains, weights):
    rows, width = own.shape
    hidden = weights.shape[1] // 2

    def body(ins, outs, _):
        kept_ref, part_ref = outs
        after = ins[0][:, :width] + both_parts(ins[1], ins[2])
        kept_ref[:, :width] = after
        kept_ref[:, width:] = ff_forward_body(
            entries_of(after, ins[3][3:4, :]), ins[4], part_ref
        )

    return on_chip(
        body,
        "second_forward",
        (conv_kept, own, other, gains, weights),
        (((rows, width + hidden), F32), ((rows, width), BF16)),
    )


def ff_back_body(gradient, pre, weight_ref, grads_ref):
    width = gradient.shape[1]
    half = weight_ref.shape[1] // 2
    branch = (0.5 * gradient).astype(BF16)
    grads_ref[:, :width] = branch
    grad_hidden = matmul(branch, weight_ref[:, half:])
    sigma = jax.nn.sigmoid(pre)
    grad_pre = (grad_hidden * swish_slope(pre, sigma)).astype(BF16)
    grads_ref[:, width : width + half] = grad_pre
    grads_ref[:, width + half : width + 2 * half] = (pre * sigma).astype(BF16)
    return right_transposed(grad_pre, weight_ref[:, :half])


def second_back(kept, own, other, cotangent, gains, weights):
    rows, width = own.shape
    hidden = weights.shape[1] // 2

    def body(ins, outs, _):
        kept_ref, own_ref, other_ref, cot_ref, gain_ref, weight_ref = ins
        out_ref, grad_ref, grads_ref, part_ref, gain_grad_ref = outs
        after = kept_ref[:, :width] + 0.5 * both_parts(own_ref, other_ref)
        normed, factor = norm_parts(after)
        gain = gain_ref[4:5, :]
        out_ref[...] = own_half(normed * gain).astype(BF16)
        gradient, gain_grad = norm_back(cot_ref[...].astype(F32), normed, factor, gain)
        gain_grad_ref[...] = gain_grad
        grad_ref[...] = gradient
        part_ref[...] = ff_back_body(
            gradient, kept_ref[:, width:], weight_ref, grads_ref
        ).astype(BF16)

    return on_chip(
        body,
        "second_back",
        (kept, own, other, cotangent, gains, weights),
        (
            ((rows // 2, width), BF16),
            ((rows, width), F32),
            ((rows, width + 2 * hidden), BF16),
            ((rows, width), BF16),
            ((1, width), F32),
        ),
    )


def ff_weight_grads(grads, residual, gains, row, name):
    width = gains.shape[1]
    half = (grads.shape[1] - width) // 2

    def body(ins, outs, _):
        grads_ref, x_ref, gain_ref = ins
        entries = entries_of(x_ref[:, :width].astype(F32), gain_ref[row : row + 1, :])
        outs[0][:, :half] = left_transposed(entries, grads_ref[:, width : width + half]).astype(
            BF16
        )
        outs[0][:, half:] = left_transposed(
            grads_ref[:, :width], grads_ref[:, width + half :]
        ).astype(BF16)

    return on_chip(body, name, (grads, residual, gains), (((width, 2 * half), BF16),))[0]


def ff_weight_split(grads, residual, gains, row, name):
    width = gains.shape[1]
    half = (grads.shape[1] - width) // 2

    def body(ins, outs, scratch):
        grads_ref, x_ref, gain_ref = ins
        entries = entries_of(x_ref[:, :width].astype(F32), gain_ref[row : row + 1, :])
        scratch[0][...] = left_transposed(entries, grads_ref[:, width : width + half])
        scatter_split(scratch[0], outs[0], outs[2], 0, 1)
        scratch[0][...] = left_transposed(grads_ref[:, :width], grads_ref[:, width + half :])
        scatter_split(scratch[0], outs[1], outs[2], 1, 1)

    values = on_chip(
        body,
        name,
        (grads, residual, gains),
        (((width // 2, half), F32),) * 2 + (((width, half), BF16),),
        scratch=(pltpu.VMEM((width, half), F32),),
    )
    return values[:2], values[2:]


def kept_residual(kept_ref, width):
    return kept_ref[:, :width].astype(F32) + kept_ref[:, width : 2 * width].astype(F32)


def position_forward(table, weights, columns):
    def body(ins, outs, _):
        outs[0][...] = matmul(ins[0][...], ins[1][:, 3 * columns : 4 * columns]).astype(BF16)

    return on_chip(
        body, "position_forward", (table, weights), (((table.shape[0], columns), BF16),)
    )[0]


def attention_forward(tokens, own, other, gains, weights, positions, biases, heads):
    rows, width = tokens.shape
    columns = biases.shape[1]
    features = columns // heads
    scale = features ** (-0.5)
    start = 2 * width

    def body(ins, outs, _):
        x_ref, own_ref, other_ref, gain_ref, weight_ref, table_ref, bias_ref = ins
        kept_ref, part_ref = outs
        after = x_ref[...].astype(F32) + 0.5 * both_parts(own_ref, other_ref)
        high = after.astype(BF16)
        kept_ref[:, :width] = high
        kept_ref[:, width : 2 * width] = (after - high.astype(F32)).astype(BF16)
        entries = entries_of(after, gain_ref[1:2, :])
        joined = matmul(entries, weight_ref[:, : 3 * columns])
        queries = joined[:, :columns]
        content_q = (queries + bias_ref[0:1, :]).astype(BF16)
        position_q = (queries + bias_ref[1:2, :]).astype(BF16)
        keys = joined[:, columns : 2 * columns].astype(BF16)
        values = joined[:, 2 * columns :].astype(BF16)
        kept_ref[:, start : start + columns] = content_q
        kept_ref[:, start + columns : start + 2 * columns] = position_q
        kept_ref[:, start + 2 * columns : start + 3 * columns] = keys
        kept_ref[:, start + 3 * columns : start + 4 * columns] = values
        mixed = []
        for head in range(heads):
            part = slice(head * features, (head + 1) * features)
            content = right_transposed(content_q[:, part], keys[:, part])
            raw = right_transposed(position_q[:, part], table_ref[:, part])
            shifted = pltpu.roll(raw, rows + 1, 1, stride=1, stride_axis=0)[:, :rows]
            scores = (content + shifted) * scale
            lifted = jnp.exp(scores - jnp.max(scores, -1, keepdims=True))
            probability = (lifted / jnp.sum(lifted, -1, keepdims=True)).astype(BF16)
            place = start + 5 * columns + head * rows
            kept_ref[:, place : place + rows] = probability
            mixed.append(matmul(probability, values[:, part]))
        attended = jnp.concatenate(mixed, 1).astype(BF16)
        kept_ref[:, start + 4 * columns : start + 5 * columns] = attended
        part_ref[...] = right_transposed(
            attended, weight_ref[:, 4 * columns : 5 * columns]
        ).astype(BF16)

    return on_chip(
        body,
        "attention_forward",
        (tokens, own, other, gains, weights, positions, biases),
        (((rows, start + 5 * columns + heads * rows), BF16), ((rows, width), BF16)),
    )


def attention_back(norm_grads, own, other, conv_kept, gains, weights, positions, kept, heads):
    rows, width = own.shape
    columns = positions.shape[1]
    features = columns // heads
    scale = features ** (-0.5)
    start = 2 * width

    def body(ins, outs, _):
        grad_ref, own_ref, other_ref, x_ref, gain_ref, weight_ref, table_ref, kept_ref = ins
        total_ref, joined_ref, table_grad_ref, part_ref, gain_grad_ref, bias_ref = outs
        normed, factor = norm_parts(x_ref[:, :width])
        passed, gain_grad = norm_back(
            both_parts(own_ref, other_ref), normed, factor, gain_ref[2:3, :]
        )
        gain_grad_ref[...] = gain_grad
        total = grad_ref[:, :width] + passed
        total_ref[...] = total
        grad_mixed = matmul(
            total.astype(BF16), weight_ref[:, 4 * columns : 5 * columns]
        ).astype(BF16)
        line = lax.broadcasted_iota(jnp.int32, (rows, rows), 0)
        place = lax.broadcasted_iota(jnp.int32, (rows, rows), 1)
        flip = (line + place == rows - 1).astype(F32).astype(BF16)
        content_q = kept_ref[:, start : start + columns]
        flipped_q = matmul(flip, kept_ref[:, start + columns : start + 2 * columns]).astype(BF16)
        keys = kept_ref[:, start + 2 * columns : start + 3 * columns]
        values = kept_ref[:, start + 3 * columns : start + 4 * columns]
        zeros = jnp.zeros((rows, rows), F32)
        from_content, from_position, to_keys, to_values, to_table = [], [], [], [], []
        for head in range(heads):
            part = slice(head * features, (head + 1) * features)
            left = start + 5 * columns + head * rows
            rounded = kept_ref[:, left : left + rows]
            probability = rounded.astype(F32)
            grad_probability = right_transposed(grad_mixed[:, part], values[:, part])
            to_values.append(left_transposed(rounded, grad_mixed[:, part]))
            inner = jnp.sum(probability * grad_probability, -1, keepdims=True)
            grad_scores = (probability * (grad_probability - inner)).astype(BF16) * scale
            grad_scores = grad_scores.astype(BF16)
            from_content.append(matmul(grad_scores, keys[:, part]))
            to_keys.append(left_transposed(grad_scores, content_q[:, part]))
            flipped = jnp.concatenate([matmul(flip, grad_scores), zeros], 1)
            spread = pltpu.roll(flipped, 0, 1, stride=1, stride_axis=0).astype(BF16)
            from_position.append(matmul(spread, table_ref[:, part]))
            to_table.append(left_transposed(spread, flipped_q[:, part]))
        grad_content = jnp.concatenate(from_content, 1)
        grad_position = jnp.concatenate(from_position, 1)
        high = grad_position.astype(BF16)
        low = (grad_position - high.astype(F32)).astype(BF16)
        grad_position = matmul(flip, high) + matmul(flip, low)
        bias_ref[0:1, :] = jnp.sum(grad_content, 0, keepdims=True)
        bias_ref[1:2, :] = jnp.sum(grad_position, 0, keepdims=True)
        joined = jnp.concatenate(
            [grad_content + grad_position] + to_keys + to_values, 1
        ).astype(BF16)
        joined_ref[...] = joined
        table_grad_ref[...] = jnp.concatenate(to_table, 1).astype(BF16)
        part_ref[...] = right_transposed(joined, weight_ref[:, : 3 * columns]).astype(BF16)

    return on_chip(
        body,
        "attention_back",
        (norm_grads, own, other, conv_kept, gains, weights, positions, kept),
        (
            ((rows, width), F32),
            ((rows, 3 * columns), BF16),
            ((2 * rows, columns), BF16),
            ((rows, width), BF16),
            ((1, width), F32),
            ((2, columns), F32),
        ),
    )


def second_assemble(halves, width):
    columns = halves[0].shape[1]

    def body(ins, outs, _):
        for group in range(2):
            for half in range(2):
                assemble(ins[half], outs[0], group, half, 1, group * columns)

    return on_chip(
        body, "second_assemble", halves, (((width, 2 * columns), BF16),), flops=1_000
    )[0]


def mixed_assemble(halves, table, width):
    columns = halves[0].shape[1]

    def body(ins, outs, _):
        for group in range(2):
            for half in range(2):
                assemble(ins[half], outs[0], group, half, 4, 4 * group * columns)
        outs[1][...] = matmul(ins[2][...], outs[0][:, 3 * columns : 4 * columns]).astype(BF16)

    return on_chip(
        body,
        "mixed_assemble",
        halves + (table,),
        (((width, 8 * columns), BF16), ((table.shape[0], columns), BF16)),
    )


def mixed_weight_grads(joined, table, table_grad, total, kept, gains, conv_grads, split):
    width = gains.shape[1]
    columns = table_grad.shape[1]

    def whole(ins, target_ref):
        joined_ref, table_ref, table_grad_ref, total_ref, kept_ref, gain_ref, conv_ref = ins
        entries = entries_of(kept_residual(kept_ref, width), gain_ref[1:2, :])
        attended = kept_ref[:, 2 * width + 4 * columns : 2 * width + 5 * columns]
        target_ref[:, : 3 * columns] = left_transposed(entries, joined_ref[...])
        target_ref[:, 3 * columns : 4 * columns] = left_transposed(
            table_ref[...], table_grad_ref[...]
        )
        target_ref[:, 4 * columns : 5 * columns] = left_transposed(
            total_ref[...].astype(BF16), attended
        )
        target_ref[:, 5 * columns :] = conv_ref[...].astype(F32)

    def body(ins, outs, scratch):
        if not split:
            whole(ins, outs[0])
            return
        whole(ins, scratch[0])
        for group in range(2):
            part = scratch[0].at[:, 4 * group * columns : 4 * (group + 1) * columns]
            scatter_split(part, outs[group], outs[2], group, 4)

    operands = (joined, table, table_grad, total, kept, gains, conv_grads)
    if not split:
        results = (((width, 8 * columns), F32),)
        return on_chip(body, "mixed_weight_grads", operands, results)[0]
    values = on_chip(
        body,
        "mixed_weight_grads",
        operands,
        (((2 * width, columns), F32),) * 2 + (((4 * width, columns), BF16),),
        scratch=(pltpu.VMEM((width, 8 * columns), F32),),
    )
    return values[:2], values[2:]


def mixed_finish(keeps, arrived):
    rows, columns = keeps[0].shape
    one = rows // 4

    def body(ins, outs, _):
        first = ins[0][...] + arrived_part(ins[2:], 0, rows)
        for matrix in range(4):
            outs[0][matrix] = first[matrix * one : (matrix + 1) * one]
        second = ins[1][...] + arrived_part(ins[2:], 1, rows)
        outs[1][...] = second[:one]
        outs[2][0] = second[one : 2 * one]
        outs[2][1] = second[2 * one : 3 * one]
        outs[3][...] = second[3 * one :]

    return on_chip(
        body,
        "mixed_finish",
        tuple(keeps) + tuple(arrived),
        (
            ((4, one, columns), F32),
            ((one, columns), F32),
            ((2, one, columns), F32),
            ((one, columns), F32),
        ),
        flops=1_000,
    )


def unpack_small(parts, taps, columns):
    upper = (taps + 1) // 2
    width = parts[0].shape[1]

    def body(ins, outs, scratch):
        total = scratch[0]
        total[...] = (ins[0][...] + ins[1][...]) + (ins[2][...] + ins[3][...])
        outs[0][...] = total[:5, :]
        outs[1][:upper, :] = total[9 : 9 + upper, :columns]
        outs[1][upper:, :] = total[9 : 9 + taps - upper, columns:]
        outs[2][0:1, :] = total[8:9, :columns]
        outs[2][1:2, :] = total[8:9, columns:]

    return on_chip(
        body,
        "unpack_small",
        parts,
        (((5, width), F32), ((taps, columns), F32), ((2, columns), F32)),
        scratch=(pltpu.VMEM(parts[0].shape, F32),),
        flops=1_000,
    )


PAD = 16


def pad_rows(padded, rows, columns, value):
    padded[:PAD, :] = jnp.zeros((PAD, columns), F32)
    padded[PAD + rows :, :] = jnp.zeros((PAD, columns), F32)
    padded[PAD : PAD + rows, :] = value


def conv_forward(kept, own, other, gains, weights, depth_kernel):
    rows, width = own.shape
    taps, columns = depth_kernel.shape
    half_taps = (taps - 1) // 2

    def body(ins, outs, scratch):
        kept_ref, own_ref, other_ref, gain_ref, weight_ref, tap_ref = ins
        conv_ref, sums_ref = outs
        padded = scratch[0]
        after = kept_residual(kept_ref, width) + both_parts(own_ref, other_ref)
        conv_ref[:, :width] = after
        entries = entries_of(after, gain_ref[2:3, :])
        joined = matmul(entries, weight_ref[:, 5 * columns : 7 * columns])
        value = joined[:, :columns]
        gate = jax.nn.sigmoid(joined[:, columns:])
        conv_ref[:, width : width + columns] = value
        conv_ref[:, width + columns : width + 2 * columns] = gate
        pad_rows(padded, rows, columns, value * gate)
        total = jnp.zeros((rows, columns), F32)
        for tap in range(taps):
            start = PAD - half_taps + tap
            total = total + tap_ref[tap : tap + 1, :] * padded[start : start + rows, :]
        conv_ref[:, width + 2 * columns :] = total
        sums_ref[0:1, :] = jnp.sum(total, 0, keepdims=True)
        sums_ref[1:2, :] = jnp.sum(total * total, 0, keepdims=True)

    return on_chip(
        body,
        "conv_forward",
        (kept, own, other, gains, weights, depth_kernel),
        (((rows, width + 3 * columns), F32), ((2, columns), F32)),
        scratch=(pltpu.VMEM((rows + 2 * PAD, columns), F32),),
    )


def batch_norm(conv_ref, sums_ref, batch_ref, token_count):
    columns = sums_ref.shape[1]
    column_mean = sums_ref[0:1, :] / token_count
    inverse = lax.rsqrt(sums_ref[1:2, :] / token_count - column_mean * column_mean + EPSILON)
    standard = (conv_ref[:, conv_ref.shape[1] - columns :] - column_mean) * inverse
    return standard, inverse, standard * batch_ref[0:1, :] + batch_ref[1:2, :]


def norm_forward(conv_kept, sums, batch, weights, token_count):
    rows = conv_kept.shape[0]
    columns = sums.shape[1]
    width = weights.shape[0]

    def body(ins, outs, _):
        conv_ref, sums_ref, batch_ref, weight_ref = ins
        _, _, shifted = batch_norm(conv_ref, sums_ref, batch_ref, token_count)
        activated = (shifted * jax.nn.sigmoid(shifted)).astype(BF16)
        outs[0][...] = right_transposed(activated, weight_ref[:, 7 * columns :]).astype(BF16)

    return on_chip(
        body, "norm_forward", (conv_kept, sums, batch, weights), (((rows, width), BF16),)
    )[0]


def norm_backward(gradient, own, other, kept, gains, weights, conv_kept, sums, batch, count):
    rows, width = gradient.shape
    columns = sums.shape[1]

    def body(ins, outs, _):
        grad_ref, own_ref, other_ref, x_ref, gain_ref, weight_ref, conv_ref, sums_ref, batch_ref = (
            ins
        )
        grads_ref, grad_sums_ref, gain_grad_ref = outs
        normed, factor = norm_parts(x_ref[:, :width])
        passed, gain_grad = norm_back(
            both_parts(own_ref, other_ref), normed, factor, gain_ref[3:4, :]
        )
        gain_grad_ref[...] = gain_grad
        total = grad_ref[...] + passed
        grads_ref[:, :width] = total
        standard, _, shifted = batch_norm(conv_ref, sums_ref, batch_ref, count)
        grad_shifted = matmul(
            total.astype(BF16), weight_ref[:, 7 * columns :]
        ) * swish_slope(shifted, jax.nn.sigmoid(shifted))
        grads_ref[:, width:] = grad_shifted
        grad_sums_ref[0:1, :] = jnp.sum(grad_shifted, 0, keepdims=True)
        grad_sums_ref[1:2, :] = jnp.sum(grad_shifted * standard, 0, keepdims=True)

    return on_chip(
        body,
        "norm_backward",
        (gradient, own, other, kept, gains, weights, conv_kept, sums, batch),
        (((rows, width + columns), F32), ((2, columns), F32), ((1, width), F32)),
    )


def conv_backward(norm_grads, grad_sums, conv_kept, sums, batch, weights, depth_kernel, count):
    rows = conv_kept.shape[0]
    columns = sums.shape[1]
    width = weights.shape[0]
    taps = depth_kernel.shape[0]
    half_taps = (taps - 1) // 2

    def body(ins, outs, scratch):
        grads_ref, grad_sums_ref, conv_ref, sums_ref, batch_ref, weight_ref, tap_ref = ins
        grad_conv_ref, joined_ref, part_ref = outs
        padded = scratch[0]
        standard, inverse, _ = batch_norm(conv_ref, sums_ref, batch_ref, count)
        grad_conv = (inverse * batch_ref[0:1, :]) * (
            grads_ref[:, width:]
            - grad_sums_ref[0:1, :] / count
            - standard * (grad_sums_ref[1:2, :] / count)
        )
        grad_conv_ref[...] = grad_conv
        pad_rows(padded, rows, columns, grad_conv)
        total = jnp.zeros((rows, columns), F32)
        for tap in range(taps):
            start = PAD + half_taps - tap
            total = total + tap_ref[tap : tap + 1, :] * padded[start : start + rows, :]
        gate_sigma = conv_ref[:, width + columns : width + 2 * columns]
        grad_value = total * gate_sigma
        grad_gate = grad_value * conv_ref[:, width : width + columns] * (1.0 - gate_sigma)
        joined = jnp.concatenate([grad_value, grad_gate], 1).astype(BF16)
        joined_ref[...] = joined
        part_ref[...] = right_transposed(
            joined, weight_ref[:, 5 * columns : 7 * columns]
        ).astype(BF16)

    return on_chip(
        body,
        "conv_backward",
        (norm_grads, grad_sums, conv_kept, sums, batch, weights, depth_kernel),
        (((rows, columns), F32), ((rows, 2 * columns), BF16), ((rows, width), BF16)),
        scratch=(pltpu.VMEM((rows + 2 * PAD, columns), F32),),
    )


def conv_weight_grads(norm_grads, grad_conv, joined, conv_kept, sums, batch, gains, taps, count):
    rows, columns = grad_conv.shape
    width = gains.shape[1]
    half_taps = (taps - 1) // 2

    def body(ins, outs, scratch):
        grads_ref, grad_ref, joined_ref, conv_ref, sums_ref, batch_ref, gain_ref = ins
        padded = scratch[0]
        entries = entries_of(conv_ref[:, :width], gain_ref[2:3, :])
        outs[0][:, : 2 * columns] = left_transposed(entries, joined_ref[...]).astype(BF16)
        _, _, shifted = batch_norm(conv_ref, sums_ref, batch_ref, count)
        activated = (shifted * jax.nn.sigmoid(shifted)).astype(BF16)
        outs[0][:, 2 * columns :] = left_transposed(
            grads_ref[:, :width].astype(BF16), activated
        ).astype(BF16)
        value = conv_ref[:, width : width + columns]
        gate = conv_ref[:, width + columns : width + 2 * columns]
        pad_rows(padded, rows, columns, value * gate)
        grad_conv_value = grad_ref[...]
        for tap in range(taps):
            start = PAD - half_taps + tap
            outs[1][tap : tap + 1, :] = jnp.sum(
                padded[start : start + rows, :] * grad_conv_value, 0, keepdims=True
            )

    return on_chip(
        body,
        "conv_weight_grads",
        (norm_grads, grad_conv, joined, conv_kept, sums, batch, gains),
        (((width, 3 * columns), BF16), ((taps, columns), F32)),
        scratch=(pltpu.VMEM((rows + 2 * PAD, columns), F32),),
    )


def first_back(gradient, own, other, kept, pre, gains, weights):
    rows, width = gradient.shape
    hidden = weights.shape[1] // 2

    def body(ins, outs, _):
        grad_ref, own_ref, other_ref, kept_ref, pre_ref, gain_ref, weight_ref = ins
        grads_ref, total_ref, part_ref, gain_grad_ref = outs
        normed, factor = norm_parts(kept_residual(kept_ref, width))
        passed, gain_grad = norm_back(
            both_parts(own_ref, other_ref), normed, factor, gain_ref[1:2, :]
        )
        gain_grad_ref[...] = gain_grad
        total = grad_ref[...] + passed
        total_ref[...] = total
        part_ref[...] = ff_back_body(total, pre_ref[...], weight_ref, grads_ref).astype(BF16)

    return on_chip(
        body,
        "first_back",
        (gradient, own, other, kept, pre, gains, weights),
        (
            ((rows, width + 2 * hidden), BF16),
            ((rows, width), F32),
            ((rows, width), BF16),
            ((1, width), F32),
        ),
    )


def input_back(total, own, other, tokens, gains, gain_grads, tap_grads, bias_grads):
    rows, width = tokens.shape
    taps, columns = tap_grads.shape
    upper = (taps + 1) // 2
    packed_rows = 8 + -(-(1 + upper) // 8) * 8

    def body(ins, outs, _):
        total_ref, own_ref, other_ref, x_ref, gain_ref = ins[:5]
        tap_ref, bias_ref = ins[9:]
        packed = outs[1]
        normed, factor = norm_parts(x_ref[...].astype(F32))
        passed, gain_grad = norm_back(
            both_parts(own_ref, other_ref), normed, factor, gain_ref[0:1, :]
        )
        outs[0][...] = own_half(total_ref[...] + passed)
        packed[...] = jnp.zeros((packed_rows, 2 * columns), F32)
        packed[0:1, :] = gain_grad
        for place in range(4):
            packed[place + 1 : place + 2, :] = ins[5 + place][...]
        packed[8:9, :columns] = bias_ref[0:1, :]
        packed[8:9, columns:] = bias_ref[1:2, :]
        packed[9 : 9 + upper, :columns] = tap_ref[:upper, :]
        packed[9 : 9 + taps - upper, columns:] = tap_ref[upper:, :]

    return on_chip(
        body,
        "input_back",
        (total, own, other, tokens, gains) + tuple(gain_grads) + (tap_grads, bias_grads),
        (((rows // 2, width), F32), ((packed_rows, 2 * columns), F32)),
        flops=1_000_000,
    )


def reduce_plain(grads):
    return lax.psum_scatter(grads.astype(BF16), "dp", scatter_dimension=0, tiled=True).astype(F32)


def stacked_columns(pieces, count):
    width = pieces.shape[1] // count
    return jnp.stack([pieces[:, index * width : (index + 1) * width] for index in range(count)])


def unstacked(stacked):
    return [stacked[index] for index in range(stacked.shape[0])]


def body(
    tokens,
    norm_gains,
    first_in,
    first_out,
    attention_in,
    attention_out,
    head_biases,
    gated_in,
    pointwise_out,
    depth_kernel,
    batch_scale,
    batch_shift,
    second_in,
    second_out,
    cotangent,
):
    local_heads = HEAD_TOTAL // lax.axis_size("tensor")
    length = tokens.shape[0] * lax.axis_size("tensor")
    token_count = float(length * lax.axis_size("dp"))
    columns = attention_out.shape[1]
    hidden = first_in.shape[1]
    width = tokens.shape[1]
    table = sinusoid(length, width).astype(BF16)
    batch = jnp.stack([batch_scale, batch_shift])
    split = doubling()

    def gather(pieces):
        return lax.all_gather(jnp.concatenate(pieces, 1), "dp", axis=0, tiled=True)

    tokens_all = both_halves(tokens)
    cotangent_all = both_halves(cotangent)

    if split:
        batch_one = (first_in, first_out)
        joint_two = jnp.concatenate(
            [
                attention_in.reshape(-1, columns),
                attention_out,
                gated_in.reshape(-1, columns),
                pointwise_out,
            ],
            0,
        )
        batch_two = (joint_two[: joint_two.shape[0] // 2], joint_two[joint_two.shape[0] // 2 :])
        batch_three = (second_in, second_out)
        joint_three = jnp.concatenate(batch_three, 0)
        arrived_one = gather_send(batch_one, 0)
        batch_one = on_chip(
            lambda ins, outs, _: (
                outs[0].__setitem__(..., ins[0][...]),
                outs[1].__setitem__(..., ins[1][...]),
            ),
            "first_copy",
            batch_one,
            tuple((value.shape, value.dtype) for value in batch_one),
            flops=1_000,
        )
        arrived_one = tie(arrived_one, (batch_one, table))
        arrived_two = gather_send((tie(joint_two, arrived_one),), 0)
        batch_one = gather_join(tuple(batch_one), tuple(arrived_one))
        arrived_one = gather_send(batch_one, 1)
        batch_one = gather_join(batch_one, tie(arrived_one, tokens_all))
        arrived_one = gather_send(batch_one, 2)
        batch_two = gather_join(batch_two, tie(arrived_two, batch_one))
        arrived_two = gather_send(batch_two, 1)
        batch_one = gather_join(
            batch_one, tie(arrived_one, (batch_two, cotangent_all)), joint=True
        )
        arrived_three = gather_send((tie(joint_three, batch_one),), 0)
        batch_one += (shift(batch_one[0], "dp", 1),)
    else:
        batch_one = gather([first_in, first_out])
        mixed_weights = gather(
            unstacked(attention_in) + [attention_out] + unstacked(gated_in) + [pointwise_out]
        )
        positions = position_forward(table, mixed_weights, columns)
        second_weights = gather([second_in, second_out])

    pre1, part1, first_weights = first_forward(tokens_all, norm_gains, batch_one)
    other1 = swap(part1)
    if split:
        batch_two = gather_join(batch_two, tie(arrived_two, part1))
        arrived_two = gather_send(batch_two, 2)
        batch_three = gather_join(batch_three, tie(arrived_three, batch_two))
        arrived_three = gather_send(batch_three, 1)
        batch_two = gather_join(batch_two, tie(arrived_two, (other1, batch_three)), joint=True)
        batch_two += (shift(batch_two[0], "dp", 1),)
        mixed_weights, positions = mixed_assemble(batch_two, table, width)
    kept, part2 = attention_forward(
        tokens_all, part1, other1, norm_gains, mixed_weights, positions, head_biases, local_heads
    )
    other2 = swap(part2)
    if split:
        batch_three = gather_join(batch_three, tie(arrived_three, part2))
        arrived_three = gather_send(batch_three, 2)
    conv_kept, sums = conv_forward(
        kept, part2, other2, norm_gains, mixed_weights, depth_kernel
    )
    if split:
        batch_three = gather_join(batch_three, tie(arrived_three, sums), joint=True)
        batch_three += (shift(batch_three[0], "dp", 1),)
        second_weights = second_assemble(batch_three, width)
    sums = sum_over(sums, "dp")
    part3 = norm_forward(conv_kept, sums, batch, mixed_weights, token_count)
    other3 = swap(part3)
    other3 = tie(other3, second_weights)
    second_kept, part4 = second_forward(conv_kept, part3, other3, norm_gains, second_weights)
    other4 = swap(part4)
    block_out, grad4, second_rows, part5, gain5 = second_back(
        second_kept, part4, other4, cotangent_all, norm_gains, second_weights
    )
    other5 = swap(part5)
    second_name = "second_weight_grads"
    if split:
        keeps, sends = ff_weight_split(second_rows, second_kept, norm_gains, 3, second_name)
        second_keeps, sends = scatter_add(keeps, scatter_send(sends, 0), 0, "second_sum")
        second_arrived = scatter_send(sends, 1)
        other5 = tie(other5, second_keeps)
    else:
        second_grads = reduce_plain(
            ff_weight_grads(second_rows, second_kept, norm_gains, 3, second_name)
        )
        second_reduced = (second_grads[:, :hidden], second_grads[:, hidden:])
    norm_grads, grad_sums, gain4 = norm_backward(
        grad4,
        part5,
        other5,
        second_kept,
        norm_gains,
        mixed_weights,
        conv_kept,
        sums,
        batch,
        token_count,
    )
    grad_sums = sum_over(grad_sums, "dp")
    if split:
        second_keeps, sends = scatter_add(second_keeps, second_arrived, 1, "second_sum")
        grad_sums = tie(grad_sums, second_keeps)
    grad_conv, joined3, part6 = conv_backward(
        norm_grads, grad_sums, conv_kept, sums, batch, mixed_weights, depth_kernel, token_count
    )
    other6 = swap(part6)
    conv_grads, tap_grads = conv_weight_grads(
        norm_grads,
        grad_conv,
        joined3,
        conv_kept,
        sums,
        batch,
        norm_gains,
        depth_kernel.shape[0],
        token_count,
    )
    other6 = tie(other6, conv_grads)
    if split:
        second_arrived = scatter_send(tie(sends, part6), 2)
        second_arrived = tie(second_arrived, conv_grads)
        second_keeps, sends = scatter_add(second_keeps, second_arrived, 2, "second_sum")
        second_arrived = scatter_send(sends, 3)
        other6 = tie(other6, second_keeps)
    grad2, joined2, table_grad, part7, gain3, bias_grads = attention_back(
        norm_grads,
        part6,
        other6,
        conv_kept,
        norm_gains,
        mixed_weights,
        positions,
        kept,
        local_heads,
    )
    other7 = swap(part7)
    mixed_grads = mixed_weight_grads(
        joined2, table, table_grad, grad2, kept, norm_gains, conv_grads, split
    )
    if split:
        keeps, sends = mixed_grads
        mixed_keeps, sends = scatter_add(keeps, scatter_send(sends, 0), 0, "mixed_sum")
        mixed_arrived = scatter_send(sends, 1)
        other7 = tie(other7, mixed_keeps)
    first_rows, grad1, part8, gain2 = first_back(
        grad2, part7, other7, kept, pre1, norm_gains, first_weights
    )
    other8 = swap(part8)
    small = ((gain2, gain3, gain4, gain5), tap_grads, bias_grads)
    if split:
        mixed_keeps, sends = scatter_add(mixed_keeps, mixed_arrived, 1, "mixed_sum")
        mixed_arrived = scatter_send(sends, 2)
        keeps, sends = ff_weight_split(
            tie(first_rows, mixed_keeps), tokens_all, norm_gains, 0, "first_weight_grads"
        )
        first_arrived = scatter_send(sends, 0)
        first_keeps, sends = scatter_add(keeps, first_arrived, 0, "first_sum")
        first_arrived = scatter_send(sends, 1)
        second_reduced, _ = scatter_add(
            second_keeps, tie(second_arrived, first_keeps), 3, "second_sum"
        )
        mixed_keeps, sends = scatter_add(
            mixed_keeps, tie(mixed_arrived, first_keeps), 2, "mixed_sum"
        )
        mixed_arrived = scatter_send(sends, 3)
        other8 = tie(other8, mixed_keeps)
        grad_start, packed = input_back(grad1, part8, other8, tokens_all, norm_gains, *small)
        first_arrived = tie(first_arrived, packed)
        first_keeps, sends = scatter_add(first_keeps, first_arrived, 1, "first_sum")
        first_arrived = scatter_send(sends, 2)
        packed = sum_over(tie(sum_over(packed, "dp", 1, 2), first_keeps), "dp", 2, 4)
        reduced_attention, reduced_mixing, reduced_gated, reduced_pointwise = mixed_finish(
            mixed_keeps, tie(mixed_arrived, first_keeps)
        )
        first_arrived = tie(first_arrived, reduced_mixing)
        first_keeps, sends = scatter_add(first_keeps, first_arrived, 2, "first_sum")
        first_arrived = scatter_send(sends, 3)
        packed = tie(packed, first_keeps)
        parts = (packed,) + tuple(shift(packed, "dp", mask) for mask in (4, 8, 12))
        (reduced_in, reduced_out), _ = scatter_add(first_keeps, first_arrived, 3, "first_sum")
    else:
        grad_start, packed = input_back(grad1, part8, other8, tokens_all, norm_gains, *small)
        first_grads = reduce_plain(
            ff_weight_grads(first_rows, tokens_all, norm_gains, 0, "first_weight_grads")
        )
        reduced_in, reduced_out = first_grads[:, :hidden], first_grads[:, hidden:]
        mixed = reduce_plain(mixed_grads)
        reduced_attention = stacked_columns(mixed[:, : 4 * columns], 4)
        reduced_mixing = mixed[:, 4 * columns : 5 * columns]
        reduced_gated = stacked_columns(mixed[:, 5 * columns : 7 * columns], 2)
        reduced_pointwise = mixed[:, 7 * columns :]
        packed = sum_over(packed, "dp")
        parts = (packed,) + (jnp.zeros_like(packed),) * 3
    gain_total, tap_total, bias_total = unpack_small(parts, depth_kernel.shape[0], columns)
    return (
        block_out,
        grad_start,
        gain_total,
        reduced_in,
        reduced_out,
        reduced_attention,
        reduced_mixing,
        bias_total,
        reduced_gated,
        reduced_pointwise,
        tap_total,
        grad_sums[1],
        grad_sums[0],
        *second_reduced,
    )


def solution(mesh):
    placed = (
        P(("dp", "tensor"), None),
        P(),
        P("dp", "tensor"),
        P("dp", "tensor"),
        P(None, "dp", "tensor"),
        P("dp", "tensor"),
        P(None, "tensor"),
        P(None, "dp", "tensor"),
        P("dp", "tensor"),
        P(None, "tensor"),
        P("tensor"),
        P("tensor"),
        P("dp", "tensor"),
        P("dp", "tensor"),
        P(("dp", "tensor"), None),
    )
    return jax.shard_map(
        body,
        mesh=mesh,
        in_specs=placed,
        out_specs=(
            P(("dp", "tensor"), None),
            P(("dp", "tensor"), None),
            P(),
            P("dp", "tensor"),
            P("dp", "tensor"),
            P(None, "dp", "tensor"),
            P("dp", "tensor"),
            P(None, "tensor"),
            P(None, "dp", "tensor"),
            P("dp", "tensor"),
            P(None, "tensor"),
            P("tensor"),
            P("tensor"),
            P("dp", "tensor"),
            P("dp", "tensor"),
        ),
        check_vma=False,
    )
```

```python
import math

import jax
import jax.numpy as jnp
from jax import lax
from jax.experimental import pallas as pl
from jax.experimental.pallas import tpu as pltpu
from jax.sharding import PartitionSpec as P

HEAD_TOTAL = 8
EPSILON = 1e-05
BF16 = jnp.bfloat16
F32 = jnp.float32


def matmul(left_side, right_side):
    return jnp.dot(left_side, right_side, preferred_element_type=F32)


def right_transposed(left_side, right_side):
    return lax.dot_general(
        left_side, right_side, (((1,), (1,)), ((), ())), preferred_element_type=F32
    )


def left_transposed(left_side, right_side):
    return lax.dot_general(
        left_side, right_side, (((0,), (0,)), ((), ())), preferred_element_type=F32
    )


def swish_slope(pre_value, gate_sigma):
    return gate_sigma * (1.0 + pre_value * (1.0 - gate_sigma))


def norm_parts(residual):
    centred = residual - jnp.mean(residual, -1, keepdims=True)
    factor = lax.rsqrt(jnp.mean(centred * centred, -1, keepdims=True) + EPSILON)
    return centred * factor, factor


def norm_back(gradient, normed, factor, norm_gain):
    scaled = gradient * norm_gain
    inner_sum = (
        scaled
        - jnp.mean(scaled, -1, keepdims=True)
        - normed * jnp.mean(scaled * normed, -1, keepdims=True)
    )
    return factor * inner_sum, jnp.sum(gradient * normed, 0, keepdims=True)


def sinusoid(length, features):
    offsets = jnp.arange(2 * length, dtype=F32) - (length - 1)
    half_width = features // 2
    frequency = jnp.exp(jnp.arange(half_width, dtype=F32) * (-math.log(10000.0) / half_width))
    angles = offsets[:, None] * frequency[None, :]
    table = jnp.concatenate([jnp.sin(angles), jnp.cos(angles)], 1)
    return jnp.where(offsets[:, None] < length, table, 0.0)


def on_chip(function, name, operands, results, scratch=(), flops=300_000_000):
    count = len(operands)
    total = count + len(results)

    def kernel(*refs):
        function(refs[:count], refs[count:total], refs[total:])

    moved = sum(value.size * value.dtype.itemsize for value in operands)
    moved += sum(math.prod(shape) * jnp.dtype(kind).itemsize for shape, kind in results)
    return pl.pallas_call(
        kernel,
        out_shape=[jax.ShapeDtypeStruct(shape, kind) for shape, kind in results],
        in_specs=[pl.BlockSpec(memory_space=pltpu.VMEM)] * count,
        out_specs=[pl.BlockSpec(memory_space=pltpu.VMEM)] * len(results),
        scratch_shapes=list(scratch),
        compiler_params=pltpu.CompilerParams(vmem_limit_bytes=24 * 1024 * 1024),
        cost_estimate=pl.CostEstimate(flops=flops, bytes_accessed=moved, transcendentals=0),
        name=name,
    )(*operands)


def swap(value):
    return lax.ppermute(value, "tensor", [(0, 1), (1, 0)])


def both_halves(own):
    other = swap(own)
    first = lax.axis_index("tensor") == 0
    return jnp.concatenate([jnp.where(first, own, other), jnp.where(first, other, own)], 0)


def own_half(value):
    half = value.shape[0] // 2
    return jnp.where(lax.axis_index("tensor") == 0, value[:half], value[half:])


def shift(value, axis, mask):
    return lax.ppermute(value, axis, [(k, k ^ mask) for k in range(lax.axis_size(axis))])


def sum_over(value, axis, step=1, stop=None):
    size = lax.axis_size(axis)
    if size & (size - 1):
        return lax.psum(value, axis)
    stop = stop or size
    while step < stop:
        if step * 4 <= stop:
            near, far, both = (shift(value, axis, step * times) for times in (1, 2, 3))
            value = (value + near) + (far + both)
            step *= 4
        else:
            value = value + shift(value, axis, step)
            step *= 2
    return value


GATHER_ORDERS = ((8, 4, 2, 1), (8, 2, 4, 1))
SCATTER_ORDERS = ((1, 2, 4, 8), (1, 4, 2, 8))


def doubling():
    return lax.axis_size("dp") == 16


def distances(order):
    blocks = [0]
    for mask in order:
        blocks = blocks + [block ^ mask for block in blocks]
    return blocks


def halving(order):
    return distances(order[::-1])


def gather_send(values, stage):
    return tuple(shift(value, "dp", order[stage]) for value, order in zip(values, GATHER_ORDERS))


def gather_join(pair, arrived, joint=False):
    sizes = [value.shape[0] for value in pair]

    def body(ins, outs, _):
        for group in range(2):
            rows = sizes[group]
            target, start = (outs[0], 2 * rows * group) if joint else (outs[group], 0)
            source, begin = (ins[2], rows * group) if len(arrived) == 1 else (ins[2 + group], 0)
            target[start : start + rows, :] = ins[group][...]
            target[start + rows : start + 2 * rows, :] = source[begin : begin + rows, :]

    columns, kind = pair[0].shape[1], pair[0].dtype
    if joint:
        results = (((2 * sum(sizes), columns), kind),)
    else:
        results = tuple(((2 * rows, columns), kind) for rows in sizes)
    return tuple(on_chip(body, "gather_join", tuple(pair) + arrived, results, flops=1_000))


def tie(values, *others):
    return lax.optimization_barrier((values, others))[0]


def assemble(ref, target_ref, group, half, matrices, first_column):
    device = lax.axis_index("dp")
    blocks = distances(GATHER_ORDERS[group])
    count = len(blocks) // 2
    rows = target_ref.shape[0] // len(blocks)
    columns = ref.shape[1]
    for place in range(count):
        owner = device ^ blocks[half * count + place]
        target = pl.ds(pl.multiple_of(owner * rows, rows), rows)
        for matrix in range(matrices):
            start = ((group * count + place) * matrices + matrix) * rows
            left = first_column + matrix * columns
            target_ref[target, left : left + columns] = ref[start : start + rows, :]


def scatter_split(total_ref, keep_ref, send_ref, group, matrices):
    device = lax.axis_index("dp")
    blocks = halving(SCATTER_ORDERS[group])
    count = len(blocks) // 2
    rows = total_ref.shape[0] // len(blocks)
    columns = keep_ref.shape[1]
    first = group * keep_ref.shape[0]
    for place, block in enumerate(blocks):
        source = pl.ds(pl.multiple_of((device ^ block) * rows, rows), rows)
        for matrix in range(matrices):
            piece = total_ref[source, matrix * columns : (matrix + 1) * columns]
            start = ((place % count) * matrices + matrix) * rows
            if place < count:
                keep_ref[start : start + rows, :] = piece
            else:
                send_ref[first + start : first + start + rows, :] = piece.astype(BF16)


def scatter_send(sends, stage):
    return tuple(shift(send, "dp", order[stage]) for send, order in zip(sends, SCATTER_ORDERS))


def arrived_part(refs, group, rows):
    if len(refs) == 1:
        return refs[0][group * rows : (group + 1) * rows, :].astype(F32)
    return refs[group][...].astype(F32)


def scatter_add(keeps, arrived, stage, name):
    rows, columns = keeps[0].shape
    half = rows // 2
    last = stage == len(SCATTER_ORDERS[0]) - 1
    joint = stage == len(SCATTER_ORDERS[0]) - 2
    results = (((rows if last else half, columns), F32),) * 2
    if not last:
        results += (((rows, columns), BF16),) if joint else (((half, columns), BF16),) * 2

    def body(ins, outs, _):
        for group in range(2):
            total = ins[group][...] + arrived_part(ins[2:], group, rows)
            if last:
                outs[group][...] = total
                continue
            outs[group][...] = total[:half]
            if joint:
                outs[2][group * half : (group + 1) * half, :] = total[half:].astype(BF16)
            else:
                outs[2 + group][...] = total[half:].astype(BF16)

    values = on_chip(body, name, tuple(keeps) + tuple(arrived), results, flops=1_000)
    return values[:2], values[2:]


def entries_of(residual, gain):
    return (norm_parts(residual)[0] * gain).astype(BF16)


def ff_forward_body(entries, weight_ref, part_ref):
    half = weight_ref.shape[1] // 2
    pre = matmul(entries, weight_ref[:, :half])
    hidden = (pre * jax.nn.sigmoid(pre)).astype(BF16)
    part_ref[...] = right_transposed(hidden, weight_ref[:, half:]).astype(BF16)
    return pre


def both_parts(own_ref, other_ref):
    return own_ref[...].astype(F32) + other_ref[...].astype(F32)


def first_forward(tokens, gains, weights):
    rows, width = tokens.shape
    split = isinstance(weights, tuple)
    pieces = weights if split else (weights,)
    hidden = pieces[0].shape[1] if split else weights.shape[1] // 2

    def body(ins, outs, _):
        weight_ref = ins[2]
        if split:
            weight_ref = outs[2]
            for group in range(2):
                for half in range(2):
                    assemble(ins[2 + half], weight_ref, group, half, 1, group * hidden)
        entries = entries_of(ins[0][...].astype(F32), ins[1][0:1, :])
        outs[0][...] = ff_forward_body(entries, weight_ref, outs[1])

    results = (((rows, hidden), F32), ((rows, width), BF16))
    if split:
        results += (((width, 2 * hidden), BF16),)
    values = on_chip(body, "first_forward", (tokens, gains) + pieces, results)
    return values if split else tuple(values) + (weights,)


def second_forward(conv_kept, own, other, gains, weights):
    rows, width = own.shape
    hidden = weights.shape[1] // 2

    def body(ins, outs, _):
        kept_ref, part_ref = outs
        after = ins[0][:, :width] + both_parts(ins[1], ins[2])
        kept_ref[:, :width] = after
        kept_ref[:, width:] = ff_forward_body(
            entries_of(after, ins[3][3:4, :]), ins[4], part_ref
        )

    return on_chip(
        body,
        "second_forward",
        (conv_kept, own, other, gains, weights),
        (((rows, width + hidden), F32), ((rows, width), BF16)),
    )


def ff_back_body(gradient, pre, weight_ref, grads_ref):
    width = gradient.shape[1]
    half = weight_ref.shape[1] // 2
    branch = (0.5 * gradient).astype(BF16)
    grads_ref[:, :width] = branch
    grad_hidden = matmul(branch, weight_ref[:, half:])
    sigma = jax.nn.sigmoid(pre)
    grad_pre = (grad_hidden * swish_slope(pre, sigma)).astype(BF16)
    grads_ref[:, width : width + half] = grad_pre
    grads_ref[:, width + half : width + 2 * half] = (pre * sigma).astype(BF16)
    return right_transposed(grad_pre, weight_ref[:, :half])


def second_back(kept, own, other, cotangent, gains, weights):
    rows, width = own.shape
    hidden = weights.shape[1] // 2

    def body(ins, outs, _):
        kept_ref, own_ref, other_ref, cot_ref, gain_ref, weight_ref = ins
        out_ref, grad_ref, grads_ref, part_ref, gain_grad_ref = outs
        after = kept_ref[:, :width] + 0.5 * both_parts(own_ref, other_ref)
        normed, factor = norm_parts(after)
        gain = gain_ref[4:5, :]
        out_ref[...] = own_half(normed * gain).astype(BF16)
        gradient, gain_grad = norm_back(cot_ref[...].astype(F32), normed, factor, gain)
        gain_grad_ref[...] = gain_grad
        grad_ref[...] = gradient
        part_ref[...] = ff_back_body(
            gradient, kept_ref[:, width:], weight_ref, grads_ref
        ).astype(BF16)

    return on_chip(
        body,
        "second_back",
        (kept, own, other, cotangent, gains, weights),
        (
            ((rows // 2, width), BF16),
            ((rows, width), F32),
            ((rows, width + 2 * hidden), BF16),
            ((rows, width), BF16),
            ((1, width), F32),
        ),
    )


def ff_weight_grads(grads, residual, gains, row, name):
    width = gains.shape[1]
    half = (grads.shape[1] - width) // 2

    def body(ins, outs, _):
        grads_ref, x_ref, gain_ref = ins
        entries = entries_of(x_ref[:, :width].astype(F32), gain_ref[row : row + 1, :])
        outs[0][:, :half] = left_transposed(entries, grads_ref[:, width : width + half]).astype(
            BF16
        )
        outs[0][:, half:] = left_transposed(
            grads_ref[:, :width], grads_ref[:, width + half :]
        ).astype(BF16)

    return on_chip(body, name, (grads, residual, gains), (((width, 2 * half), BF16),))[0]


def ff_weight_split(grads, residual, gains, row, name):
    width = gains.shape[1]
    half = (grads.shape[1] - width) // 2

    def body(ins, outs, scratch):
        grads_ref, x_ref, gain_ref = ins
        entries = entries_of(x_ref[:, :width].astype(F32), gain_ref[row : row + 1, :])
        scratch[0][...] = left_transposed(entries, grads_ref[:, width : width + half])
        scatter_split(scratch[0], outs[0], outs[2], 0, 1)
        scratch[0][...] = left_transposed(grads_ref[:, :width], grads_ref[:, width + half :])
        scatter_split(scratch[0], outs[1], outs[2], 1, 1)

    values = on_chip(
        body,
        name,
        (grads, residual, gains),
        (((width // 2, half), F32),) * 2 + (((width, half), BF16),),
        scratch=(pltpu.VMEM((width, half), F32),),
    )
    return values[:2], values[2:]


def kept_residual(kept_ref, width):
    return kept_ref[:, :width].astype(F32) + kept_ref[:, width : 2 * width].astype(F32)


def position_forward(table, weights, columns):
    def body(ins, outs, _):
        outs[0][...] = matmul(ins[0][...], ins[1][:, 3 * columns : 4 * columns]).astype(BF16)

    return on_chip(
        body, "position_forward", (table, weights), (((table.shape[0], columns), BF16),)
    )[0]


def attention_forward(tokens, own, other, gains, weights, positions, biases, heads):
    rows, width = tokens.shape
    columns = biases.shape[1]
    features = columns // heads
    scale = features ** (-0.5)
    start = 2 * width

    def body(ins, outs, _):
        x_ref, own_ref, other_ref, gain_ref, weight_ref, table_ref, bias_ref = ins
        kept_ref, part_ref = outs
        after = x_ref[...].astype(F32) + 0.5 * both_parts(own_ref, other_ref)
        high = after.astype(BF16)
        kept_ref[:, :width] = high
        kept_ref[:, width : 2 * width] = (after - high.astype(F32)).astype(BF16)
        entries = entries_of(after, gain_ref[1:2, :])
        joined = matmul(entries, weight_ref[:, : 3 * columns])
        queries = joined[:, :columns]
        content_q = (queries + bias_ref[0:1, :]).astype(BF16)
        position_q = (queries + bias_ref[1:2, :]).astype(BF16)
        keys = joined[:, columns : 2 * columns].astype(BF16)
        values = joined[:, 2 * columns :].astype(BF16)
        kept_ref[:, start : start + columns] = content_q
        kept_ref[:, start + columns : start + 2 * columns] = position_q
        kept_ref[:, start + 2 * columns : start + 3 * columns] = keys
        kept_ref[:, start + 3 * columns : start + 4 * columns] = values
        mixed = []
        for head in range(heads):
            part = slice(head * features, (head + 1) * features)
            content = right_transposed(content_q[:, part], keys[:, part])
            raw = right_transposed(position_q[:, part], table_ref[:, part])
            shifted = pltpu.roll(raw, rows + 1, 1, stride=1, stride_axis=0)[:, :rows]
            scores = (content + shifted) * scale
            lifted = jnp.exp(scores - jnp.max(scores, -1, keepdims=True))
            probability = (lifted / jnp.sum(lifted, -1, keepdims=True)).astype(BF16)
            place = start + 5 * columns + head * rows
            kept_ref[:, place : place + rows] = probability
            mixed.append(matmul(probability, values[:, part]))
        attended = jnp.concatenate(mixed, 1).astype(BF16)
        kept_ref[:, start + 4 * columns : start + 5 * columns] = attended
        part_ref[...] = right_transposed(
            attended, weight_ref[:, 4 * columns : 5 * columns]
        ).astype(BF16)

    return on_chip(
        body,
        "attention_forward",
        (tokens, own, other, gains, weights, positions, biases),
        (((rows, start + 5 * columns + heads * rows), BF16), ((rows, width), BF16)),
    )


def attention_back(norm_grads, own, other, conv_kept, gains, weights, positions, kept, heads):
    rows, width = own.shape
    columns = positions.shape[1]
    features = columns // heads
    scale = features ** (-0.5)
    start = 2 * width

    def body(ins, outs, _):
        grad_ref, own_ref, other_ref, x_ref, gain_ref, weight_ref, table_ref, kept_ref = ins
        total_ref, joined_ref, table_grad_ref, part_ref, gain_grad_ref, bias_ref = outs
        normed, factor = norm_parts(x_ref[:, :width])
        passed, gain_grad = norm_back(
            both_parts(own_ref, other_ref), normed, factor, gain_ref[2:3, :]
        )
        gain_grad_ref[...] = gain_grad
        total = grad_ref[:, :width] + passed
        total_ref[...] = total
        grad_mixed = matmul(
            total.astype(BF16), weight_ref[:, 4 * columns : 5 * columns]
        ).astype(BF16)
        line = lax.broadcasted_iota(jnp.int32, (rows, rows), 0)
        place = lax.broadcasted_iota(jnp.int32, (rows, rows), 1)
        flip = (line + place == rows - 1).astype(F32).astype(BF16)
        content_q = kept_ref[:, start : start + columns]
        flipped_q = matmul(flip, kept_ref[:, start + columns : start + 2 * columns]).astype(BF16)
        keys = kept_ref[:, start + 2 * columns : start + 3 * columns]
        values = kept_ref[:, start + 3 * columns : start + 4 * columns]
        zeros = jnp.zeros((rows, rows), F32)
        from_content, from_position, to_keys, to_values, to_table = [], [], [], [], []
        for head in range(heads):
            part = slice(head * features, (head + 1) * features)
            left = start + 5 * columns + head * rows
            rounded = kept_ref[:, left : left + rows]
            probability = rounded.astype(F32)
            grad_probability = right_transposed(grad_mixed[:, part], values[:, part])
            to_values.append(left_transposed(rounded, grad_mixed[:, part]))
            inner = jnp.sum(probability * grad_probability, -1, keepdims=True)
            grad_scores = (probability * (grad_probability - inner)).astype(BF16) * scale
            grad_scores = grad_scores.astype(BF16)
            from_content.append(matmul(grad_scores, keys[:, part]))
            to_keys.append(left_transposed(grad_scores, content_q[:, part]))
            flipped = jnp.concatenate([matmul(flip, grad_scores), zeros], 1)
            spread = pltpu.roll(flipped, 0, 1, stride=1, stride_axis=0).astype(BF16)
            from_position.append(matmul(spread, table_ref[:, part]))
            to_table.append(left_transposed(spread, flipped_q[:, part]))
        grad_content = jnp.concatenate(from_content, 1)
        grad_position = jnp.concatenate(from_position, 1)
        high = grad_position.astype(BF16)
        low = (grad_position - high.astype(F32)).astype(BF16)
        grad_position = matmul(flip, high) + matmul(flip, low)
        bias_ref[0:1, :] = jnp.sum(grad_content, 0, keepdims=True)
        bias_ref[1:2, :] = jnp.sum(grad_position, 0, keepdims=True)
        joined = jnp.concatenate(
            [grad_content + grad_position] + to_keys + to_values, 1
        ).astype(BF16)
        joined_ref[...] = joined
        table_grad_ref[...] = jnp.concatenate(to_table, 1).astype(BF16)
        part_ref[...] = right_transposed(joined, weight_ref[:, : 3 * columns]).astype(BF16)

    return on_chip(
        body,
        "attention_back",
        (norm_grads, own, other, conv_kept, gains, weights, positions, kept),
        (
            ((rows, width), F32),
            ((rows, 3 * columns), BF16),
            ((2 * rows, columns), BF16),
            ((rows, width), BF16),
            ((1, width), F32),
            ((2, columns), F32),
        ),
    )


def second_assemble(halves, width):
    columns = halves[0].shape[1]

    def body(ins, outs, _):
        for group in range(2):
            for half in range(2):
                assemble(ins[half], outs[0], group, half, 1, group * columns)

    return on_chip(
        body, "second_assemble", halves, (((width, 2 * columns), BF16),), flops=1_000
    )[0]


def mixed_assemble(halves, table, width):
    columns = halves[0].shape[1]

    def body(ins, outs, _):
        for group in range(2):
            for half in range(2):
                assemble(ins[half], outs[0], group, half, 4, 4 * group * columns)
        outs[1][...] = matmul(ins[2][...], outs[0][:, 3 * columns : 4 * columns]).astype(BF16)

    return on_chip(
        body,
        "mixed_assemble",
        halves + (table,),
        (((width, 8 * columns), BF16), ((table.shape[0], columns), BF16)),
    )


def mixed_weight_grads(joined, table, table_grad, total, kept, gains, conv_grads, split):
    width = gains.shape[1]
    columns = table_grad.shape[1]

    def whole(ins, target_ref):
        joined_ref, table_ref, table_grad_ref, total_ref, kept_ref, gain_ref, conv_ref = ins
        entries = entries_of(kept_residual(kept_ref, width), gain_ref[1:2, :])
        attended = kept_ref[:, 2 * width + 4 * columns : 2 * width + 5 * columns]
        target_ref[:, : 3 * columns] = left_transposed(entries, joined_ref[...])
        target_ref[:, 3 * columns : 4 * columns] = left_transposed(
            table_ref[...], table_grad_ref[...]
        )
        target_ref[:, 4 * columns : 5 * columns] = left_transposed(
            total_ref[...].astype(BF16), attended
        )
        target_ref[:, 5 * columns :] = conv_ref[...].astype(F32)

    def body(ins, outs, scratch):
        if not split:
            whole(ins, outs[0])
            return
        whole(ins, scratch[0])
        for group in range(2):
            part = scratch[0].at[:, 4 * group * columns : 4 * (group + 1) * columns]
            scatter_split(part, outs[group], outs[2], group, 4)

    operands = (joined, table, table_grad, total, kept, gains, conv_grads)
    if not split:
        results = (((width, 8 * columns), F32),)
        return on_chip(body, "mixed_weight_grads", operands, results)[0]
    values = on_chip(
        body,
        "mixed_weight_grads",
        operands,
        (((2 * width, columns), F32),) * 2 + (((4 * width, columns), BF16),),
        scratch=(pltpu.VMEM((width, 8 * columns), F32),),
    )
    return values[:2], values[2:]


def mixed_finish(keeps, arrived):
    rows, columns = keeps[0].shape
    one = rows // 4

    def body(ins, outs, _):
        first = ins[0][...] + arrived_part(ins[2:], 0, rows)
        for matrix in range(4):
            outs[0][matrix] = first[matrix * one : (matrix + 1) * one]
        second = ins[1][...] + arrived_part(ins[2:], 1, rows)
        outs[1][...] = second[:one]
        outs[2][0] = second[one : 2 * one]
        outs[2][1] = second[2 * one : 3 * one]
        outs[3][...] = second[3 * one :]

    return on_chip(
        body,
        "mixed_finish",
        tuple(keeps) + tuple(arrived),
        (
            ((4, one, columns), F32),
            ((one, columns), F32),
            ((2, one, columns), F32),
            ((one, columns), F32),
        ),
        flops=1_000,
    )


def unpack_small(parts, taps, columns):
    upper = (taps + 1) // 2
    width = parts[0].shape[1]

    def body(ins, outs, scratch):
        total = scratch[0]
        total[...] = (ins[0][...] + ins[1][...]) + (ins[2][...] + ins[3][...])
        outs[0][...] = total[:5, :]
        outs[1][:upper, :] = total[9 : 9 + upper, :columns]
        outs[1][upper:, :] = total[9 : 9 + taps - upper, columns:]
        outs[2][0:1, :] = total[8:9, :columns]
        outs[2][1:2, :] = total[8:9, columns:]

    return on_chip(
        body,
        "unpack_small",
        parts,
        (((5, width), F32), ((taps, columns), F32), ((2, columns), F32)),
        scratch=(pltpu.VMEM(parts[0].shape, F32),),
        flops=1_000,
    )


PAD = 16


def pad_rows(padded, rows, columns, value):
    padded[:PAD, :] = jnp.zeros((PAD, columns), F32)
    padded[PAD + rows :, :] = jnp.zeros((PAD, columns), F32)
    padded[PAD : PAD + rows, :] = value


def conv_forward(kept, own, other, gains, weights, depth_kernel):
    rows, width = own.shape
    taps, columns = depth_kernel.shape
    half_taps = (taps - 1) // 2

    def body(ins, outs, scratch):
        kept_ref, own_ref, other_ref, gain_ref, weight_ref, tap_ref = ins
        conv_ref, sums_ref = outs
        padded = scratch[0]
        after = kept_residual(kept_ref, width) + both_parts(own_ref, other_ref)
        conv_ref[:, :width] = after
        entries = entries_of(after, gain_ref[2:3, :])
        joined = matmul(entries, weight_ref[:, 5 * columns : 7 * columns])
        value = joined[:, :columns]
        gate = jax.nn.sigmoid(joined[:, columns:])
        conv_ref[:, width : width + columns] = value
        conv_ref[:, width + columns : width + 2 * columns] = gate
        pad_rows(padded, rows, columns, value * gate)
        total = jnp.zeros((rows, columns), F32)
        for tap in range(taps):
            start = PAD - half_taps + tap
            total = total + tap_ref[tap : tap + 1, :] * padded[start : start + rows, :]
        conv_ref[:, width + 2 * columns :] = total
        sums_ref[0:1, :] = jnp.sum(total, 0, keepdims=True)
        sums_ref[1:2, :] = jnp.sum(total * total, 0, keepdims=True)

    return on_chip(
        body,
        "conv_forward",
        (kept, own, other, gains, weights, depth_kernel),
        (((rows, width + 3 * columns), F32), ((2, columns), F32)),
        scratch=(pltpu.VMEM((rows + 2 * PAD, columns), F32),),
    )


def batch_norm(conv_ref, sums_ref, batch_ref, token_count):
    columns = sums_ref.shape[1]
    column_mean = sums_ref[0:1, :] / token_count
    inverse = lax.rsqrt(sums_ref[1:2, :] / token_count - column_mean * column_mean + EPSILON)
    standard = (conv_ref[:, conv_ref.shape[1] - columns :] - column_mean) * inverse
    return standard, inverse, standard * batch_ref[0:1, :] + batch_ref[1:2, :]


def norm_forward(conv_kept, sums, batch, weights, token_count):
    rows = conv_kept.shape[0]
    columns = sums.shape[1]
    width = weights.shape[0]

    def body(ins, outs, _):
        conv_ref, sums_ref, batch_ref, weight_ref = ins
        _, _, shifted = batch_norm(conv_ref, sums_ref, batch_ref, token_count)
        activated = (shifted * jax.nn.sigmoid(shifted)).astype(BF16)
        outs[0][...] = right_transposed(activated, weight_ref[:, 7 * columns :]).astype(BF16)

    return on_chip(
        body, "norm_forward", (conv_kept, sums, batch, weights), (((rows, width), BF16),)
    )[0]


def norm_backward(gradient, own, other, kept, gains, weights, conv_kept, sums, batch, count):
    rows, width = gradient.shape
    columns = sums.shape[1]

    def body(ins, outs, _):
        grad_ref, own_ref, other_ref, x_ref, gain_ref, weight_ref, conv_ref, sums_ref, batch_ref = (
            ins
        )
        grads_ref, grad_sums_ref, gain_grad_ref = outs
        normed, factor = norm_parts(x_ref[:, :width])
        passed, gain_grad = norm_back(
            both_parts(own_ref, other_ref), normed, factor, gain_ref[3:4, :]
        )
        gain_grad_ref[...] = gain_grad
        total = grad_ref[...] + passed
        grads_ref[:, :width] = total
        standard, _, shifted = batch_norm(conv_ref, sums_ref, batch_ref, count)
        grad_shifted = matmul(
            total.astype(BF16), weight_ref[:, 7 * columns :]
        ) * swish_slope(shifted, jax.nn.sigmoid(shifted))
        grads_ref[:, width:] = grad_shifted
        grad_sums_ref[0:1, :] = jnp.sum(grad_shifted, 0, keepdims=True)
        grad_sums_ref[1:2, :] = jnp.sum(grad_shifted * standard, 0, keepdims=True)

    return on_chip(
        body,
        "norm_backward",
        (gradient, own, other, kept, gains, weights, conv_kept, sums, batch),
        (((rows, width + columns), F32), ((2, columns), F32), ((1, width), F32)),
    )


def conv_backward(norm_grads, grad_sums, conv_kept, sums, batch, weights, depth_kernel, count):
    rows = conv_kept.shape[0]
    columns = sums.shape[1]
    width = weights.shape[0]
    taps = depth_kernel.shape[0]
    half_taps = (taps - 1) // 2

    def body(ins, outs, scratch):
        grads_ref, grad_sums_ref, conv_ref, sums_ref, batch_ref, weight_ref, tap_ref = ins
        grad_conv_ref, joined_ref, part_ref = outs
        padded = scratch[0]
        standard, inverse, _ = batch_norm(conv_ref, sums_ref, batch_ref, count)
        grad_conv = (inverse * batch_ref[0:1, :]) * (
            grads_ref[:, width:]
            - grad_sums_ref[0:1, :] / count
            - standard * (grad_sums_ref[1:2, :] / count)
        )
        grad_conv_ref[...] = grad_conv
        pad_rows(padded, rows, columns, grad_conv)
        total = jnp.zeros((rows, columns), F32)
        for tap in range(taps):
            start = PAD + half_taps - tap
            total = total + tap_ref[tap : tap + 1, :] * padded[start : start + rows, :]
        gate_sigma = conv_ref[:, width + columns : width + 2 * columns]
        grad_value = total * gate_sigma
        grad_gate = grad_value * conv_ref[:, width : width + columns] * (1.0 - gate_sigma)
        joined = jnp.concatenate([grad_value, grad_gate], 1).astype(BF16)
        joined_ref[...] = joined
        part_ref[...] = right_transposed(
            joined, weight_ref[:, 5 * columns : 7 * columns]
        ).astype(BF16)

    return on_chip(
        body,
        "conv_backward",
        (norm_grads, grad_sums, conv_kept, sums, batch, weights, depth_kernel),
        (((rows, columns), F32), ((rows, 2 * columns), BF16), ((rows, width), BF16)),
        scratch=(pltpu.VMEM((rows + 2 * PAD, columns), F32),),
    )


def conv_weight_grads(norm_grads, grad_conv, joined, conv_kept, sums, batch, gains, taps, count):
    rows, columns = grad_conv.shape
    width = gains.shape[1]
    half_taps = (taps - 1) // 2

    def body(ins, outs, scratch):
        grads_ref, grad_ref, joined_ref, conv_ref, sums_ref, batch_ref, gain_ref = ins
        padded = scratch[0]
        entries = entries_of(conv_ref[:, :width], gain_ref[2:3, :])
        outs[0][:, : 2 * columns] = left_transposed(entries, joined_ref[...]).astype(BF16)
        _, _, shifted = batch_norm(conv_ref, sums_ref, batch_ref, count)
        activated = (shifted * jax.nn.sigmoid(shifted)).astype(BF16)
        outs[0][:, 2 * columns :] = left_transposed(
            grads_ref[:, :width].astype(BF16), activated
        ).astype(BF16)
        value = conv_ref[:, width : width + columns]
        gate = conv_ref[:, width + columns : width + 2 * columns]
        pad_rows(padded, rows, columns, value * gate)
        grad_conv_value = grad_ref[...]
        for tap in range(taps):
            start = PAD - half_taps + tap
            outs[1][tap : tap + 1, :] = jnp.sum(
                padded[start : start + rows, :] * grad_conv_value, 0, keepdims=True
            )

    return on_chip(
        body,
        "conv_weight_grads",
        (norm_grads, grad_conv, joined, conv_kept, sums, batch, gains),
        (((width, 3 * columns), BF16), ((taps, columns), F32)),
        scratch=(pltpu.VMEM((rows + 2 * PAD, columns), F32),),
    )


def first_back(gradient, own, other, kept, pre, gains, weights):
    rows, width = gradient.shape
    hidden = weights.shape[1] // 2

    def body(ins, outs, _):
        grad_ref, own_ref, other_ref, kept_ref, pre_ref, gain_ref, weight_ref = ins
        grads_ref, total_ref, part_ref, gain_grad_ref = outs
        normed, factor = norm_parts(kept_residual(kept_ref, width))
        passed, gain_grad = norm_back(
            both_parts(own_ref, other_ref), normed, factor, gain_ref[1:2, :]
        )
        gain_grad_ref[...] = gain_grad
        total = grad_ref[...] + passed
        total_ref[...] = total
        part_ref[...] = ff_back_body(total, pre_ref[...], weight_ref, grads_ref).astype(BF16)

    return on_chip(
        body,
        "first_back",
        (gradient, own, other, kept, pre, gains, weights),
        (
            ((rows, width + 2 * hidden), BF16),
            ((rows, width), F32),
            ((rows, width), BF16),
            ((1, width), F32),
        ),
    )


def input_back(total, own, other, tokens, gains, gain_grads, tap_grads, bias_grads):
    rows, width = tokens.shape
    taps, columns = tap_grads.shape
    upper = (taps + 1) // 2
    packed_rows = 8 + -(-(1 + upper) // 8) * 8

    def body(ins, outs, _):
        total_ref, own_ref, other_ref, x_ref, gain_ref = ins[:5]
        tap_ref, bias_ref = ins[9:]
        packed = outs[1]
        normed, factor = norm_parts(x_ref[...].astype(F32))
        passed, gain_grad = norm_back(
            both_parts(own_ref, other_ref), normed, factor, gain_ref[0:1, :]
        )
        outs[0][...] = own_half(total_ref[...] + passed)
        packed[...] = jnp.zeros((packed_rows, 2 * columns), F32)
        packed[0:1, :] = gain_grad
        for place in range(4):
            packed[place + 1 : place + 2, :] = ins[5 + place][...]
        packed[8:9, :columns] = bias_ref[0:1, :]
        packed[8:9, columns:] = bias_ref[1:2, :]
        packed[9 : 9 + upper, :columns] = tap_ref[:upper, :]
        packed[9 : 9 + taps - upper, columns:] = tap_ref[upper:, :]

    return on_chip(
        body,
        "input_back",
        (total, own, other, tokens, gains) + tuple(gain_grads) + (tap_grads, bias_grads),
        (((rows // 2, width), F32), ((packed_rows, 2 * columns), F32)),
        flops=1_000_000,
    )


def reduce_plain(grads):
    return lax.psum_scatter(grads.astype(BF16), "dp", scatter_dimension=0, tiled=True).astype(F32)


def stacked_columns(pieces, count):
    width = pieces.shape[1] // count
    return jnp.stack([pieces[:, index * width : (index + 1) * width] for index in range(count)])


def unstacked(stacked):
    return [stacked[index] for index in range(stacked.shape[0])]


def body(
    tokens,
    norm_gains,
    first_in,
    first_out,
    attention_in,
    attention_out,
    head_biases,
    gated_in,
    pointwise_out,
    depth_kernel,
    batch_scale,
    batch_shift,
    second_in,
    second_out,
    cotangent,
):
    local_heads = HEAD_TOTAL // lax.axis_size("tensor")
    length = tokens.shape[0] * lax.axis_size("tensor")
    token_count = float(length * lax.axis_size("dp"))
    columns = attention_out.shape[1]
    hidden = first_in.shape[1]
    width = tokens.shape[1]
    table = sinusoid(length, width).astype(BF16)
    batch = jnp.stack([batch_scale, batch_shift])
    split = doubling()

    def gather(pieces):
        return lax.all_gather(jnp.concatenate(pieces, 1), "dp", axis=0, tiled=True)

    batch_one = None
    if split:
        batch_one = on_chip(
            lambda ins, outs, _: (
                outs[0].__setitem__(..., ins[0][...]),
                outs[1].__setitem__(..., ins[1][...]),
            ),
            "first_copy",
            (first_in, first_out),
            tuple((value.shape, value.dtype) for value in (first_in, first_out)),
            flops=1_000,
        )
        batch_one = tuple(batch_one)
    tokens_all = both_halves(tie(tokens, batch_one))
    cotangent_all = both_halves(cotangent)

    if split:
        joint_two = jnp.concatenate(
            [
                attention_in.reshape(-1, columns),
                attention_out,
                gated_in.reshape(-1, columns),
                pointwise_out,
            ],
            0,
        )
        batch_two = (joint_two[: joint_two.shape[0] // 2], joint_two[joint_two.shape[0] // 2 :])
        batch_three = (second_in, second_out)
        joint_three = jnp.concatenate(batch_three, 0)
        arrived_one = gather_send((first_in, first_out), 0)
        arrived_one = tie(arrived_one, batch_one)
        arrived_two = gather_send((tie(joint_two, arrived_one),), 0)
        batch_one = gather_join(batch_one, tuple(arrived_one))
        arrived_one = gather_send(batch_one, 1)
        batch_one = gather_join(batch_one, tie(arrived_one, table))
        arrived_one = gather_send(batch_one, 2)
        batch_two = gather_join(batch_two, tie(arrived_two, batch_one))
        arrived_two = gather_send(batch_two, 1)
        batch_one = gather_join(
            batch_one, tie(arrived_one, (batch_two, cotangent_all)), joint=True
        )
        arrived_three = gather_send((tie(joint_three, batch_one),), 0)
        batch_one += (shift(batch_one[0], "dp", 1),)
    else:
        batch_one = gather([first_in, first_out])
        mixed_weights = gather(
            unstacked(attention_in) + [attention_out] + unstacked(gated_in) + [pointwise_out]
        )
        positions = position_forward(table, mixed_weights, columns)
        second_weights = gather([second_in, second_out])

    pre1, part1, first_weights = first_forward(tokens_all, norm_gains, batch_one)
    other1 = swap(part1)
    if split:
        batch_two = gather_join(batch_two, tie(arrived_two, part1))
        arrived_two = gather_send(batch_two, 2)
        batch_three = gather_join(batch_three, tie(arrived_three, batch_two))
        arrived_three = gather_send(batch_three, 1)
        batch_two = gather_join(batch_two, tie(arrived_two, (other1, batch_three)), joint=True)
        batch_two += (shift(batch_two[0], "dp", 1),)
        mixed_weights, positions = mixed_assemble(batch_two, table, width)
    kept, part2 = attention_forward(
        tokens_all, part1, other1, norm_gains, mixed_weights, positions, head_biases, local_heads
    )
    other2 = swap(part2)
    if split:
        batch_three = gather_join(batch_three, tie(arrived_three, part2))
        arrived_three = gather_send(batch_three, 2)
    conv_kept, sums = conv_forward(
        kept, part2, other2, norm_gains, mixed_weights, depth_kernel
    )
    if split:
        batch_three = gather_join(batch_three, tie(arrived_three, sums), joint=True)
        batch_three += (shift(batch_three[0], "dp", 1),)
        second_weights = second_assemble(batch_three, width)
    sums = sum_over(sums, "dp")
    part3 = norm_forward(conv_kept, sums, batch, mixed_weights, token_count)
    other3 = swap(part3)
    other3 = tie(other3, second_weights)
    second_kept, part4 = second_forward(conv_kept, part3, other3, norm_gains, second_weights)
    other4 = swap(part4)
    block_out, grad4, second_rows, part5, gain5 = second_back(
        second_kept, part4, other4, cotangent_all, norm_gains, second_weights
    )
    other5 = swap(part5)
    second_name = "second_weight_grads"
    if split:
        keeps, sends = ff_weight_split(second_rows, second_kept, norm_gains, 3, second_name)
        second_keeps, sends = scatter_add(keeps, scatter_send(sends, 0), 0, "second_sum")
        second_arrived = scatter_send(sends, 1)
        other5 = tie(other5, second_keeps)
    else:
        second_grads = reduce_plain(
            ff_weight_grads(second_rows, second_kept, norm_gains, 3, second_name)
        )
        second_reduced = (second_grads[:, :hidden], second_grads[:, hidden:])
    norm_grads, grad_sums, gain4 = norm_backward(
        grad4,
        part5,
        other5,
        second_kept,
        norm_gains,
        mixed_weights,
        conv_kept,
        sums,
        batch,
        token_count,
    )
    grad_sums = sum_over(grad_sums, "dp")
    if split:
        second_keeps, sends = scatter_add(second_keeps, second_arrived, 1, "second_sum")
        grad_sums = tie(grad_sums, second_keeps)
    grad_conv, joined3, part6 = conv_backward(
        norm_grads, grad_sums, conv_kept, sums, batch, mixed_weights, depth_kernel, token_count
    )
    other6 = swap(part6)
    conv_grads, tap_grads = conv_weight_grads(
        norm_grads,
        grad_conv,
        joined3,
        conv_kept,
        sums,
        batch,
        norm_gains,
        depth_kernel.shape[0],
        token_count,
    )
    other6 = tie(other6, conv_grads)
    if split:
        second_arrived = scatter_send(tie(sends, part6), 2)
        second_arrived = tie(second_arrived, conv_grads)
        second_keeps, sends = scatter_add(second_keeps, second_arrived, 2, "second_sum")
        second_arrived = scatter_send(sends, 3)
        other6 = tie(other6, second_keeps)
    grad2, joined2, table_grad, part7, gain3, bias_grads = attention_back(
        norm_grads,
        part6,
        other6,
        conv_kept,
        norm_gains,
        mixed_weights,
        positions,
        kept,
        local_heads,
    )
    other7 = swap(part7)
    mixed_grads = mixed_weight_grads(
        joined2, table, table_grad, grad2, kept, norm_gains, conv_grads, split
    )
    if split:
        keeps, sends = mixed_grads
        mixed_keeps, sends = scatter_add(keeps, scatter_send(sends, 0), 0, "mixed_sum")
        mixed_arrived = scatter_send(sends, 1)
        other7 = tie(other7, mixed_keeps)
    first_rows, grad1, part8, gain2 = first_back(
        grad2, part7, other7, kept, pre1, norm_gains, first_weights
    )
    other8 = swap(part8)
    small = ((gain2, gain3, gain4, gain5), tap_grads, bias_grads)
    if split:
        mixed_keeps, sends = scatter_add(mixed_keeps, mixed_arrived, 1, "mixed_sum")
        mixed_arrived = scatter_send(sends, 2)
        keeps, sends = ff_weight_split(
            tie(first_rows, mixed_keeps), tokens_all, norm_gains, 0, "first_weight_grads"
        )
        first_arrived = scatter_send(sends, 0)
        first_keeps, sends = scatter_add(keeps, first_arrived, 0, "first_sum")
        first_arrived = scatter_send(sends, 1)
        second_reduced, _ = scatter_add(
            second_keeps, tie(second_arrived, first_keeps), 3, "second_sum"
        )
        mixed_keeps, sends = scatter_add(
            mixed_keeps, tie(mixed_arrived, first_keeps), 2, "mixed_sum"
        )
        mixed_arrived = scatter_send(sends, 3)
        other8 = tie(other8, mixed_keeps)
        grad_start, packed = input_back(grad1, part8, other8, tokens_all, norm_gains, *small)
        first_arrived = tie(first_arrived, packed)
        first_keeps, sends = scatter_add(first_keeps, first_arrived, 1, "first_sum")
        first_arrived = scatter_send(sends, 2)
        packed = sum_over(tie(sum_over(packed, "dp", 1, 2), first_keeps), "dp", 2, 4)
        reduced_attention, reduced_mixing, reduced_gated, reduced_pointwise = mixed_finish(
            mixed_keeps, tie(mixed_arrived, first_keeps)
        )
        first_arrived = tie(first_arrived, reduced_mixing)
        first_keeps, sends = scatter_add(first_keeps, first_arrived, 2, "first_sum")
        first_arrived = scatter_send(sends, 3)
        packed = tie(packed, first_keeps)
        parts = (packed,) + tuple(shift(packed, "dp", mask) for mask in (4, 8, 12))
        (reduced_in, reduced_out), _ = scatter_add(first_keeps, first_arrived, 3, "first_sum")
    else:
        grad_start, packed = input_back(grad1, part8, other8, tokens_all, norm_gains, *small)
        first_grads = reduce_plain(
            ff_weight_grads(first_rows, tokens_all, norm_gains, 0, "first_weight_grads")
        )
        reduced_in, reduced_out = first_grads[:, :hidden], first_grads[:, hidden:]
        mixed = reduce_plain(mixed_grads)
        reduced_attention = stacked_columns(mixed[:, : 4 * columns], 4)
        reduced_mixing = mixed[:, 4 * columns : 5 * columns]
        reduced_gated = stacked_columns(mixed[:, 5 * columns : 7 * columns], 2)
        reduced_pointwise = mixed[:, 7 * columns :]
        packed = sum_over(packed, "dp")
        parts = (packed,) + (jnp.zeros_like(packed),) * 3
    gain_total, tap_total, bias_total = unpack_small(parts, depth_kernel.shape[0], columns)
    return (
        block_out,
        grad_start,
        gain_total,
        reduced_in,
        reduced_out,
        reduced_attention,
        reduced_mixing,
        bias_total,
        reduced_gated,
        reduced_pointwise,
        tap_total,
        grad_sums[1],
        grad_sums[0],
        *second_reduced,
    )


def solution(mesh):
    placed = (
        P(("dp", "tensor"), None),
        P(),
        P("dp", "tensor"),
        P("dp", "tensor"),
        P(None, "dp", "tensor"),
        P("dp", "tensor"),
        P(None, "tensor"),
        P(None, "dp", "tensor"),
        P("dp", "tensor"),
        P(None, "tensor"),
        P("tensor"),
        P("tensor"),
        P("dp", "tensor"),
        P("dp", "tensor"),
        P(("dp", "tensor"), None),
    )
    return jax.shard_map(
        body,
        mesh=mesh,
        in_specs=placed,
        out_specs=(
            P(("dp", "tensor"), None),
            P(("dp", "tensor"), None),
            P(),
            P("dp", "tensor"),
            P("dp", "tensor"),
            P(None, "dp", "tensor"),
            P("dp", "tensor"),
            P(None, "tensor"),
            P(None, "dp", "tensor"),
            P("dp", "tensor"),
            P(None, "tensor"),
            P("tensor"),
            P("tensor"),
            P("dp", "tensor"),
            P("dp", "tensor"),
        ),
        check_vma=False,
    )
```
